32 devices in a mesh: grp: 4 (over y, x), tile: 8 (over z, core).
Axes of the slice: x: 2, y: 2, z: 4, core: 2. Of those that a mesh axis runs over, the one named last changes fastest.
Arguments:
- right_side: float32 [16, 32, 1024], P(None, 'grp', 'tile'), may hold values from -6 to 6
- amplitude: float32 [32, 1024], P('grp', 'tile'), may hold values from 0.2 to 1
- factor: bfloat16 [2048, 32, 1024], P('tile', 'grp'), may hold values from -6 to 6
- scale: float32 [2048], P('tile'), may hold values from 0.5 to 2
Outputs:
- solution_field: float32 [16, 32, 1024], P(None, 'grp', 'tile')
- residual: float32 [16, 32, 1024], P(None, 'grp', 'tile')
The draws below stay inside these ranges and needn't reach their ends.
All inputs are finite; a program needn't handle non-finite values.
Results may differ from the reference program's by a relative error of at most 0.0041.
Values may be sent and summed in bfloat16 or wider, within the bound.
No kernel may reach another device: no remote copies, remote signals or barrier semaphores. Data moves between devices by JAX's collectives and lax.ppermute only.
A program may use at most 64 MiB of HBM per device.

```python
import math
import jax
import jax.numpy as jnp

RANK = 2048
COLS = 16
REACH = 8
ITERS = 2
NX = 32
NY = 1024
NCELLS = 32768


def steps_of(key, shape, cuts, low, largest):
    gain = 1.0
    for axis_at, shards_of in cuts:
        draws = jax.random.uniform(jax.random.fold_in(jax.random.fold_in(key, 6), axis_at), (shards_of,), jnp.float32, low / len(cuts), largest / len(cuts))
        gain = gain * jnp.repeat(jnp.exp(draws), shape[axis_at] // shards_of).reshape((-1,) + (1,) * (len(shape) - 1 - axis_at))
    return gain


def scatter_about(own_key, extent, scale, bound, pieces=(), held_as=jnp.bfloat16):
    entries = scale * jax.random.normal(own_key, extent, jnp.float32)
    if pieces:
        entries = entries * steps_of(own_key, extent, pieces, -0.22, 0.18)
    return jnp.clip(entries, -bound, bound).astype(held_as)


def setup_inputs(seed: int = 0) -> dict:
    key_list = jax.random.split(jax.random.key(seed), 5)
    right_side = scatter_about(key_list[0], (COLS, NX, NY), 1.0, 6.0, ((1, 4), (2, 8)), jnp.float32)
    amplitude = jnp.clip(jnp.exp(math.log(1.0) - 1.609438 * jax.random.uniform(key_list[1], (NX, NY), jnp.float32) ** steps_of(key_list[1], (NX, NY), ((0, 4), (1, 8)), -0.2, 0.2)), 0.2, 1.0)
    factor = scatter_about(key_list[2], (RANK, NX, NY), 1.0, 6.0, ((0, 8), (1, 4)))
    scale = jnp.clip(jnp.exp(math.log(2.0) - 1.3862944 * jax.random.uniform(key_list[3], (RANK,), jnp.float32) ** steps_of(key_list[3], (RANK,), ((0, 8),), -0.2, 0.2)), 0.5, 2.0)
    return dict(right_side=right_side, amplitude=amplitude, factor=factor, scale=scale)


def taper(sigma):
    offsets = jnp.arange(-REACH, REACH + 1).astype(jnp.float32)
    values = jnp.exp(-offsets * offsets / (2.0 * sigma * sigma)) * jnp.cos(jnp.pi * offsets / (2.0 * REACH + 2.0)) ** 2
    return values / jnp.sum(values)


def smooth(padded, rows_out, cols_out):
    row_kernel = taper(3.0)
    col_kernel = taper(5.0)
    along = row_kernel[0] * padded[:, 0:rows_out, :]
    for index in range(1, 2 * REACH + 1):
        along = along + row_kernel[index] * padded[:, index:index + rows_out, :]
    result = col_kernel[0] * along[:, :, 0:cols_out]
    for index in range(1, 2 * REACH + 1):
        result = result + col_kernel[index] * along[:, :, index:index + cols_out]
    return result


def operate(field, amplitude, factor, scale):
    padded = jnp.pad(field, ((0, 0), (REACH, REACH), (REACH, REACH)))
    conv = smooth(padded, NX, NY)
    flat_factor = factor.reshape(RANK, NCELLS)
    rounded = field.astype(jnp.bfloat16).reshape(COLS, NCELLS)
    project = jnp.dot(flat_factor, rounded.T, preferred_element_type=jnp.float32)
    weights = scale * scale / NCELLS
    coefficients = (project * weights[:, None]).astype(jnp.bfloat16)
    lowrank = jnp.dot(coefficients.T, flat_factor, preferred_element_type=jnp.float32).reshape(COLS, NX, NY)
    return field + amplitude[None] * conv + lowrank


def reference(right_side, amplitude, factor, scale):
    current = 0.5 * right_side
    residual = right_side
    for step in range(ITERS):
        residual = right_side - operate(current, amplitude, factor, scale)
        current = current + 0.5 * residual
    return current, residual
```

```python
import math
from functools import partial

import jax
import jax.numpy as jnp
import numpy as np
from jax import lax
from jax.experimental import pallas as pl
from jax.experimental.pallas import tpu as pltpu
from jax.sharding import PartitionSpec as P

REACH = 8
ITERS = 2
LANES = 128


def taper(sigma):
    offsets = np.arange(-REACH, REACH + 1).astype(np.float64)
    values = np.exp(-offsets * offsets / (2.0 * sigma * sigma))
    values = values * np.cos(np.pi * offsets / (2.0 * REACH + 2.0)) ** 2
    return [float(v) for v in (values / values.sum()).astype(np.float32)]


ROW_TAPS = taper(3.0)
COL_TAPS = taper(5.0)


def stencil(low, own, high, taps, axis):
    size = own.shape[axis]
    place = lax.broadcasted_iota(jnp.int32, own.shape, axis)
    total = taps[REACH] * own
    for shift in range(1, REACH + 1):
        after = pltpu.roll(jnp.where(place < shift, high, own), size - shift, axis)
        before = pltpu.roll(jnp.where(place >= size - shift, low, own), shift, axis)
        total = total + taps[REACH + shift] * after + taps[REACH - shift] * before
    return total


def project_kernel(rows, cols, x_ref, fields_ref, factor_ref, pay_ref, along_ref, diag):
    tiles = fields_ref.shape[0]
    ranks = factor_ref.shape[0] // rows
    lines = cols * rows
    me = lax.axis_index("tile")

    field = jnp.concatenate([fields_ref[t] for t in range(tiles)], axis=1)
    step = min(256, ranks * rows)
    row_of = lax.broadcasted_iota(jnp.int32, (rows, lines), 0)
    lane_of = lax.broadcasted_iota(jnp.int32, (rows, lines), 1)
    same = (lax.rem(lane_of, rows) == row_of).astype(jnp.float32)
    if diag.shape[0] > ranks:
        diag[...] = jnp.zeros_like(diag)
    for at in range(0, ranks * rows, step):
        part = lax.dot_general(
            factor_ref[at : at + step, :],
            field,
            (((1,), (1,)), ((), ())),
            preferred_element_type=jnp.float32,
        )
        part = part.reshape(step // rows, rows, lines) * same[None]
        diag[at // rows : (at + step) // rows, :] = jnp.sum(part, axis=1)
    pick = (
        lax.broadcasted_iota(jnp.int32, (cols, lines), 1) // rows
        == lax.broadcasted_iota(jnp.int32, (cols, lines), 0)
    ).astype(jnp.bfloat16)
    for at in range(0, diag.shape[0], LANES):
        part = diag[at : at + LANES, :]
        upper = part.astype(jnp.bfloat16)
        lower = (part - upper.astype(jnp.float32)).astype(jnp.bfloat16)
        dims = (((1,), (1,)), ((), ()))
        proj = lax.dot_general(pick, upper, dims, preferred_element_type=jnp.float32)
        proj = proj + lax.dot_general(pick, lower, dims, preferred_element_type=jnp.float32)
        first = at // LANES * 2 * cols
        upper = proj.astype(jnp.bfloat16)
        pay_ref[first : first + cols, :] = upper
        lower = proj - upper.astype(jnp.float32)
        pay_ref[first + cols : first + 2 * cols, :] = lower.astype(jnp.bfloat16)

    head = diag.shape[0] // LANES * 2 * cols
    low = fields_ref[jnp.maximum(me - 1, 0)].astype(jnp.float32)
    low = jnp.where(me > 0, low, 0.0)
    high = fields_ref[jnp.minimum(me + 1, tiles - 1)].astype(jnp.float32)
    high = jnp.where(me < tiles - 1, high, 0.0)
    along = stencil(low, x_ref[...], high, COL_TAPS, 1)
    along_ref[...] = along
    pay_ref[head:, :] = along.astype(jnp.bfloat16)


def term_kernel(rows, cols, weights_ref, pays_ref, factor_ref, term_ref, coef):
    groups = pays_ref.shape[0]
    ranks = factor_ref.shape[0] // rows
    lines = cols * rows
    blocks = weights_ref.shape[0]
    span = LANES // rows
    width = min(ranks, span)

    spread = (
        lax.broadcasted_iota(jnp.int32, (LANES, LANES), 1) // rows
        == lax.broadcasted_iota(jnp.int32, (LANES, LANES), 0)
    ).astype(jnp.bfloat16)
    same = (
        lax.rem(lax.broadcasted_iota(jnp.int32, (lines, LANES), 1), rows)
        == lax.rem(lax.broadcasted_iota(jnp.int32, (lines, LANES), 0), rows)
    ).astype(jnp.float32)
    for block in range(blocks):
        first = block * 2 * cols
        both = pays_ref[0, first : first + 2 * cols, :].astype(jnp.float32)
        for g in range(1, groups):
            both = both + pays_ref[g, first : first + 2 * cols, :].astype(jnp.float32)
        proj = both[:cols] + both[cols:]
        c = proj * weights_ref[block : block + 1, :]
        turned = [c if n == 0 else pltpu.roll(c, LANES - n * span, 1) for n in range(rows)]
        stacked = jnp.concatenate(turned, axis=0).astype(jnp.bfloat16)
        wide = jnp.dot(stacked, spread, preferred_element_type=jnp.float32)
        for n in range(rows):
            at = (block * LANES + n * span) * rows
            if at >= ranks * rows:
                break
            piece = wide[n * cols : (n + 1) * cols, :]
            piece = jnp.broadcast_to(piece[:, None, :], (cols, rows, LANES)).reshape(lines, LANES)
            coef[:, at : at + LANES] = (piece * same).astype(jnp.bfloat16)
    tiles = term_ref.shape[0]
    pair = 2 if tiles % 2 == 0 else 1
    for t in range(0, tiles, pair):
        term = jnp.dot(
            coef[...],
            factor_ref[:, t * LANES : (t + pair) * LANES],
            preferred_element_type=jnp.float32,
        )
        for s in range(pair):
            term_ref[t + s] = term[:, s * LANES : (s + 1) * LANES].astype(jnp.bfloat16)


def update_kernel(
    rows, cols, b_ref, x_ref, amp_ref, along_ref, pays_ref, terms_ref, new_ref, res_ref, short_ref
):
    groups = pays_ref.shape[0]
    lines = cols * rows
    head = pays_ref.shape[1] - lines
    me = lax.axis_index("grp")
    low = pays_ref[jnp.maximum(me - 1, 0), head:, :].astype(jnp.float32)
    low = jnp.where(me > 0, low, 0.0).reshape(cols, rows, LANES)
    high = pays_ref[jnp.minimum(me + 1, groups - 1), head:, :].astype(jnp.float32)
    high = jnp.where(me < groups - 1, high, 0.0).reshape(cols, rows, LANES)
    own = along_ref[...].reshape(cols, rows, LANES)
    conv = stencil(low, own, high, ROW_TAPS, 1)
    rank_sum = terms_ref[0].astype(jnp.float32)
    for t in range(1, terms_ref.shape[0]):
        rank_sum = rank_sum + terms_ref[t].astype(jnp.float32)
    x = x_ref[...]
    scaled = (amp_ref[...][None] * conv).reshape(lines, LANES)
    residual = b_ref[...] - (x + scaled + rank_sum)
    new = x + 0.5 * residual
    new_ref[...] = new
    res_ref[...] = residual
    short_ref[...] = new.astype(jnp.bfloat16)


def on_device(right_side, amplitude, factor, scale):
    cols, rows, width = right_side.shape
    ranks = factor.shape[0]
    tiles = lax.axis_size("tile")
    groups = lax.axis_size("grp")
    lines = cols * rows
    ncells_all = rows * width * groups * tiles
    blocks = -(-ranks // LANES)
    padded = blocks * LANES
    weights = scale * scale / ncells_all
    weights = jnp.pad(weights, (0, padded - ranks)).reshape(blocks, LANES)
    flat = factor.reshape(ranks * rows, tiles * width)
    b = right_side.reshape(lines, width)
    x = 0.5 * b
    short = x.astype(jnp.bfloat16)
    pay_rows = blocks * 2 * cols + lines
    vmem = pltpu.CompilerParams(vmem_limit_bytes=32 * 1024 * 1024)
    project = pl.pallas_call(
        partial(project_kernel, rows, cols),
        out_shape=(
            jax.ShapeDtypeStruct((pay_rows, width), jnp.bfloat16),
            jax.ShapeDtypeStruct((lines, width), jnp.float32),
        ),
        scratch_shapes=[pltpu.VMEM((padded, lines), jnp.float32)],
        compiler_params=vmem,
        name="project",
    )
    term = pl.pallas_call(
        partial(term_kernel, rows, cols),
        out_shape=jax.ShapeDtypeStruct((tiles, lines, width), jnp.bfloat16),
        scratch_shapes=[pltpu.VMEM((lines, ranks * rows), jnp.bfloat16)],
        compiler_params=vmem,
        name="term",
    )
    update = pl.pallas_call(
        partial(update_kernel, rows, cols),
        out_shape=(
            jax.ShapeDtypeStruct((lines, width), jnp.float32),
            jax.ShapeDtypeStruct((lines, width), jnp.float32),
            jax.ShapeDtypeStruct((lines, width), jnp.bfloat16),
        ),
        compiler_params=vmem,
        name="update",
    )
    for step in range(ITERS):
        fields = lax.all_gather(short, "tile", axis=0)
        pay, along = project(x, fields, flat)
        pays = lax.all_gather(pay, "grp", axis=0)
        sent = term(weights, pays, flat)
        terms = lax.all_to_all(sent, "tile", split_axis=0, concat_axis=0, tiled=True)
        x, residual, short = update(b, x, amplitude, along, pays, terms)
    return x.reshape(cols, rows, width), residual.reshape(cols, rows, width)


def solution(mesh):
    in_specs = (P(None, "grp", "tile"), P("grp", "tile"), P("tile", "grp", None), P("tile"))
    out_specs = (P(None, "grp", "tile"), P(None, "grp", "tile"))
    return jax.shard_map(
        on_device, mesh=mesh, in_specs=in_specs, out_specs=out_specs, check_vma=False
    )
```

```python
import math
from functools import partial

import jax
import jax.numpy as jnp
import numpy as np
from jax import lax
from jax.experimental import pallas as pl
from jax.experimental.pallas import tpu as pltpu
from jax.sharding import PartitionSpec as P

REACH = 8
ITERS = 2
LANES = 128


def taper(sigma):
    offsets = np.arange(-REACH, REACH + 1).astype(np.float64)
    values = np.exp(-offsets * offsets / (2.0 * sigma * sigma))
    values = values * np.cos(np.pi * offsets / (2.0 * REACH + 2.0)) ** 2
    return [float(v) for v in (values / values.sum()).astype(np.float32)]


ROW_TAPS = taper(3.0)
COL_TAPS = taper(5.0)


def stencil(low, own, high, taps, axis):
    size = own.shape[axis]
    place = lax.broadcasted_iota(jnp.int32, own.shape, axis)
    total = taps[REACH] * own
    for shift in range(1, REACH + 1):
        after = pltpu.roll(jnp.where(place < shift, high, own), size - shift, axis)
        before = pltpu.roll(jnp.where(place >= size - shift, low, own), shift, axis)
        total = total + taps[REACH + shift] * after + taps[REACH - shift] * before
    return total


def swap(value, axis, mask):
    return lax.ppermute(value, axis, [(i, i ^ mask) for i in range(lax.axis_size(axis))])


def project_kernel(rows, cols, halve, x_ref, fields_ref, factor_ref, pay_ref, along_ref, diag):
    tiles = fields_ref.shape[0]
    ranks = factor_ref.shape[0] // rows
    lines = cols * rows
    me = lax.axis_index("tile")
    near = tiles // 2

    def slot(t):
        return lax.rem(t, 2) * near + lax.div(t, 2)

    field = jnp.concatenate([fields_ref[t % 2 * near + t // 2] for t in range(tiles)], axis=1)
    step = min(256, ranks * rows)
    row_of = lax.broadcasted_iota(jnp.int32, (rows, lines), 0)
    lane_of = lax.broadcasted_iota(jnp.int32, (rows, lines), 1)
    same = (lax.rem(lane_of, rows) == row_of).astype(jnp.float32)
    if diag.shape[0] > ranks:
        diag[...] = jnp.zeros_like(diag)
    for at in range(0, ranks * rows, step):
        part = lax.dot_general(
            factor_ref[at : at + step, :],
            field,
            (((1,), (1,)), ((), ())),
            preferred_element_type=jnp.float32,
        )
        part = part.reshape(step // rows, rows, lines) * same[None]
        diag[at // rows : (at + step) // rows, :] = jnp.sum(part, axis=1)
    pick = (
        lax.broadcasted_iota(jnp.int32, (cols, lines), 1) // rows
        == lax.broadcasted_iota(jnp.int32, (cols, lines), 0)
    ).astype(jnp.bfloat16)
    for at in range(0, diag.shape[0], LANES):
        part = diag[at : at + LANES, :]
        upper = part.astype(jnp.bfloat16)
        lower = (part - upper.astype(jnp.float32)).astype(jnp.bfloat16)
        dims = (((1,), (1,)), ((), ()))
        proj = lax.dot_general(pick, upper, dims, preferred_element_type=jnp.float32)
        proj = proj + lax.dot_general(pick, lower, dims, preferred_element_type=jnp.float32)
        first = at // LANES * 2 * cols
        upper = proj.astype(jnp.bfloat16)
        pay_ref[first : first + cols, :] = upper
        lower = proj - upper.astype(jnp.float32)
        pay_ref[first + cols : first + 2 * cols, :] = lower.astype(jnp.bfloat16)

    head = diag.shape[0] // LANES * 2 * cols
    low = fields_ref[slot(jnp.maximum(me - 1, 0))].astype(jnp.float32)
    low = jnp.where(me > 0, low, 0.0)
    high = fields_ref[slot(jnp.minimum(me + 1, tiles - 1))].astype(jnp.float32)
    high = jnp.where(me < tiles - 1, high, 0.0)
    own = 0.5 * x_ref[...] if halve else x_ref[...]
    along = stencil(low, own, high, COL_TAPS, 1)
    along_ref[...] = along
    pay_ref[head:, :] = along.astype(jnp.bfloat16)


def term_kernel(rows, cols, groups, tiles, ncells, scale_ref, factor_ref, *refs):
    pay_refs, (mine_ref, other_ref, coef) = refs[:groups], refs[groups:]
    ranks = factor_ref.shape[0] // rows
    lines = cols * rows
    span = LANES // rows

    spread = (
        lax.broadcasted_iota(jnp.int32, (LANES, LANES), 1) // rows
        == lax.broadcasted_iota(jnp.int32, (LANES, LANES), 0)
    ).astype(jnp.bfloat16)
    same = (
        lax.rem(lax.broadcasted_iota(jnp.int32, (lines, LANES), 1), rows)
        == lax.rem(lax.broadcasted_iota(jnp.int32, (lines, LANES), 0), rows)
    ).astype(jnp.float32)
    for at in range(0, ranks, LANES):
        count = min(LANES, ranks - at)
        first = at // LANES * 2 * cols
        both = pay_refs[0][first : first + 2 * cols, :].astype(jnp.float32)
        for ref in pay_refs[1:]:
            both = both + ref[first : first + 2 * cols, :].astype(jnp.float32)
        proj = both[:cols] + both[cols:]
        scale = scale_ref[:, at : at + count]
        weights = scale * scale / ncells
        if count < LANES:
            weights = jnp.concatenate([weights, jnp.zeros((1, LANES - count), jnp.float32)], axis=1)
        c = proj * weights
        turned = [c if n == 0 else pltpu.roll(c, LANES - n * span, 1) for n in range(rows)]
        stacked = jnp.concatenate(turned, axis=0).astype(jnp.bfloat16)
        wide = jnp.dot(stacked, spread, preferred_element_type=jnp.float32)
        for n in range(rows):
            start = (at + n * span) * rows
            if start >= ranks * rows:
                break
            piece = wide[n * cols : (n + 1) * cols, :]
            piece = jnp.broadcast_to(piece[:, None, :], (cols, rows, LANES)).reshape(lines, LANES)
            coef[:, start : start + LANES] = (piece * same).astype(jnp.bfloat16)
    odd = lax.rem(lax.axis_index("tile"), 2) == 1
    for n in range(tiles // 2):
        term = jnp.dot(
            coef[...],
            factor_ref[:, 2 * n * LANES : 2 * (n + 1) * LANES],
            preferred_element_type=jnp.float32,
        )
        even_part, odd_part = term[:, :LANES], term[:, LANES:]
        mine_ref[n] = jnp.where(odd, odd_part, even_part)
        other_ref[n] = jnp.where(odd, even_part, odd_part).astype(jnp.bfloat16)


def pair_kernel(mine_ref, got_ref, *send_refs):
    me = lax.div(lax.axis_index("tile"), 2)
    for mask, ref in enumerate(send_refs):
        at = me ^ mask
        ref[...] = (mine_ref[at] + got_ref[at].astype(jnp.float32)).astype(ref.dtype)


def update_kernel(rows, cols, groups, near, first, b_ref, x_ref, amp_ref, along_ref, *refs):
    pay_refs, refs = refs[: groups - 1], refs[groups - 1 :]
    term_refs, (new_ref, res_ref, short_ref) = refs[:near], refs[near:]
    lines = cols * rows
    head = pay_refs[0].shape[0] - lines
    me = lax.axis_index("grp")
    low = jnp.zeros((lines, LANES), jnp.float32)
    high = low
    for mask, ref in enumerate(pay_refs, 1):
        part = ref[head:, :].astype(jnp.float32)
        low = jnp.where((me ^ mask) == me - 1, part, low)
        high = jnp.where((me ^ mask) == me + 1, part, high)
    low = low.reshape(cols, rows, LANES)
    high = high.reshape(cols, rows, LANES)
    own = along_ref[...].reshape(cols, rows, LANES)
    conv = stencil(low, own, high, ROW_TAPS, 1)
    rank_sum = term_refs[0][...]
    for ref in term_refs[1:]:
        rank_sum = rank_sum + ref[...].astype(jnp.float32)
    x = 0.5 * x_ref[...] if first else x_ref[...]
    scaled = (amp_ref[...][None] * conv).reshape(lines, LANES)
    residual = b_ref[...] - (x + scaled + rank_sum)
    new = x + 0.5 * residual
    new_ref[...] = new
    res_ref[...] = residual
    short_ref[...] = new.astype(jnp.bfloat16)


def on_device(right_side, amplitude, factor, scale):
    cols, rows, width = right_side.shape
    ranks = factor.shape[0]
    tiles = lax.axis_size("tile")
    groups = lax.axis_size("grp")
    near = tiles // 2
    lines = cols * rows
    ncells_all = rows * width * groups * tiles
    blocks = -(-ranks // LANES)
    flat = factor.reshape(ranks * rows, tiles * width)
    b = right_side.reshape(lines, width)
    scale = scale.reshape(1, ranks)
    x = b
    short = (0.5 * b).astype(jnp.bfloat16)
    pay_rows = blocks * 2 * cols + lines
    vmem = pltpu.CompilerParams(vmem_limit_bytes=32 * 1024 * 1024)

    def shape(dtype, *dims):
        return jax.ShapeDtypeStruct(dims, dtype)

    f32, bf16 = jnp.float32, jnp.bfloat16
    along_z = [[2 * z + core for z in range(near)] for core in range(2)]
    cores = [[2 * z, 2 * z + 1] for z in range(near)]
    for step in range(ITERS):
        fields = lax.all_gather(short, "tile", axis=0, axis_index_groups=along_z)
        fields = lax.all_gather(fields, "tile", axis=0, axis_index_groups=cores, tiled=True)
        pay, along = pl.pallas_call(
            partial(project_kernel, rows, cols, step == 0),
            out_shape=(shape(bf16, pay_rows, width), shape(f32, lines, width)),
            scratch_shapes=[pltpu.VMEM((blocks * LANES, lines), f32)],
            compiler_params=vmem,
            name="project",
        )(x, fields, flat)
        pays = [swap(pay, "grp", mask) for mask in range(1, groups)]
        mine, other = pl.pallas_call(
            partial(term_kernel, rows, cols, groups, tiles, ncells_all),
            out_shape=(shape(f32, near, lines, width), shape(bf16, near, lines, width)),
            scratch_shapes=[pltpu.VMEM((lines, ranks * rows), bf16)],
            compiler_params=vmem,
            name="term",
        )(scale, flat, pay, *pays)
        got = swap(other, "tile", 1)
        kept, *sends = pl.pallas_call(
            pair_kernel,
            out_shape=[shape(f32 if n == 0 else bf16, lines, width) for n in range(near)],
            compiler_params=vmem,
            name="pair",
        )(mine, got)
        terms = [swap(part, "tile", 2 * mask) for mask, part in enumerate(sends, 1)]
        x, residual, short = pl.pallas_call(
            partial(update_kernel, rows, cols, groups, near, step == 0),
            out_shape=(shape(f32, lines, width), shape(f32, lines, width), shape(bf16, lines, width)),
            compiler_params=vmem,
            name="update",
        )(b, x, amplitude, along, *pays, kept, *terms)
    return x.reshape(cols, rows, width), residual.reshape(cols, rows, width)


def solution(mesh):
    in_specs = (P(None, "grp", "tile"), P("grp", "tile"), P("tile", "grp", None), P("tile"))
    out_specs = (P(None, "grp", "tile"), P(None, "grp", "tile"))
    return jax.shard_map(
        on_device, mesh=mesh, in_specs=in_specs, out_specs=out_specs, check_vma=False
    )
```

```python
import math
from functools import partial

import jax
import jax.numpy as jnp
import numpy as np
from jax import lax
from jax.experimental import pallas as pl
from jax.experimental.pallas import tpu as pltpu
from jax.sharding import PartitionSpec as P

REACH = 8
ITERS = 2
LANES = 128


def taper(sigma):
    offsets = np.arange(-REACH, REACH + 1).astype(np.float64)
    values = np.exp(-offsets * offsets / (2.0 * sigma * sigma))
    values = values * np.cos(np.pi * offsets / (2.0 * REACH + 2.0)) ** 2
    return [float(v) for v in (values / values.sum()).astype(np.float32)]


ROW_TAPS = taper(3.0)
COL_TAPS = taper(5.0)


def stencil(low, own, high, taps, axis):
    size = own.shape[axis]
    place = lax.broadcasted_iota(jnp.int32, own.shape, axis)
    total = taps[REACH] * own
    for shift in range(1, REACH + 1):
        after = pltpu.roll(jnp.where(place < shift, high, own), size - shift, axis)
        before = pltpu.roll(jnp.where(place >= size - shift, low, own), shift, axis)
        total = total + taps[REACH + shift] * after + taps[REACH - shift] * before
    return total


def swap(value, axis, mask):
    return lax.ppermute(value, axis, [(i, i ^ mask) for i in range(lax.axis_size(axis))])


def gather_kernel(*refs):
    part_refs, out_ref = refs[1:-1], refs[-1]
    me = lax.div(lax.axis_index("tile"), 2)
    for mask, ref in enumerate(part_refs):
        out_ref[me ^ mask] = ref[...]


def load_kernel(source_ref, out_ref, sems):
    chunks = sems.shape[0]
    count = source_ref.shape[0] // chunks
    copies = [
        pltpu.make_async_copy(
            source_ref.at[pl.ds(n * count, count)], out_ref.at[pl.ds(n * count, count)], sems.at[n]
        )
        for n in range(chunks)
    ]
    for copy in copies:
        copy.start()
    for copy in copies:
        copy.wait()


def diagonal(rows, parity, fields_ref, factor_ref, store):
    near, lines, _ = fields_ref.shape
    count = factor_ref.shape[0]
    field = jnp.concatenate([fields_ref[z] for z in range(near)], axis=1)
    step = min(256, count)
    row_of = lax.broadcasted_iota(jnp.int32, (rows, lines), 0)
    lane_of = lax.broadcasted_iota(jnp.int32, (rows, lines), 1)
    same = (lax.rem(lane_of, rows) == row_of).astype(jnp.float32)
    starts = [pl.multiple_of((2 * z + parity) * LANES, LANES) for z in range(near)]
    for at in range(0, count, step):
        left = jnp.concatenate(
            [factor_ref[at : at + step, pl.ds(start, LANES)] for start in starts], axis=1
        )
        part = lax.dot_general(
            left, field, (((1,), (1,)), ((), ())), preferred_element_type=jnp.float32
        )
        part = part.reshape(step // rows, rows, lines) * same[None]
        store(at // rows, (at + step) // rows, jnp.sum(part, axis=1))


def first_kernel(rows, fields_ref, factor_ref, diag_ref):
    parity = lax.rem(lax.axis_index("tile"), 2)
    ranks = factor_ref.shape[0] // rows
    if diag_ref.shape[0] > ranks:
        diag_ref[...] = jnp.zeros_like(diag_ref)

    def store(start, end, value):
        diag_ref[start:end, :] = value

    diagonal(rows, parity, fields_ref, factor_ref, store)


def second_kernel(
    rows, cols, halve, x_ref, fields_ref, factor_ref, diag_ref, pay_ref, along_ref, total
):
    near = fields_ref.shape[0]
    lines = cols * rows
    me = lax.axis_index("tile")
    parity = lax.rem(me, 2)
    if total.shape[0] > factor_ref.shape[0] // rows:
        total[...] = jnp.zeros_like(total)

    def store(start, end, value):
        total[start:end, :] = diag_ref[start:end, :] + value

    diagonal(rows, 1 - parity, fields_ref, factor_ref, store)
    pick = (
        lax.broadcasted_iota(jnp.int32, (cols, lines), 1) // rows
        == lax.broadcasted_iota(jnp.int32, (cols, lines), 0)
    ).astype(jnp.bfloat16)
    for at in range(0, total.shape[0], LANES):
        part = total[at : at + LANES, :]
        upper = part.astype(jnp.bfloat16)
        lower = (part - upper.astype(jnp.float32)).astype(jnp.bfloat16)
        dims = (((1,), (1,)), ((), ()))
        proj = lax.dot_general(pick, upper, dims, preferred_element_type=jnp.float32)
        proj = proj + lax.dot_general(pick, lower, dims, preferred_element_type=jnp.float32)
        first = at // LANES * 2 * cols
        upper = proj.astype(jnp.bfloat16)
        pay_ref[first : first + cols, :] = upper
        lower = proj - upper.astype(jnp.float32)
        pay_ref[first + cols : first + 2 * cols, :] = lower.astype(jnp.bfloat16)

    head = total.shape[0] // LANES * 2 * cols
    left, right = lax.div(me + 1, 2) - 1, lax.div(me + 1, 2)
    low = fields_ref[jnp.maximum(left, 0)].astype(jnp.float32)
    low = jnp.where(left >= 0, low, 0.0)
    high = fields_ref[jnp.minimum(right, near - 1)].astype(jnp.float32)
    high = jnp.where(right < near, high, 0.0)
    own = 0.5 * x_ref[...] if halve else x_ref[...]
    along = stencil(low, own, high, COL_TAPS, 1)
    along_ref[...] = along
    pay_ref[head:, :] = along.astype(jnp.bfloat16)


def product(parity, coef, factor_ref, out_ref):
    near = out_ref.shape[0]
    pair = 2 if near % 2 == 0 else 1
    for z in range(0, near, pair):
        starts = [pl.multiple_of((2 * (z + n) + parity) * LANES, LANES) for n in range(pair)]
        right = jnp.concatenate([factor_ref[:, pl.ds(start, LANES)] for start in starts], axis=1)
        term = jnp.dot(coef, right, preferred_element_type=jnp.float32)
        for n in range(pair):
            out_ref[z + n] = term[:, n * LANES : (n + 1) * LANES].astype(out_ref.dtype)


def far_kernel(rows, cols, groups, ncells, scale_ref, factor_ref, *refs):
    pay_refs, (coef_ref, out_ref) = refs[:groups], refs[groups:]
    ranks = factor_ref.shape[0] // rows
    lines = cols * rows
    span = LANES // rows

    spread = (
        lax.broadcasted_iota(jnp.int32, (LANES, LANES), 1) // rows
        == lax.broadcasted_iota(jnp.int32, (LANES, LANES), 0)
    ).astype(jnp.bfloat16)
    same = (
        lax.rem(lax.broadcasted_iota(jnp.int32, (lines, LANES), 1), rows)
        == lax.rem(lax.broadcasted_iota(jnp.int32, (lines, LANES), 0), rows)
    ).astype(jnp.float32)
    for at in range(0, ranks, LANES):
        count = min(LANES, ranks - at)
        first = at // LANES * 2 * cols
        both = pay_refs[0][first : first + 2 * cols, :].astype(jnp.float32)
        for ref in pay_refs[1:]:
            both = both + ref[first : first + 2 * cols, :].astype(jnp.float32)
        proj = both[:cols] + both[cols:]
        scale = scale_ref[:, at : at + count]
        weights = scale * scale / ncells
        if count < LANES:
            weights = jnp.concatenate([weights, jnp.zeros((1, LANES - count), jnp.float32)], axis=1)
        c = proj * weights
        turned = [c if n == 0 else pltpu.roll(c, LANES - n * span, 1) for n in range(rows)]
        stacked = jnp.concatenate(turned, axis=0).astype(jnp.bfloat16)
        wide = jnp.dot(stacked, spread, preferred_element_type=jnp.float32)
        for n in range(rows):
            start = (at + n * span) * rows
            if start >= ranks * rows:
                break
            piece = wide[n * cols : (n + 1) * cols, :]
            piece = jnp.broadcast_to(piece[:, None, :], (cols, rows, LANES)).reshape(lines, LANES)
            coef_ref[:, start : start + LANES] = (piece * same).astype(jnp.bfloat16)
    parity = 1 - lax.rem(lax.axis_index("tile"), 2)
    product(parity, coef_ref[...], factor_ref, out_ref)


def near_kernel(coef_ref, factor_ref, out_ref):
    product(lax.rem(lax.axis_index("tile"), 2), coef_ref[...], factor_ref, out_ref)


def pair_kernel(mine_ref, got_ref, *send_refs):
    me = lax.div(lax.axis_index("tile"), 2)
    for mask, ref in enumerate(send_refs):
        at = me ^ mask
        ref[...] = (mine_ref[at] + got_ref[at].astype(jnp.float32)).astype(ref.dtype)


def local_kernel(rows, cols, halve, b_ref, x_ref, amp_ref, along_ref, *refs):
    pay_refs, base_ref = refs[:-1], refs[-1]
    lines = cols * rows
    head = pay_refs[0].shape[0] - lines
    me = lax.axis_index("grp")
    low = jnp.zeros((lines, LANES), jnp.float32)
    high = low
    for mask, ref in enumerate(pay_refs, 1):
        part = ref[head:, :].astype(jnp.float32)
        low = jnp.where((me ^ mask) == me - 1, part, low)
        high = jnp.where((me ^ mask) == me + 1, part, high)
    low = low.reshape(cols, rows, LANES)
    high = high.reshape(cols, rows, LANES)
    own = along_ref[...].reshape(cols, rows, LANES)
    conv = stencil(low, own, high, ROW_TAPS, 1)
    x = 0.5 * x_ref[...] if halve else x_ref[...]
    scaled = (amp_ref[...][None] * conv).reshape(lines, LANES)
    base_ref[...] = b_ref[...] - (x + scaled)


def update_kernel(near, halve, x_ref, base_ref, *refs):
    term_refs, out_refs = refs[:near], refs[near:]
    rank_sum = term_refs[0][...]
    for ref in term_refs[1:]:
        rank_sum = rank_sum + ref[...].astype(jnp.float32)
    x = 0.5 * x_ref[...] if halve else x_ref[...]
    residual = base_ref[...] - rank_sum
    new = x + 0.5 * residual
    out_refs[0][...] = new
    if len(out_refs) > 1:
        out_refs[1][...] = residual if out_refs[1].dtype == jnp.float32 else new.astype(jnp.bfloat16)


def on_device(right_side, amplitude, factor, scale):
    cols, rows, width = right_side.shape
    ranks = factor.shape[0]
    tiles = lax.axis_size("tile")
    groups = lax.axis_size("grp")
    near = tiles // 2
    lines = cols * rows
    ncells_all = rows * width * groups * tiles
    blocks = -(-ranks // LANES)
    flat = factor.reshape(ranks * rows, tiles * width)
    b = right_side.reshape(lines, width)
    scale = scale.reshape(1, ranks)
    x = b
    short = (0.5 * b).astype(jnp.bfloat16)
    pay_rows = blocks * 2 * cols + lines

    f32, bf16 = jnp.float32, jnp.bfloat16

    def shape(dtype, *dims):
        return jax.ShapeDtypeStruct(dims, dtype)

    def call(kernel, out_shape, flops=0, moved=1 << 18, **options):
        return pl.pallas_call(
            kernel,
            out_shape=out_shape,
            compiler_params=pltpu.CompilerParams(vmem_limit_bytes=32 * 1024 * 1024),
            cost_estimate=pl.CostEstimate(flops=flops, bytes_accessed=moved, transcendentals=0),
            **options,
        )

    work = lines * ranks * rows * tiles * width
    held = call(
        load_kernel,
        shape(bf16, *flat.shape),
        moved=4 * flat.size,
        in_specs=[pl.BlockSpec(memory_space=pltpu.HBM)],
        out_specs=pl.BlockSpec(memory_space=pltpu.VMEM),
        scratch_shapes=[pltpu.SemaphoreType.DMA((8,))],
        name="load",
    )(flat)
    for step in range(ITERS):
        halve = step == 0
        parts = [swap(short, "tile", 2 * mask) for mask in range(1, near)]
        whole = [pl.BlockSpec(memory_space=pl.ANY)] + [pl.BlockSpec(memory_space=pltpu.VMEM)] * near
        own = call(
            gather_kernel, shape(bf16, near, lines, width), in_specs=whole, name="order"
        )(held, short, *parts)
        across = swap(own, "tile", 1)
        diag = call(
            partial(first_kernel, rows),
            shape(f32, blocks * LANES, lines),
            flops=work,
            moved=flat.size,
            name="project_own",
        )(own, held)
        pay, along = call(
            partial(second_kernel, rows, cols, halve),
            (shape(bf16, pay_rows, width), shape(f32, lines, width)),
            flops=work,
            moved=flat.size,
            scratch_shapes=[pltpu.VMEM((blocks * LANES, lines), f32)],
            name="project_across",
        )(x, across, held, diag)
        pays = [swap(pay, "grp", mask) for mask in range(1, groups)]
        coef, far = call(
            partial(far_kernel, rows, cols, groups, ncells_all),
            (shape(bf16, lines, ranks * rows), shape(bf16, near, lines, width)),
            flops=work,
            moved=flat.size,
            name="term_across",
        )(scale, held, pay, *pays)
        got = swap(far, "tile", 1)
        mine = call(
            near_kernel,
            shape(f32, near, lines, width),
            flops=work,
            moved=flat.size,
            name="term_own",
        )(coef, held)
        kept, *sends = call(
            pair_kernel,
            [shape(f32 if n == 0 else bf16, lines, width) for n in range(near)],
            name="pair",
        )(mine, got)
        terms = [swap(part, "tile", 2 * mask) for mask, part in enumerate(sends, 1)]
        base = call(
            partial(local_kernel, rows, cols, halve), shape(f32, lines, width), name="local"
        )(b, x, amplitude, along, *pays)
        last = step == ITERS - 1
        x, residual = call(
            partial(update_kernel, near, halve),
            (shape(f32, lines, width), shape(f32 if last else bf16, lines, width)),
            name="update",
        )(x, base, kept, *terms)
        short = residual
    return x.reshape(cols, rows, width), residual.reshape(cols, rows, width)


def solution(mesh):
    in_specs = (P(None, "grp", "tile"), P("grp", "tile"), P("tile", "grp", None), P("tile"))
    out_specs = (P(None, "grp", "tile"), P(None, "grp", "tile"))
    return jax.shard_map(
        on_device, mesh=mesh, in_specs=in_specs, out_specs=out_specs, check_vma=False
    )
```

```python
import math
from functools import partial

import jax
import jax.numpy as jnp
import numpy as np
from jax import lax
from jax.experimental import pallas as pl
from jax.experimental.pallas import tpu as pltpu
from jax.sharding import PartitionSpec as P

REACH = 8
ITERS = 2
LANES = 128


def taper(sigma):
    offsets = np.arange(-REACH, REACH + 1).astype(np.float64)
    values = np.exp(-offsets * offsets / (2.0 * sigma * sigma))
    values = values * np.cos(np.pi * offsets / (2.0 * REACH + 2.0)) ** 2
    return [float(v) for v in (values / values.sum()).astype(np.float32)]


ROW_TAPS = taper(3.0)
COL_TAPS = taper(5.0)


def stencil(low, own, high, taps, axis):
    size = own.shape[axis]
    place = lax.broadcasted_iota(jnp.int32, own.shape, axis)
    total = taps[REACH] * own
    for shift in range(1, REACH + 1):
        after = pltpu.roll(jnp.where(place < shift, high, own), size - shift, axis)
        before = pltpu.roll(jnp.where(place >= size - shift, low, own), shift, axis)
        total = total + taps[REACH + shift] * after + taps[REACH - shift] * before
    return total


def swap(value, axis, mask):
    return lax.ppermute(value, axis, [(i, i ^ mask) for i in range(lax.axis_size(axis))])


def split(value):
    upper = value.astype(jnp.bfloat16)
    lower = (value - upper.astype(jnp.float32)).astype(jnp.bfloat16)
    return jnp.concatenate([upper, lower], axis=0)


def whole(both):
    half = both.shape[0] // 2
    both = both.astype(jnp.float32)
    return both[:half] + both[half:]


def load_kernel(source_ref, out_ref, sems):
    chunks = sems.shape[0]
    count = source_ref.shape[0] // chunks
    copies = [
        pltpu.make_async_copy(
            source_ref.at[pl.ds(n * count, count)], out_ref.at[pl.ds(n * count, count)], sems.at[n]
        )
        for n in range(chunks)
    ]
    for copy in copies:
        copy.start()
    for copy in copies:
        copy.wait()


def join_kernel(*refs):
    part_refs, out_ref = refs[-3:-1], refs[-1]
    half = out_ref.shape[0] // 2
    for n, ref in enumerate(part_refs):
        out_ref[n * half : (n + 1) * half] = ref[...]


def starts_of(masks, other):
    me = lax.axis_index("tile")
    chip, core = lax.div(me, 2), lax.rem(me, 2)
    core = 1 - core if other else core
    return [pl.multiple_of((2 * (chip ^ mask) + core) * LANES, LANES) for mask in masks]


def project_kernel(rows, masks, other, last, *refs):
    fields_ref, factor_ref = refs[:2]
    count, lines = factor_ref.shape[0], fields_ref.shape[1]
    cols = lines // rows
    before_ref = refs[2] if len(refs) > 3 + last else None
    out_ref = refs[-1]
    if out_ref.shape[0] > count // rows:
        out_ref[...] = jnp.zeros_like(out_ref)
    field = jnp.concatenate([fields_ref[n] for n in range(len(masks))], axis=1)
    step = min(256, count)
    row_of = lax.broadcasted_iota(jnp.int32, (rows, lines), 0)
    lane_of = lax.broadcasted_iota(jnp.int32, (rows, lines), 1)
    same = (lax.rem(lane_of, rows) == row_of).astype(jnp.float32)
    starts = starts_of(masks, other)
    for at in range(0, count, step):
        left = jnp.concatenate(
            [factor_ref[at : at + step, pl.ds(start, LANES)] for start in starts], axis=1
        )
        part = lax.dot_general(
            left, field, (((1,), (1,)), ((), ())), preferred_element_type=jnp.float32
        )
        part = part.reshape(step // rows, rows, lines) * same[None]
        part = jnp.sum(part, axis=1)
        first, end = at // rows, (at + step) // rows
        out_ref[first:end, :] = part if before_ref is None else before_ref[first:end, :] + part
    if not last:
        return
    pick = (
        lax.broadcasted_iota(jnp.int32, (cols, lines), 1) // rows
        == lax.broadcasted_iota(jnp.int32, (cols, lines), 0)
    ).astype(jnp.bfloat16)
    pay_ref = refs[-2]
    for at in range(0, out_ref.shape[0], LANES):
        both = split(out_ref[at : at + LANES, :])
        proj = lax.dot_general(
            pick, both, (((1,), (1,)), ((), ())), preferred_element_type=jnp.float32
        )
        first = at // LANES * cols
        pay_ref[first : first + cols, :] = proj[:, :LANES] + proj[:, LANES:]


def split_kernel(value_ref, out_ref):
    out_ref[...] = split(value_ref[...])


def merge_kernel(left_ref, right_ref, out_ref):
    out_ref[...] = split(whole(left_ref[...]) + whole(right_ref[...]))


def columns_kernel(masks, halve, x_ref, fields_ref, along_ref, short_ref):
    near = fields_ref.shape[0]
    me = lax.axis_index("tile")
    chip = lax.div(me, 2)
    left, right = lax.div(me + 1, 2) - 1, lax.div(me + 1, 2)
    low = jnp.zeros(x_ref.shape, jnp.float32)
    high = low
    for n in range(near):
        part = fields_ref[n].astype(jnp.float32)
        low = jnp.where((chip ^ masks[n]) == left, part, low)
        high = jnp.where((chip ^ masks[n]) == right, part, high)
    own = 0.5 * x_ref[...] if halve else x_ref[...]
    along = stencil(low, own, high, COL_TAPS, 1)
    along_ref[...] = along
    short_ref[...] = along.astype(jnp.bfloat16)


def product(coef, starts, factor_ref, out_ref):
    for n in range(0, len(starts), 2):
        pair = starts[n : n + 2]
        right = jnp.concatenate([factor_ref[:, pl.ds(start, LANES)] for start in pair], axis=1)
        term = jnp.dot(coef, right, preferred_element_type=jnp.float32)
        for m in range(len(pair)):
            out_ref[n + m] = term[:, m * LANES : (m + 1) * LANES].astype(out_ref.dtype)


def first_term_kernel(
    rows, cols, ncells, masks, scale_ref, factor_ref, left_ref, right_ref, coef_ref, out_ref
):
    ranks = factor_ref.shape[0] // rows
    lines = cols * rows
    span = LANES // rows

    spread = (
        lax.broadcasted_iota(jnp.int32, (LANES, LANES), 1) // rows
        == lax.broadcasted_iota(jnp.int32, (LANES, LANES), 0)
    ).astype(jnp.bfloat16)
    same = (
        lax.rem(lax.broadcasted_iota(jnp.int32, (lines, LANES), 1), rows)
        == lax.rem(lax.broadcasted_iota(jnp.int32, (lines, LANES), 0), rows)
    ).astype(jnp.float32)
    total = whole(left_ref[...]) + whole(right_ref[...])
    for at in range(0, ranks, LANES):
        count = min(LANES, ranks - at)
        first = at // LANES * cols
        proj = total[first : first + cols]
        scale = scale_ref[:, at : at + count]
        weights = scale * scale / ncells
        if count < LANES:
            weights = jnp.concatenate([weights, jnp.zeros((1, LANES - count), jnp.float32)], axis=1)
        c = proj * weights
        turned = [c if n == 0 else pltpu.roll(c, LANES - n * span, 1) for n in range(rows)]
        stacked = jnp.concatenate(turned, axis=0).astype(jnp.bfloat16)
        wide = jnp.dot(stacked, spread, preferred_element_type=jnp.float32)
        for n in range(rows):
            start = (at + n * span) * rows
            if start >= ranks * rows:
                break
            piece = wide[n * cols : (n + 1) * cols, :]
            piece = jnp.broadcast_to(piece[:, None, :], (cols, rows, LANES)).reshape(lines, LANES)
            coef_ref[:, start : start + LANES] = (piece * same).astype(jnp.bfloat16)
    product(coef_ref[...], starts_of(masks, True), factor_ref, out_ref)


def term_kernel(wanted, coef_ref, factor_ref, *out_refs):
    for (masks, other, _), out_ref in zip(wanted, out_refs):
        product(coef_ref[...], starts_of(masks, other), factor_ref, out_ref)


def add_kernel(mine_ref, got_ref, out_ref):
    out_ref[...] = (mine_ref[...] + got_ref[...].astype(jnp.float32)).astype(out_ref.dtype)


def halve_kernel(*refs):
    part_refs, (keep_ref, send_ref) = refs[:-2], refs[-2:]
    half = keep_ref.shape[0]
    total = part_refs[0][...]
    for ref in part_refs[1:]:
        total = total + ref[...].astype(jnp.float32)
    keep_ref[...] = total[:half]
    send_ref[...] = total[half:].astype(send_ref.dtype)


def local_kernel(rows, cols, halve, b_ref, x_ref, amp_ref, along_ref, twin_ref, beyond_ref, base_ref):
    lines = cols * rows
    odd = lax.rem(lax.axis_index("grp"), 2) == 1
    twin = twin_ref[...].astype(jnp.float32)
    beyond = beyond_ref[...].astype(jnp.float32)
    low = jnp.where(odd, twin, beyond).reshape(cols, rows, LANES)
    high = jnp.where(odd, beyond, twin).reshape(cols, rows, LANES)
    own = along_ref[...].reshape(cols, rows, LANES)
    conv = stencil(low, own, high, ROW_TAPS, 1)
    x = 0.5 * x_ref[...] if halve else x_ref[...]
    scaled = (amp_ref[...][None] * conv).reshape(lines, LANES)
    base_ref[...] = b_ref[...] - (x + scaled)


def update_kernel(count, halve, x_ref, base_ref, *refs):
    term_refs, (new_ref, other_ref) = refs[:count], refs[count:]
    rank_sum = term_refs[0][0].astype(jnp.float32)
    for ref in term_refs[1:]:
        rank_sum = rank_sum + ref[0].astype(jnp.float32)
    x = 0.5 * x_ref[...] if halve else x_ref[...]
    residual = base_ref[...] - rank_sum
    new = x + 0.5 * residual
    new_ref[...] = new
    if other_ref.dtype == jnp.float32:
        other_ref[...] = residual
    else:
        other_ref[0] = new.astype(jnp.bfloat16)


def on_device(right_side, amplitude, factor, scale):
    cols, rows, width = right_side.shape
    ranks = factor.shape[0]
    tiles = lax.axis_size("tile")
    groups = lax.axis_size("grp")
    near = tiles // 2
    lines = cols * rows
    ncells_all = rows * width * groups * tiles
    blocks = -(-ranks // LANES)
    flat = factor.reshape(ranks * rows, tiles * width)
    b = right_side.reshape(lines, width)
    scale = scale.reshape(1, ranks)
    x = b
    short = (0.5 * b).astype(jnp.bfloat16)[None]

    f32, bf16 = jnp.float32, jnp.bfloat16

    def shape(dtype, *dims):
        return jax.ShapeDtypeStruct(dims, dtype)

    def call(kernel, out_shape, flops=0, moved=1 << 18, outside=0, inside=0, **options):
        if outside:
            options["in_specs"] = [pl.BlockSpec(memory_space=pl.ANY)] * outside + [
                pl.BlockSpec(memory_space=pltpu.VMEM)
            ] * inside
        return pl.pallas_call(
            kernel,
            out_shape=out_shape,
            compiler_params=pltpu.CompilerParams(vmem_limit_bytes=32 << 20),
            cost_estimate=pl.CostEstimate(flops=flops, bytes_accessed=moved, transcendentals=0),
            **options,
        )

    work = 2 * lines * ranks * rows * width
    held = call(
        load_kernel,
        shape(bf16, *flat.shape),
        moved=4 * flat.size,
        in_specs=[pl.BlockSpec(memory_space=pltpu.HBM)],
        out_specs=pl.BlockSpec(memory_space=pltpu.VMEM),
        scratch_shapes=[pltpu.SemaphoreType.DMA((8,))],
        name="load",
    )(flat)
    bits = [1 << n for n in range(near.bit_length() - 1)]
    twins = [(i, i ^ 1) for i in range(groups)]
    beyond = [(i, i + 1 if i % 2 else i - 1) for i in range(1, groups - 1)]
    for step in range(ITERS):
        halve = step == 0

        def project(fields, masks, other, before=None, last=False):
            count = 2 * len(masks) * rows * ranks * width
            return call(
                partial(project_kernel, rows, masks, other, last),
                shape(f32, blocks * cols, LANES) if last else shape(f32, blocks * LANES, lines),
                flops=work * len(masks),
                moved=count,
                scratch_shapes=[pltpu.VMEM((blocks * LANES, lines), f32)] if last else [],
                name="project",
            )(fields, held, *([] if before is None else [before]))

        fields, masks = short, [0]
        fresh, fresh_masks = short, [0]
        diag = None
        for at, bit in enumerate(reversed(bits)):
            got = swap(fields, "tile", 2 * bit)
            if at:
                diag = project(fresh, fresh_masks, False, diag)
            size = 2 * len(masks)
            joined = call(
                join_kernel,
                shape(bf16, size, lines, width),
                outside=1,
                inside=2,
                name="join",
            )(held if diag is None else diag, fields, got)
            fresh_masks = [mask ^ bit for mask in masks]
            fresh = got
            masks = masks + fresh_masks
            fields = joined
            if at == 0:
                fresh, fresh_masks = fields, masks
        across = swap(fields, "tile", 1)
        diag = project(fresh, fresh_masks, False, diag)
        proj = project(across, masks, True, diag, True)
        along, along_short = call(
            partial(columns_kernel, masks, halve),
            (shape(f32, lines, width), shape(bf16, lines, width)),
            name="columns",
        )(x, across)
        both = shape(bf16, 2 * blocks * cols, LANES)
        part = call(split_kernel, both, name="split")(proj)
        mask = 1
        while 2 * mask < groups:
            part = call(merge_kernel, both, name="merge")(part, swap(part, "grp", mask))
            mask *= 2
        rest = swap(part, "grp", mask)

        first, second = masks[: near // 2], masks[near // 2 :]
        half = near // 2
        coef, far = call(
            partial(first_term_kernel, rows, cols, ncells_all, second),
            (shape(bf16, lines, ranks * rows), shape(bf16, half, lines, width)),
            flops=work * half,
            moved=flat.size // 2,
            name="term",
        )(scale, held, part, rest)
        got = swap(far, "tile", 1)

        def term(*wanted):
            count = sum(len(masks) for masks, _, _ in wanted)
            return call(
                partial(term_kernel, wanted),
                [shape(dtype, len(masks), lines, width) for masks, _, dtype in wanted],
                flops=work * count,
                moved=flat.size // 2,
                name="term",
            )(coef, held)

        mine, far = term((second, False, f32), (first, True, bf16))
        send = call(add_kernel, shape(bf16, half, lines, width), name="add")(mine, got)
        arrived = swap(send, "tile", 2)
        got = swap(far, "tile", 1)
        (mine,) = term((first, False, f32))
        terms = [mine, got, arrived]
        for bit in bits[1:]:
            half //= 2
            keep, send = call(
                halve_kernel,
                (shape(f32, half, lines, width), shape(bf16, half, lines, width)),
                name="halve",
            )(*terms)
            terms = [keep, swap(send, "tile", 2 * bit)]
        twin = lax.ppermute(along_short, "grp", twins)
        other = lax.ppermute(along_short, "grp", beyond)
        base = call(
            partial(local_kernel, rows, cols, halve), shape(f32, lines, width), name="local"
        )(b, x, amplitude, along, twin, other)
        last = step == ITERS - 1
        x, short = call(
            partial(update_kernel, len(terms), halve),
            (shape(f32, lines, width), shape(f32, lines, width) if last else shape(bf16, 1, lines, width)),
            name="update",
        )(x, base, *terms)
    return x.reshape(cols, rows, width), short.reshape(cols, rows, width)


def solution(mesh):
    in_specs = (P(None, "grp", "tile"), P("grp", "tile"), P("tile", "grp", None), P("tile"))
    out_specs = (P(None, "grp", "tile"), P(None, "grp", "tile"))
    return jax.shard_map(
        on_device, mesh=mesh, in_specs=in_specs, out_specs=out_specs, check_vma=False
    )
```

```python
import math
from functools import partial

import jax
import jax.numpy as jnp
import numpy as np
from jax import lax
from jax.experimental import pallas as pl
from jax.experimental.pallas import tpu as pltpu
from jax.sharding import PartitionSpec as P

REACH = 8
ITERS = 2
LANES = 128


def taper(sigma):
    offsets = np.arange(-REACH, REACH + 1).astype(np.float64)
    values = np.exp(-offsets * offsets / (2.0 * sigma * sigma))
    values = values * np.cos(np.pi * offsets / (2.0 * REACH + 2.0)) ** 2
    return [float(v) for v in (values / values.sum()).astype(np.float32)]


ROW_TAPS = taper(3.0)
COL_TAPS = taper(5.0)


def stencil(low, own, high, taps, axis):
    size = own.shape[axis]
    place = lax.broadcasted_iota(jnp.int32, own.shape, axis)
    total = taps[REACH] * own
    for shift in range(1, REACH + 1):
        after = pltpu.roll(jnp.where(place < shift, high, own), size - shift, axis)
        before = pltpu.roll(jnp.where(place >= size - shift, low, own), shift, axis)
        total = total + taps[REACH + shift] * after + taps[REACH - shift] * before
    return total


def swap(value, axis, mask):
    return lax.ppermute(value, axis, [(i, i ^ mask) for i in range(lax.axis_size(axis))])


def gather_kernel(*refs):
    part_refs, out_ref = refs[1:-1], refs[-1]
    me = lax.div(lax.axis_index("tile"), 2)
    for mask, ref in enumerate(part_refs):
        out_ref[me ^ mask] = ref[...]


def load_kernel(source_ref, out_ref, sems):
    chunks = sems.shape[0]
    count = source_ref.shape[0] // chunks
    copies = [
        pltpu.make_async_copy(
            source_ref.at[pl.ds(n * count, count)], out_ref.at[pl.ds(n * count, count)], sems.at[n]
        )
        for n in range(chunks)
    ]
    for copy in copies:
        copy.start()
    for copy in copies:
        copy.wait()


def diagonal(rows, parity, fields_ref, factor_ref, store):
    near, lines, _ = fields_ref.shape
    count = factor_ref.shape[0]
    field = jnp.concatenate([fields_ref[z] for z in range(near)], axis=1)
    step = min(256, count)
    row_of = lax.broadcasted_iota(jnp.int32, (rows, lines), 0)
    lane_of = lax.broadcasted_iota(jnp.int32, (rows, lines), 1)
    same = (lax.rem(lane_of, rows) == row_of).astype(jnp.float32)
    starts = [pl.multiple_of((2 * z + parity) * LANES, LANES) for z in range(near)]
    for at in range(0, count, step):
        left = jnp.concatenate(
            [factor_ref[at : at + step, pl.ds(start, LANES)] for start in starts], axis=1
        )
        part = lax.dot_general(
            left, field, (((1,), (1,)), ((), ())), preferred_element_type=jnp.float32
        )
        part = part.reshape(step // rows, rows, lines) * same[None]
        store(at // rows, (at + step) // rows, jnp.sum(part, axis=1))


def first_kernel(rows, fields_ref, factor_ref, diag_ref):
    parity = lax.rem(lax.axis_index("tile"), 2)
    ranks = factor_ref.shape[0] // rows
    if diag_ref.shape[0] > ranks:
        diag_ref[...] = jnp.zeros_like(diag_ref)

    def store(start, end, value):
        diag_ref[start:end, :] = value

    diagonal(rows, parity, fields_ref, factor_ref, store)


def second_kernel(
    rows, cols, halve, x_ref, fields_ref, factor_ref, diag_ref, pay_ref, along_ref, total
):
    near = fields_ref.shape[0]
    lines = cols * rows
    me = lax.axis_index("tile")
    parity = lax.rem(me, 2)
    if total.shape[0] > factor_ref.shape[0] // rows:
        total[...] = jnp.zeros_like(total)

    def store(start, end, value):
        total[start:end, :] = diag_ref[start:end, :] + value

    diagonal(rows, 1 - parity, fields_ref, factor_ref, store)
    pick = (
        lax.broadcasted_iota(jnp.int32, (cols, lines), 1) // rows
        == lax.broadcasted_iota(jnp.int32, (cols, lines), 0)
    ).astype(jnp.bfloat16)
    for at in range(0, total.shape[0], LANES):
        part = total[at : at + LANES, :]
        upper = part.astype(jnp.bfloat16)
        lower = (part - upper.astype(jnp.float32)).astype(jnp.bfloat16)
        dims = (((1,), (1,)), ((), ()))
        proj = lax.dot_general(pick, upper, dims, preferred_element_type=jnp.float32)
        proj = proj + lax.dot_general(pick, lower, dims, preferred_element_type=jnp.float32)
        first = at // LANES * 2 * cols
        upper = proj.astype(jnp.bfloat16)
        pay_ref[first : first + cols, :] = upper
        lower = proj - upper.astype(jnp.float32)
        pay_ref[first + cols : first + 2 * cols, :] = lower.astype(jnp.bfloat16)

    head = total.shape[0] // LANES * 2 * cols
    left, right = lax.div(me + 1, 2) - 1, lax.div(me + 1, 2)
    low = fields_ref[jnp.maximum(left, 0)].astype(jnp.float32)
    low = jnp.where(left >= 0, low, 0.0)
    high = fields_ref[jnp.minimum(right, near - 1)].astype(jnp.float32)
    high = jnp.where(right < near, high, 0.0)
    own = 0.5 * x_ref[...] if halve else x_ref[...]
    along = stencil(low, own, high, COL_TAPS, 1)
    along_ref[...] = along
    pay_ref[head:, :] = along.astype(jnp.bfloat16)


def product(parity, coef, factor_ref, out_ref):
    near = out_ref.shape[0]
    pair = 2 if near % 2 == 0 else 1
    for z in range(0, near, pair):
        starts = [pl.multiple_of((2 * (z + n) + parity) * LANES, LANES) for n in range(pair)]
        right = jnp.concatenate([factor_ref[:, pl.ds(start, LANES)] for start in starts], axis=1)
        term = jnp.dot(coef, right, preferred_element_type=jnp.float32)
        for n in range(pair):
            out_ref[z + n] = term[:, n * LANES : (n + 1) * LANES].astype(out_ref.dtype)


def far_kernel(rows, cols, groups, ncells, scale_ref, factor_ref, *refs):
    pay_refs, (coef_ref, out_ref) = refs[:groups], refs[groups:]
    ranks = factor_ref.shape[0] // rows
    lines = cols * rows
    span = LANES // rows

    spread = (
        lax.broadcasted_iota(jnp.int32, (LANES, LANES), 1) // rows
        == lax.broadcasted_iota(jnp.int32, (LANES, LANES), 0)
    ).astype(jnp.bfloat16)
    same = (
        lax.rem(lax.broadcasted_iota(jnp.int32, (lines, LANES), 1), rows)
        == lax.rem(lax.broadcasted_iota(jnp.int32, (lines, LANES), 0), rows)
    ).astype(jnp.float32)
    for at in range(0, ranks, LANES):
        count = min(LANES, ranks - at)
        first = at // LANES * 2 * cols
        both = pay_refs[0][first : first + 2 * cols, :].astype(jnp.float32)
        for ref in pay_refs[1:]:
            both = both + ref[first : first + 2 * cols, :].astype(jnp.float32)
        proj = both[:cols] + both[cols:]
        scale = scale_ref[:, at : at + count]
        weights = scale * scale / ncells
        if count < LANES:
            weights = jnp.concatenate([weights, jnp.zeros((1, LANES - count), jnp.float32)], axis=1)
        c = proj * weights
        turned = [c if n == 0 else pltpu.roll(c, LANES - n * span, 1) for n in range(rows)]
        stacked = jnp.concatenate(turned, axis=0).astype(jnp.bfloat16)
        wide = jnp.dot(stacked, spread, preferred_element_type=jnp.float32)
        for n in range(rows):
            start = (at + n * span) * rows
            if start >= ranks * rows:
                break
            piece = wide[n * cols : (n + 1) * cols, :]
            piece = jnp.broadcast_to(piece[:, None, :], (cols, rows, LANES)).reshape(lines, LANES)
            coef_ref[:, start : start + LANES] = (piece * same).astype(jnp.bfloat16)
    parity = 1 - lax.rem(lax.axis_index("tile"), 2)
    product(parity, coef_ref[...], factor_ref, out_ref)


def near_kernel(coef_ref, factor_ref, out_ref):
    product(lax.rem(lax.axis_index("tile"), 2), coef_ref[...], factor_ref, out_ref)


def pair_kernel(mine_ref, got_ref, out_ref):
    out_ref[...] = (mine_ref[...] + got_ref[...].astype(jnp.float32)).astype(out_ref.dtype)


def local_kernel(rows, cols, halve, b_ref, x_ref, amp_ref, along_ref, *refs):
    pay_refs, base_ref = refs[:-1], refs[-1]
    lines = cols * rows
    head = pay_refs[0].shape[0] - lines
    me = lax.axis_index("grp")
    low = jnp.zeros((lines, LANES), jnp.float32)
    high = low
    for mask, ref in enumerate(pay_refs, 1):
        part = ref[head:, :].astype(jnp.float32)
        low = jnp.where((me ^ mask) == me - 1, part, low)
        high = jnp.where((me ^ mask) == me + 1, part, high)
    low = low.reshape(cols, rows, LANES)
    high = high.reshape(cols, rows, LANES)
    own = along_ref[...].reshape(cols, rows, LANES)
    conv = stencil(low, own, high, ROW_TAPS, 1)
    x = 0.5 * x_ref[...] if halve else x_ref[...]
    scaled = (amp_ref[...][None] * conv).reshape(lines, LANES)
    base_ref[...] = b_ref[...] - (x + scaled)


def update_kernel(halve, x_ref, base_ref, terms_ref, new_ref, other_ref):
    rank_sum = terms_ref[0].astype(jnp.float32)
    for n in range(1, terms_ref.shape[0]):
        rank_sum = rank_sum + terms_ref[n].astype(jnp.float32)
    x = 0.5 * x_ref[...] if halve else x_ref[...]
    residual = base_ref[...] - rank_sum
    new = x + 0.5 * residual
    new_ref[...] = new
    if other_ref.dtype == jnp.float32:
        other_ref[...] = residual
    else:
        short = new.astype(jnp.bfloat16)
        for n in range(other_ref.shape[0]):
            other_ref[n] = short


def on_device(right_side, amplitude, factor, scale):
    cols, rows, width = right_side.shape
    ranks = factor.shape[0]
    tiles = lax.axis_size("tile")
    groups = lax.axis_size("grp")
    near = tiles // 2
    lines = cols * rows
    ncells_all = rows * width * groups * tiles
    blocks = -(-ranks // LANES)
    flat = factor.reshape(ranks * rows, tiles * width)
    b = right_side.reshape(lines, width)
    scale = scale.reshape(1, ranks)
    x = b
    short = (0.5 * b).astype(jnp.bfloat16)
    pay_rows = blocks * 2 * cols + lines

    f32, bf16 = jnp.float32, jnp.bfloat16

    def shape(dtype, *dims):
        return jax.ShapeDtypeStruct(dims, dtype)

    def call(kernel, out_shape, flops=0, moved=1 << 18, **options):
        return pl.pallas_call(
            kernel,
            out_shape=out_shape,
            compiler_params=pltpu.CompilerParams(vmem_limit_bytes=32 * 1024 * 1024),
            cost_estimate=pl.CostEstimate(flops=flops, bytes_accessed=moved, transcendentals=0),
            **options,
        )

    along_z = [[2 * z + core for z in range(near)] for core in range(2)]

    def exchange(value):
        return lax.all_to_all(
            value, "tile", split_axis=0, concat_axis=0, axis_index_groups=along_z, tiled=True
        )

    work = lines * ranks * rows * tiles * width
    held = call(
        load_kernel,
        shape(bf16, *flat.shape),
        moved=4 * flat.size,
        in_specs=[pl.BlockSpec(memory_space=pltpu.HBM)],
        out_specs=pl.BlockSpec(memory_space=pltpu.VMEM),
        scratch_shapes=[pltpu.SemaphoreType.DMA((8,))],
        name="load",
    )(flat)
    for step in range(ITERS):
        halve = step == 0
        if step == 0:
            parts = [swap(short, "tile", 2 * mask) for mask in range(1, near)]
            whole = [pl.BlockSpec(memory_space=pl.ANY)]
            whole += [pl.BlockSpec(memory_space=pltpu.VMEM)] * near
            own = call(
                gather_kernel, shape(bf16, near, lines, width), in_specs=whole, name="order"
            )(held, short, *parts)
        else:
            own = exchange(copies)
        across = swap(own, "tile", 1)
        diag = call(
            partial(first_kernel, rows),
            shape(f32, blocks * LANES, lines),
            flops=work,
            moved=flat.size,
            name="project_own",
        )(own, held)
        pay, along = call(
            partial(second_kernel, rows, cols, halve),
            (shape(bf16, pay_rows, width), shape(f32, lines, width)),
            flops=work,
            moved=flat.size,
            scratch_shapes=[pltpu.VMEM((blocks * LANES, lines), f32)],
            name="project_across",
        )(x, across, held, diag)
        pays = [swap(pay, "grp", mask) for mask in range(1, groups)]
        coef, far = call(
            partial(far_kernel, rows, cols, groups, ncells_all),
            (shape(bf16, lines, ranks * rows), shape(bf16, near, lines, width)),
            flops=work,
            moved=flat.size,
            name="term_across",
        )(scale, held, pay, *pays)
        got = swap(far, "tile", 1)
        mine = call(
            near_kernel,
            shape(f32, near, lines, width),
            flops=work,
            moved=flat.size,
            name="term_own",
        )(coef, held)
        sums = call(pair_kernel, shape(bf16, near, lines, width), name="pair")(mine, got)
        terms = exchange(sums)
        base = call(
            partial(local_kernel, rows, cols, halve), shape(f32, lines, width), name="local"
        )(b, x, amplitude, along, *pays)
        last = step == ITERS - 1
        x, copies = call(
            partial(update_kernel, halve),
            (
                shape(f32, lines, width),
                shape(f32, lines, width) if last else shape(bf16, near, lines, width),
            ),
            name="update",
        )(x, base, terms)
    residual = copies
    return x.reshape(cols, rows, width), residual.reshape(cols, rows, width)


def solution(mesh):
    in_specs = (P(None, "grp", "tile"), P("grp", "tile"), P("tile", "grp", None), P("tile"))
    out_specs = (P(None, "grp", "tile"), P(None, "grp", "tile"))
    return jax.shard_map(
        on_device, mesh=mesh, in_specs=in_specs, out_specs=out_specs, check_vma=False
    )
```

```python
import math
from functools import partial

import jax
import jax.numpy as jnp
import numpy as np
from jax import lax
from jax.experimental import pallas as pl
from jax.experimental.pallas import tpu as pltpu
from jax.sharding import PartitionSpec as P

REACH = 8
ITERS = 2
LANES = 128


def taper(sigma):
    offsets = np.arange(-REACH, REACH + 1).astype(np.float64)
    values = np.exp(-offsets * offsets / (2.0 * sigma * sigma))
    values = values * np.cos(np.pi * offsets / (2.0 * REACH + 2.0)) ** 2
    return [float(v) for v in (values / values.sum()).astype(np.float32)]


ROW_TAPS = taper(3.0)
COL_TAPS = taper(5.0)


def stencil(low, own, high, taps, axis):
    size = own.shape[axis]
    place = lax.broadcasted_iota(jnp.int32, own.shape, axis)
    total = taps[REACH] * own
    for shift in range(1, REACH + 1):
        after = pltpu.roll(jnp.where(place < shift, high, own), size - shift, axis)
        before = pltpu.roll(jnp.where(place >= size - shift, low, own), shift, axis)
        total = total + taps[REACH + shift] * after + taps[REACH - shift] * before
    return total


def swap(value, axis, mask):
    return lax.ppermute(value, axis, [(i, i ^ mask) for i in range(lax.axis_size(axis))])


def gather_kernel(*refs):
    part_refs, out_ref = refs[1:-1], refs[-1]
    me = lax.div(lax.axis_index("tile"), 2)
    for mask, ref in enumerate(part_refs):
        out_ref[me ^ mask] = ref[...]


def load_kernel(source_ref, out_ref, sems):
    chunks = sems.shape[0]
    count = source_ref.shape[0] // chunks
    copies = [
        pltpu.make_async_copy(
            source_ref.at[pl.ds(n * count, count)], out_ref.at[pl.ds(n * count, count)], sems.at[n]
        )
        for n in range(chunks)
    ]
    for copy in copies:
        copy.start()
    for copy in copies:
        copy.wait()


def diagonal(rows, parity, fields_ref, factor_ref, store):
    near, lines, _ = fields_ref.shape
    count = factor_ref.shape[0]
    field = jnp.concatenate([fields_ref[z] for z in range(near)], axis=1)
    step = min(256, count)
    row_of = lax.broadcasted_iota(jnp.int32, (rows, lines), 0)
    lane_of = lax.broadcasted_iota(jnp.int32, (rows, lines), 1)
    same = (lax.rem(lane_of, rows) == row_of).astype(jnp.float32)
    starts = [pl.multiple_of((2 * z + parity) * LANES, LANES) for z in range(near)]
    for at in range(0, count, step):
        left = jnp.concatenate(
            [factor_ref[at : at + step, pl.ds(start, LANES)] for start in starts], axis=1
        )
        part = lax.dot_general(
            left, field, (((1,), (1,)), ((), ())), preferred_element_type=jnp.float32
        )
        part = part.reshape(step // rows, rows, lines) * same[None]
        store(at // rows, (at + step) // rows, jnp.sum(part, axis=1))


def first_kernel(rows, fields_ref, factor_ref, diag_ref):
    parity = lax.rem(lax.axis_index("tile"), 2)
    ranks = factor_ref.shape[0] // rows
    if diag_ref.shape[0] > ranks:
        diag_ref[...] = jnp.zeros_like(diag_ref)

    def store(start, end, value):
        diag_ref[start:end, :] = value

    diagonal(rows, parity, fields_ref, factor_ref, store)


def second_kernel(
    rows, cols, halve, x_ref, fields_ref, factor_ref, diag_ref, pay_ref, part_ref, along_ref, total
):
    near = fields_ref.shape[0]
    lines = cols * rows
    me = lax.axis_index("tile")
    parity = lax.rem(me, 2)
    if total.shape[0] > factor_ref.shape[0] // rows:
        total[...] = jnp.zeros_like(total)

    def store(start, end, value):
        total[start:end, :] = diag_ref[start:end, :] + value

    diagonal(rows, 1 - parity, fields_ref, factor_ref, store)
    pick = (
        lax.broadcasted_iota(jnp.int32, (cols, lines), 1) // rows
        == lax.broadcasted_iota(jnp.int32, (cols, lines), 0)
    ).astype(jnp.bfloat16)
    for at in range(0, total.shape[0], LANES):
        part = total[at : at + LANES, :]
        upper = part.astype(jnp.bfloat16)
        lower = (part - upper.astype(jnp.float32)).astype(jnp.bfloat16)
        dims = (((1,), (1,)), ((), ()))
        proj = lax.dot_general(pick, upper, dims, preferred_element_type=jnp.float32)
        proj = proj + lax.dot_general(pick, lower, dims, preferred_element_type=jnp.float32)
        first = at // LANES * 2 * cols
        upper = proj.astype(jnp.bfloat16)
        lower = (proj - upper.astype(jnp.float32)).astype(jnp.bfloat16)
        for ref in (pay_ref, part_ref):
            ref[first : first + cols, :] = upper
            ref[first + cols : first + 2 * cols, :] = lower

    head = total.shape[0] // LANES * 2 * cols
    left, right = lax.div(me + 1, 2) - 1, lax.div(me + 1, 2)
    low = fields_ref[jnp.maximum(left, 0)].astype(jnp.float32)
    low = jnp.where(left >= 0, low, 0.0)
    high = fields_ref[jnp.minimum(right, near - 1)].astype(jnp.float32)
    high = jnp.where(right < near, high, 0.0)
    own = 0.5 * x_ref[...] if halve else x_ref[...]
    along = stencil(low, own, high, COL_TAPS, 1)
    along_ref[...] = along
    pay_ref[head:, :] = along.astype(jnp.bfloat16)


def product(coef, masks, other, factor_ref, out_ref):
    me = lax.axis_index("tile")
    chip, core = lax.div(me, 2), lax.rem(me, 2)
    core = 1 - core if other else core
    starts = [pl.multiple_of((2 * (chip ^ mask) + core) * LANES, LANES) for mask in masks]
    for n in range(0, len(starts), 2):
        pair = starts[n : n + 2]
        right = jnp.concatenate([factor_ref[:, pl.ds(start, LANES)] for start in pair], axis=1)
        term = jnp.dot(coef, right, preferred_element_type=jnp.float32)
        for m in range(len(pair)):
            out_ref[n + m] = term[:, m * LANES : (m + 1) * LANES].astype(out_ref.dtype)


def far_kernel(rows, cols, groups, ncells, masks, scale_ref, factor_ref, *refs):
    pay_refs, (coef_ref, out_ref) = refs[:groups], refs[groups:]
    ranks = factor_ref.shape[0] // rows
    lines = cols * rows
    span = LANES // rows

    spread = (
        lax.broadcasted_iota(jnp.int32, (LANES, LANES), 1) // rows
        == lax.broadcasted_iota(jnp.int32, (LANES, LANES), 0)
    ).astype(jnp.bfloat16)
    same = (
        lax.rem(lax.broadcasted_iota(jnp.int32, (lines, LANES), 1), rows)
        == lax.rem(lax.broadcasted_iota(jnp.int32, (lines, LANES), 0), rows)
    ).astype(jnp.float32)
    for at in range(0, ranks, LANES):
        count = min(LANES, ranks - at)
        first = at // LANES * 2 * cols
        both = pay_refs[0][first : first + 2 * cols, :].astype(jnp.float32)
        for ref in pay_refs[1:]:
            both = both + ref[first : first + 2 * cols, :].astype(jnp.float32)
        proj = both[:cols] + both[cols:]
        scale = scale_ref[:, at : at + count]
        weights = scale * scale / ncells
        if count < LANES:
            weights = jnp.concatenate([weights, jnp.zeros((1, LANES - count), jnp.float32)], axis=1)
        c = proj * weights
        turned = [c if n == 0 else pltpu.roll(c, LANES - n * span, 1) for n in range(rows)]
        stacked = jnp.concatenate(turned, axis=0).astype(jnp.bfloat16)
        wide = jnp.dot(stacked, spread, preferred_element_type=jnp.float32)
        for n in range(rows):
            start = (at + n * span) * rows
            if start >= ranks * rows:
                break
            piece = wide[n * cols : (n + 1) * cols, :]
            piece = jnp.broadcast_to(piece[:, None, :], (cols, rows, LANES)).reshape(lines, LANES)
            coef_ref[:, start : start + LANES] = (piece * same).astype(jnp.bfloat16)
    product(coef_ref[...], masks, True, factor_ref, out_ref)


def term_kernel(wanted, after, coef_ref, factor_ref, *refs):
    for (masks, other, _), out_ref in zip(wanted, refs[after:]):
        product(coef_ref[...], masks, other, factor_ref, out_ref)


def pair_kernel(mine_ref, got_ref, *out_refs):
    for n, ref in enumerate(out_refs):
        ref[...] = (mine_ref[n] + got_ref[n].astype(jnp.float32)).astype(ref.dtype)


def local_kernel(rows, cols, halve, b_ref, x_ref, amp_ref, along_ref, *refs):
    pay_refs, base_ref = refs[:-1], refs[-1]
    lines = cols * rows
    head = pay_refs[0].shape[0] - lines
    me = lax.axis_index("grp")
    low = jnp.zeros((lines, LANES), jnp.float32)
    high = low
    for n, ref in enumerate(pay_refs, 1):
        mask = (1 << n) - 1
        part = ref[head:, :].astype(jnp.float32)
        low = jnp.where((me ^ mask) == me - 1, part, low)
        high = jnp.where((me ^ mask) == me + 1, part, high)
    low = low.reshape(cols, rows, LANES)
    high = high.reshape(cols, rows, LANES)
    own = along_ref[...].reshape(cols, rows, LANES)
    conv = stencil(low, own, high, ROW_TAPS, 1)
    x = 0.5 * x_ref[...] if halve else x_ref[...]
    scaled = (amp_ref[...][None] * conv).reshape(lines, LANES)
    base_ref[...] = b_ref[...] - (x + scaled)


def update_kernel(near, halve, x_ref, base_ref, *refs):
    term_refs, out_refs = refs[:near], refs[near:]
    rank_sum = term_refs[0][...]
    for ref in term_refs[1:]:
        rank_sum = rank_sum + ref[...].astype(jnp.float32)
    x = 0.5 * x_ref[...] if halve else x_ref[...]
    residual = base_ref[...] - rank_sum
    new = x + 0.5 * residual
    out_refs[0][...] = new
    if len(out_refs) > 1:
        out_refs[1][...] = residual if out_refs[1].dtype == jnp.float32 else new.astype(jnp.bfloat16)


def on_device(right_side, amplitude, factor, scale):
    cols, rows, width = right_side.shape
    ranks = factor.shape[0]
    tiles = lax.axis_size("tile")
    groups = lax.axis_size("grp")
    near = tiles // 2
    lines = cols * rows
    ncells_all = rows * width * groups * tiles
    blocks = -(-ranks // LANES)
    flat = factor.reshape(ranks * rows, tiles * width)
    b = right_side.reshape(lines, width)
    scale = scale.reshape(1, ranks)
    x = b
    short = (0.5 * b).astype(jnp.bfloat16)
    pay_rows = blocks * 2 * cols + lines

    f32, bf16 = jnp.float32, jnp.bfloat16

    def shape(dtype, *dims):
        return jax.ShapeDtypeStruct(dims, dtype)

    def call(kernel, out_shape, flops=0, moved=1 << 18, **options):
        return pl.pallas_call(
            kernel,
            out_shape=out_shape,
            compiler_params=pltpu.CompilerParams(vmem_limit_bytes=32 * 1024 * 1024),
            cost_estimate=pl.CostEstimate(flops=flops, bytes_accessed=moved, transcendentals=0),
            **options,
        )

    work = lines * ranks * rows * tiles * width
    held = call(
        load_kernel,
        shape(bf16, *flat.shape),
        moved=4 * flat.size,
        in_specs=[pl.BlockSpec(memory_space=pltpu.HBM)],
        out_specs=pl.BlockSpec(memory_space=pltpu.VMEM),
        scratch_shapes=[pltpu.SemaphoreType.DMA((8,))],
        name="load",
    )(flat)
    for step in range(ITERS):
        halve = step == 0
        parts = [swap(short, "tile", 2 * mask) for mask in range(1, near)]
        whole = [pl.BlockSpec(memory_space=pl.ANY)] + [pl.BlockSpec(memory_space=pltpu.VMEM)] * near
        own = call(
            gather_kernel, shape(bf16, near, lines, width), in_specs=whole, name="order"
        )(held, short, *parts)
        across = swap(own, "tile", 1)
        diag = call(
            partial(first_kernel, rows),
            shape(f32, blocks * LANES, lines),
            flops=work,
            moved=flat.size,
            name="project_own",
        )(own, held)
        pay, part, along = call(
            partial(second_kernel, rows, cols, halve),
            (
                shape(bf16, pay_rows, width),
                shape(bf16, pay_rows - lines, width),
                shape(f32, lines, width),
            ),
            flops=work,
            moved=flat.size,
            scratch_shapes=[pltpu.VMEM((blocks * LANES, lines), f32)],
            name="project_across",
        )(x, across, held, diag)
        pays = [swap(part if mask & (mask + 1) else pay, "grp", mask) for mask in range(1, groups)]
        half = near // 2
        close, away = list(range(half)), list(range(near - 1, half - 1, -1))
        coef, far = call(
            partial(far_kernel, rows, cols, groups, ncells_all, away),
            (shape(bf16, lines, ranks * rows), shape(bf16, half, lines, width)),
            flops=work // 2,
            moved=flat.size,
            name="term_first",
        )(scale, held, part, *pays)
        got = swap(far, "tile", 1)

        def term(*wanted, after=()):
            return call(
                partial(term_kernel, wanted, len(after)),
                in_specs=[pl.BlockSpec(memory_space=pltpu.VMEM)] * 2
                + [pl.BlockSpec(memory_space=pl.ANY)] * len(after),
                out_shape=[shape(dtype, len(masks), lines, width) for masks, _, dtype in wanted],
                flops=work // 2 * len(wanted),
                moved=flat.size,
                name="term",
            )(coef, held, *after)

        def pair(mine, got, masks):
            return call(
                pair_kernel,
                [shape(bf16 if mask else f32, lines, width) for mask in masks],
                name="pair",
            )(mine, got)

        mine, far = term((away, False, f32), (close, True, bf16))
        sends = pair(mine, got, away)
        terms = [swap(send, "tile", 2 * mask) for send, mask in zip(sends, away)]
        got = swap(far, "tile", 1)
        (mine,) = term((close, False, f32), after=sends)
        kept, *sends = pair(mine, got, close)
        terms += [swap(send, "tile", 2 * mask) for send, mask in zip(sends, close[1:])]
        rims = [pay for mask, pay in enumerate(pays, 1) if not mask & (mask + 1)]
        base = call(
            partial(local_kernel, rows, cols, halve), shape(f32, lines, width), name="local"
        )(b, x, amplitude, along, *rims)
        last = step == ITERS - 1
        x, residual = call(
            partial(update_kernel, near, halve),
            (shape(f32, lines, width), shape(f32 if last else bf16, lines, width)),
            name="update",
        )(x, base, kept, *terms)
        short = residual
    return x.reshape(cols, rows, width), residual.reshape(cols, rows, width)


def solution(mesh):
    in_specs = (P(None, "grp", "tile"), P("grp", "tile"), P("tile", "grp", None), P("tile"))
    out_specs = (P(None, "grp", "tile"), P(None, "grp", "tile"))
    return jax.shard_map(
        on_device, mesh=mesh, in_specs=in_specs, out_specs=out_specs, check_vma=False
    )
```

```python
import math
from functools import partial

import jax
import jax.numpy as jnp
import numpy as np
from jax import lax
from jax.experimental import pallas as pl
from jax.experimental.pallas import tpu as pltpu
from jax.sharding import PartitionSpec as P

REACH = 8
ITERS = 2
LANES = 128


def taper(sigma):
    offsets = np.arange(-REACH, REACH + 1).astype(np.float64)
    values = np.exp(-offsets * offsets / (2.0 * sigma * sigma))
    values = values * np.cos(np.pi * offsets / (2.0 * REACH + 2.0)) ** 2
    return [float(v) for v in (values / values.sum()).astype(np.float32)]


ROW_TAPS = taper(3.0)
COL_TAPS = taper(5.0)


def stencil(low, own, high, taps, axis):
    size = own.shape[axis]
    place = lax.broadcasted_iota(jnp.int32, own.shape, axis)
    total = taps[REACH] * own
    for shift in range(1, REACH + 1):
        after = pltpu.roll(jnp.where(place < shift, high, own), size - shift, axis)
        before = pltpu.roll(jnp.where(place >= size - shift, low, own), shift, axis)
        total = total + taps[REACH + shift] * after + taps[REACH - shift] * before
    return total


def swap(value, axis, mask):
    return lax.ppermute(value, axis, [(i, i ^ mask) for i in range(lax.axis_size(axis))])


def place_of(spot):
    even, odd, which = spot
    me = lax.axis_index("tile")
    chip, core = lax.div(me, 2), lax.rem(me, 2)
    chip = chip ^ jnp.where(core == 0, even, odd)
    if which == "own":
        which = core
    elif which == "other":
        which = 1 - core
    return 2 * chip + which


def columns_of(spots):
    return [pl.multiple_of(place_of(spot) * LANES, LANES) for spot in spots]


def duo_kernel(short_ref, twin_ref, out_ref):
    core = lax.rem(lax.axis_index("tile"), 2)
    out_ref[core] = short_ref[0]
    out_ref[1 - core] = twin_ref[0]


def join_kernel(*refs):
    part_refs, out_ref = refs[1:-1], refs[-1]
    at = 0
    for ref in part_refs:
        out_ref[at : at + ref.shape[0]] = ref[...]
        at += ref.shape[0]


def load_kernel(source_ref, out_ref, sems):
    chunks = sems.shape[0]
    count = source_ref.shape[0] // chunks
    copies = [
        pltpu.make_async_copy(
            source_ref.at[pl.ds(n * count, count)], out_ref.at[pl.ds(n * count, count)], sems.at[n]
        )
        for n in range(chunks)
    ]
    for copy in copies:
        copy.start()
    for copy in copies:
        copy.wait()


def diagonal(rows, spots, fields, factor_ref, store):
    lines = fields[0].shape[0]
    count = factor_ref.shape[0]
    field = jnp.concatenate(fields, axis=1)
    step = min(256, count)
    row_of = lax.broadcasted_iota(jnp.int32, (rows, lines), 0)
    lane_of = lax.broadcasted_iota(jnp.int32, (rows, lines), 1)
    same = (lax.rem(lane_of, rows) == row_of).astype(jnp.float32)
    starts = columns_of(spots)
    for at in range(0, count, step):
        left = jnp.concatenate(
            [factor_ref[at : at + step, pl.ds(start, LANES)] for start in starts], axis=1
        )
        part = lax.dot_general(
            left, field, (((1,), (1,)), ((), ())), preferred_element_type=jnp.float32
        )
        part = part.reshape(step // rows, rows, lines) * same[None]
        store(at // rows, (at + step) // rows, jnp.sum(part, axis=1))


def blocks_of(refs):
    return [ref[n] for ref in refs for n in range(ref.shape[0])]


def first_kernel(rows, spots, added, factor_ref, *refs):
    diag_ref = refs[-1]
    field_refs = refs[: len(refs) - 1 - added]
    ranks = factor_ref.shape[0] // rows
    if diag_ref.shape[0] > ranks:
        diag_ref[...] = jnp.zeros_like(diag_ref)

    def store(start, end, value):
        diag_ref[start:end, :] = refs[-2][start:end, :] + value if added else value

    diagonal(rows, spots, blocks_of(field_refs), factor_ref, store)


def second_kernel(rows, cols, halve, spots, known, x_ref, factor_ref, diag_ref, fields_ref, *refs):
    other_refs, (pay_ref, part_ref, along_ref, total) = refs[:-4], refs[-4:]
    lines = cols * rows
    if total.shape[0] > factor_ref.shape[0] // rows:
        total[...] = jnp.zeros_like(total)

    def store(start, end, value):
        total[start:end, :] = diag_ref[start:end, :] + value

    diagonal(rows, spots, blocks_of([fields_ref]), factor_ref, store)
    pick = (
        lax.broadcasted_iota(jnp.int32, (cols, lines), 1) // rows
        == lax.broadcasted_iota(jnp.int32, (cols, lines), 0)
    ).astype(jnp.bfloat16)
    for at in range(0, total.shape[0], LANES):
        part = total[at : at + LANES, :]
        upper = part.astype(jnp.bfloat16)
        lower = (part - upper.astype(jnp.float32)).astype(jnp.bfloat16)
        dims = (((1,), (1,)), ((), ()))
        proj = lax.dot_general(pick, upper, dims, preferred_element_type=jnp.float32)
        proj = proj + lax.dot_general(pick, lower, dims, preferred_element_type=jnp.float32)
        first = at // LANES * 2 * cols
        upper = proj.astype(jnp.bfloat16)
        lower = (proj - upper.astype(jnp.float32)).astype(jnp.bfloat16)
        for ref in (pay_ref, part_ref):
            ref[first : first + cols, :] = upper
            ref[first + cols : first + 2 * cols, :] = lower

    head = total.shape[0] // LANES * 2 * cols
    me = lax.axis_index("tile")
    low = jnp.zeros((lines, LANES), jnp.float32)
    high = low
    for spot, block in zip(spots + known, blocks_of((fields_ref,) + other_refs)):
        part, place = block.astype(jnp.float32), place_of(spot)
        low = jnp.where(place == me - 1, part, low)
        high = jnp.where(place == me + 1, part, high)
    own = 0.5 * x_ref[...] if halve else x_ref[...]
    along = stencil(low, own, high, COL_TAPS, 1)
    along_ref[...] = along
    pay_ref[head:, :] = along.astype(jnp.bfloat16)


def product(coef, spots, factor_ref, out_ref):
    starts = columns_of(spots)
    for n in range(0, len(starts), 2):
        pair = starts[n : n + 2]
        right = jnp.concatenate([factor_ref[:, pl.ds(start, LANES)] for start in pair], axis=1)
        term = jnp.dot(coef, right, preferred_element_type=jnp.float32)
        for m in range(len(pair)):
            out_ref[n + m] = term[:, m * LANES : (m + 1) * LANES].astype(out_ref.dtype)


def far_kernel(rows, cols, groups, ncells, spots, scale_ref, factor_ref, *refs):
    pay_refs, (coef_ref, out_ref) = refs[:groups], refs[groups:]
    ranks = factor_ref.shape[0] // rows
    lines = cols * rows
    span = LANES // rows

    spread = (
        lax.broadcasted_iota(jnp.int32, (LANES, LANES), 1) // rows
        == lax.broadcasted_iota(jnp.int32, (LANES, LANES), 0)
    ).astype(jnp.bfloat16)
    same = (
        lax.rem(lax.broadcasted_iota(jnp.int32, (lines, LANES), 1), rows)
        == lax.rem(lax.broadcasted_iota(jnp.int32, (lines, LANES), 0), rows)
    ).astype(jnp.float32)
    for at in range(0, ranks, LANES):
        count = min(LANES, ranks - at)
        first = at // LANES * 2 * cols
        both = pay_refs[0][first : first + 2 * cols, :].astype(jnp.float32)
        for ref in pay_refs[1:]:
            both = both + ref[first : first + 2 * cols, :].astype(jnp.float32)
        proj = both[:cols] + both[cols:]
        scale = scale_ref[:, at : at + count]
        weights = scale * scale / ncells
        if count < LANES:
            weights = jnp.concatenate([weights, jnp.zeros((1, LANES - count), jnp.float32)], axis=1)
        c = proj * weights
        turned = [c if n == 0 else pltpu.roll(c, LANES - n * span, 1) for n in range(rows)]
        stacked = jnp.concatenate(turned, axis=0).astype(jnp.bfloat16)
        wide = jnp.dot(stacked, spread, preferred_element_type=jnp.float32)
        for n in range(rows):
            start = (at + n * span) * rows
            if start >= ranks * rows:
                break
            piece = wide[n * cols : (n + 1) * cols, :]
            piece = jnp.broadcast_to(piece[:, None, :], (cols, rows, LANES)).reshape(lines, LANES)
            coef_ref[:, start : start + LANES] = (piece * same).astype(jnp.bfloat16)
    product(coef_ref[...], spots, factor_ref, out_ref)


def term_kernel(wanted, after, coef_ref, factor_ref, *refs):
    for (spots, _), out_ref in zip(wanted, refs[after:]):
        product(coef_ref[...], spots, factor_ref, out_ref)


def pair_kernel(mine_ref, got_ref, *out_refs):
    at = 0
    for ref in out_refs:
        end = at + ref.shape[0]
        ref[...] = (mine_ref[at:end] + got_ref[at:end].astype(jnp.float32)).astype(ref.dtype)
        at = end


def give_kernel(*refs):
    part_refs, out_ref = refs[:-1], refs[-1]
    other = 1 - lax.rem(lax.axis_index("tile"), 2)
    total = part_refs[0][other].astype(jnp.float32)
    for ref in part_refs[1:]:
        total = total + ref[other].astype(jnp.float32)
    out_ref[...] = total.astype(out_ref.dtype)


def local_kernel(rows, cols, halve, b_ref, x_ref, amp_ref, along_ref, *refs):
    pay_refs, base_ref = refs[:-1], refs[-1]
    lines = cols * rows
    head = pay_refs[0].shape[0] - lines
    me = lax.axis_index("grp")
    low = jnp.zeros((lines, LANES), jnp.float32)
    high = low
    for n, ref in enumerate(pay_refs, 1):
        mask = (1 << n) - 1
        part = ref[head:, :].astype(jnp.float32)
        low = jnp.where((me ^ mask) == me - 1, part, low)
        high = jnp.where((me ^ mask) == me + 1, part, high)
    low = low.reshape(cols, rows, LANES)
    high = high.reshape(cols, rows, LANES)
    own = along_ref[...].reshape(cols, rows, LANES)
    conv = stencil(low, own, high, ROW_TAPS, 1)
    x = 0.5 * x_ref[...] if halve else x_ref[...]
    scaled = (amp_ref[...][None] * conv).reshape(lines, LANES)
    base_ref[...] = b_ref[...] - (x + scaled)


def update_kernel(halve, last, x_ref, base_ref, kept_ref, one_ref, given_ref, *refs):
    part_refs, (new_ref, other_ref) = refs[:-2], refs[-2:]
    core = lax.rem(lax.axis_index("tile"), 2)
    rank_sum = kept_ref[0] + one_ref[0].astype(jnp.float32) + given_ref[...].astype(jnp.float32)
    for ref in part_refs:
        rank_sum = rank_sum + ref[core].astype(jnp.float32)
    x = 0.5 * x_ref[...] if halve else x_ref[...]
    residual = base_ref[...] - rank_sum
    new = x + 0.5 * residual
    new_ref[...] = new
    if last:
        other_ref[...] = residual
    else:
        other_ref[0] = new.astype(jnp.bfloat16)


def on_device(right_side, amplitude, factor, scale):
    cols, rows, width = right_side.shape
    ranks = factor.shape[0]
    tiles = lax.axis_size("tile")
    groups = lax.axis_size("grp")
    near = tiles // 2
    lines = cols * rows
    ncells_all = rows * width * groups * tiles
    blocks = -(-ranks // LANES)
    flat = factor.reshape(ranks * rows, tiles * width)
    b = right_side.reshape(lines, width)
    scale = scale.reshape(1, ranks)
    x = b
    short = (0.5 * b).astype(jnp.bfloat16)[None]
    pay_rows = blocks * 2 * cols + lines

    f32, bf16 = jnp.float32, jnp.bfloat16

    def shape(dtype, *dims):
        return jax.ShapeDtypeStruct(dims, dtype)

    def call(kernel, out_shape, flops=0, moved=1 << 18, **options):
        return pl.pallas_call(
            kernel,
            out_shape=out_shape,
            compiler_params=pltpu.CompilerParams(vmem_limit_bytes=32 * 1024 * 1024),
            cost_estimate=pl.CostEstimate(flops=flops, bytes_accessed=moved, transcendentals=0),
            **options,
        )

    work = lines * ranks * rows * tiles * width
    held = call(
        load_kernel,
        shape(bf16, *flat.shape),
        moved=4 * flat.size,
        in_specs=[pl.BlockSpec(memory_space=pltpu.HBM)],
        out_specs=pl.BlockSpec(memory_space=pltpu.VMEM),
        scratch_shapes=[pltpu.SemaphoreType.DMA((8,))],
        name="load",
    )(flat)
    rounds = [
        [(2 * (chip ^ (2 * n + 1 - core)) + core) for chip in range(near) for core in range(2)]
        for n in range(near // 2 - 1, 0, -1)
    ]
    own_away = [(2 * n + 1, 2 * n, q) for n in range(near // 2 - 1, 0, -1) for q in range(2)]
    other_away = [(2 * n, 2 * n + 1, q) for n in range(near // 2 - 1, 0, -1) for q in range(2)]
    home = [(0, 0, 0), (0, 0, 1)]
    own_close = [(0, 0, "own"), (1, 1, "own")]
    other_close = [(0, 0, "other"), (1, 1, "other")]

    def travel(value, targets):
        return lax.ppermute(value, "tile", list(enumerate(targets)))

    def first(fields, spots, *before):
        return call(
            partial(first_kernel, rows, spots, len(before)),
            shape(f32, blocks * LANES, lines),
            flops=work,
            moved=flat.size,
            name="project_own",
        )(held, *fields, *before)

    for step in range(ITERS):
        halve = step == 0
        twin = swap(short, "tile", 1)
        one = swap(short, "tile", 2)
        duo = call(duo_kernel, shape(bf16, 2, lines, width), name="duo")(short, twin)
        gots = [travel(duo, targets) for targets in rounds]
        diag = first([duo], home)
        bundle = call(
            join_kernel,
            shape(bf16, near - 1, lines, width),
            in_specs=[pl.BlockSpec(memory_space=pl.ANY)]
            + [pl.BlockSpec(memory_space=pltpu.VMEM)] * (len(gots) + 1),
            name="join",
        )(diag, *gots, one)
        across = swap(bundle, "tile", 1)
        diag = first([bundle], own_away + own_close[1:], diag)
        spots = other_away + other_close[1:]
        pay, part, along = call(
            partial(second_kernel, rows, cols, halve, spots, home + own_away + own_close[1:]),
            (
                shape(bf16, pay_rows, width),
                shape(bf16, pay_rows - lines, width),
                shape(f32, lines, width),
            ),
            flops=work,
            moved=flat.size,
            scratch_shapes=[pltpu.VMEM((blocks * LANES, lines), f32)],
            name="project_across",
        )(x, held, diag, across, duo, bundle)
        pays = [swap(part if mask & (mask + 1) else pay, "grp", mask) for mask in range(1, groups)]
        coef, far = call(
            partial(far_kernel, rows, cols, groups, ncells_all, other_away),
            (shape(bf16, lines, ranks * rows), shape(bf16, near - 2, lines, width)),
            flops=work // 2,
            moved=flat.size,
            name="term_first",
        )(scale, held, part, *pays)
        got = swap(far, "tile", 1)

        def term(*wanted, after=()):
            return call(
                partial(term_kernel, wanted, len(after)),
                in_specs=[pl.BlockSpec(memory_space=pltpu.VMEM)] * 2
                + [pl.BlockSpec(memory_space=pl.ANY)] * len(after),
                out_shape=[shape(dtype, len(spots), lines, width) for spots, dtype in wanted],
                flops=work // 2 * len(wanted),
                moved=flat.size,
                name="term",
            )(coef, held, *after)

        mine, far = term((own_away, f32), (other_close, bf16))
        sends = call(
            pair_kernel, [shape(bf16, 2, lines, width) for _ in rounds], name="pair"
        )(mine, got)
        terms = [travel(send, targets) for send, targets in zip(sends, rounds)]
        got = swap(far, "tile", 1)
        (mine,) = term((own_close, f32), after=sends)
        kept, send = call(
            pair_kernel,
            [shape(f32, 1, lines, width), shape(bf16, 1, lines, width)],
            name="pair",
        )(mine, got)
        close = swap(send, "tile", 2)
        given = swap(call(give_kernel, shape(bf16, lines, width), name="give")(*terms), "tile", 1)
        rims = [pay for mask, pay in enumerate(pays, 1) if not mask & (mask + 1)]
        base = call(
            partial(local_kernel, rows, cols, halve), shape(f32, lines, width), name="local"
        )(b, x, amplitude, along, *rims)
        last = step == ITERS - 1
        x, short = call(
            partial(update_kernel, halve, last),
            (
                shape(f32, lines, width),
                shape(f32, lines, width) if last else shape(bf16, 1, lines, width),
            ),
            name="update",
        )(x, base, kept, close, given, *terms)
    return x.reshape(cols, rows, width), short.reshape(cols, rows, width)


def solution(mesh):
    in_specs = (P(None, "grp", "tile"), P("grp", "tile"), P("tile", "grp", None), P("tile"))
    out_specs = (P(None, "grp", "tile"), P(None, "grp", "tile"))
    return jax.shard_map(
        on_device, mesh=mesh, in_specs=in_specs, out_specs=out_specs, check_vma=False
    )
```

```python
import math
from functools import partial

import jax
import jax.numpy as jnp
import numpy as np
from jax import lax
from jax.experimental import pallas as pl
from jax.experimental.pallas import tpu as pltpu
from jax.sharding import PartitionSpec as P

REACH = 8
ITERS = 2
LANES = 128


def taper(sigma):
    offsets = np.arange(-REACH, REACH + 1).astype(np.float64)
    values = np.exp(-offsets * offsets / (2.0 * sigma * sigma))
    values = values * np.cos(np.pi * offsets / (2.0 * REACH + 2.0)) ** 2
    return [float(v) for v in (values / values.sum()).astype(np.float32)]


ROW_TAPS = taper(3.0)
COL_TAPS = taper(5.0)


def stencil(low, own, high, taps, axis):
    size = own.shape[axis]
    place = lax.broadcasted_iota(jnp.int32, own.shape, axis)
    total = taps[REACH] * own
    for shift in range(1, REACH + 1):
        after = pltpu.roll(jnp.where(place < shift, high, own), size - shift, axis)
        before = pltpu.roll(jnp.where(place >= size - shift, low, own), shift, axis)
        total = total + taps[REACH + shift] * after + taps[REACH - shift] * before
    return total


def swap(value, axis, mask):
    return lax.ppermute(value, axis, [(i, i ^ mask) for i in range(lax.axis_size(axis))])


def gather_kernel(masks, *refs):
    part_refs, out_ref = refs[1:-1], refs[-1]
    me = lax.div(lax.axis_index("tile"), 2)
    for mask, ref in zip(masks, part_refs):
        out_ref[me ^ mask] = ref[...]


def load_kernel(source_ref, out_ref, sems):
    chunks = sems.shape[0]
    count = source_ref.shape[0] // chunks
    copies = [
        pltpu.make_async_copy(
            source_ref.at[pl.ds(n * count, count)], out_ref.at[pl.ds(n * count, count)], sems.at[n]
        )
        for n in range(chunks)
    ]
    for copy in copies:
        copy.start()
    for copy in copies:
        copy.wait()


def diagonal(rows, parity, fields_ref, factor_ref, store):
    near, lines, _ = fields_ref.shape
    count = factor_ref.shape[0]
    field = jnp.concatenate([fields_ref[z] for z in range(near)], axis=1)
    step = min(1024, count)
    row_of = lax.broadcasted_iota(jnp.int32, (rows, lines), 0)
    lane_of = lax.broadcasted_iota(jnp.int32, (rows, lines), 1)
    same = (lax.rem(lane_of, rows) == row_of).astype(jnp.float32)
    starts = [pl.multiple_of((2 * z + parity) * LANES, LANES) for z in range(near)]
    for at in range(0, count, step):
        left = jnp.concatenate(
            [factor_ref[at : at + step, pl.ds(start, LANES)] for start in starts], axis=1
        )
        part = lax.dot_general(
            left, field, (((1,), (1,)), ((), ())), preferred_element_type=jnp.float32
        )
        part = part.reshape(step // rows, rows, lines) * same[None]
        store(at // rows, (at + step) // rows, jnp.sum(part, axis=1))


def first_kernel(rows, fields_ref, factor_ref, diag_ref):
    parity = lax.rem(lax.axis_index("tile"), 2)
    ranks = factor_ref.shape[0] // rows
    if diag_ref.shape[0] > ranks:
        diag_ref[...] = jnp.zeros_like(diag_ref)

    def store(start, end, value):
        diag_ref[start:end, :] = value

    diagonal(rows, parity, fields_ref, factor_ref, store)


def second_kernel(
    rows, cols, halve, x_ref, fields_ref, factor_ref, diag_ref, pay_ref, part_ref, along_ref, total
):
    near = fields_ref.shape[0]
    lines = cols * rows
    me = lax.axis_index("tile")
    parity = lax.rem(me, 2)
    if total.shape[0] > factor_ref.shape[0] // rows:
        total[...] = jnp.zeros_like(total)

    def store(start, end, value):
        total[start:end, :] = diag_ref[start:end, :] + value

    diagonal(rows, 1 - parity, fields_ref, factor_ref, store)
    pick = (
        lax.broadcasted_iota(jnp.int32, (cols, lines), 1) // rows
        == lax.broadcasted_iota(jnp.int32, (cols, lines), 0)
    ).astype(jnp.bfloat16)
    for at in range(0, total.shape[0], LANES):
        part = total[at : at + LANES, :]
        upper = part.astype(jnp.bfloat16)
        lower = (part - upper.astype(jnp.float32)).astype(jnp.bfloat16)
        dims = (((1,), (1,)), ((), ()))
        proj = lax.dot_general(pick, upper, dims, preferred_element_type=jnp.float32)
        proj = proj + lax.dot_general(pick, lower, dims, preferred_element_type=jnp.float32)
        first = at // LANES * 2 * cols
        upper = proj.astype(jnp.bfloat16)
        lower = (proj - upper.astype(jnp.float32)).astype(jnp.bfloat16)
        for ref in (pay_ref, part_ref):
            ref[first : first + cols, :] = upper
            ref[first + cols : first + 2 * cols, :] = lower

    head = total.shape[0] // LANES * 2 * cols
    left, right = lax.div(me + 1, 2) - 1, lax.div(me + 1, 2)
    low = fields_ref[jnp.maximum(left, 0)].astype(jnp.float32)
    low = jnp.where(left >= 0, low, 0.0)
    high = fields_ref[jnp.minimum(right, near - 1)].astype(jnp.float32)
    high = jnp.where(right < near, high, 0.0)
    own = 0.5 * x_ref[...] if halve else x_ref[...]
    along = stencil(low, own, high, COL_TAPS, 1)
    along_ref[...] = along
    pay_ref[head:, :] = along.astype(jnp.bfloat16)


def product(coef, masks, other, factor_ref, out_ref):
    me = lax.axis_index("tile")
    chip, core = lax.div(me, 2), lax.rem(me, 2)
    core = 1 - core if other else core
    starts = [pl.multiple_of((2 * (chip ^ mask) + core) * LANES, LANES) for mask in masks]
    for n in range(0, len(starts), 2):
        pair = starts[n : n + 2]
        right = jnp.concatenate([factor_ref[:, pl.ds(start, LANES)] for start in pair], axis=1)
        term = jnp.dot(coef, right, preferred_element_type=jnp.float32)
        for m in range(len(pair)):
            out_ref[n + m] = term[:, m * LANES : (m + 1) * LANES].astype(out_ref.dtype)


def far_kernel(rows, cols, groups, ncells, masks, scale_ref, factor_ref, *refs):
    pay_refs, (coef_ref, out_ref) = refs[:groups], refs[groups:]
    ranks = factor_ref.shape[0] // rows
    lines = cols * rows
    span = LANES // rows

    spread = (
        lax.broadcasted_iota(jnp.int32, (LANES, LANES), 1) // rows
        == lax.broadcasted_iota(jnp.int32, (LANES, LANES), 0)
    ).astype(jnp.bfloat16)
    same = (
        lax.rem(lax.broadcasted_iota(jnp.int32, (lines, LANES), 1), rows)
        == lax.rem(lax.broadcasted_iota(jnp.int32, (lines, LANES), 0), rows)
    ).astype(jnp.float32)
    for at in range(0, ranks, LANES):
        count = min(LANES, ranks - at)
        first = at // LANES * 2 * cols
        both = pay_refs[0][first : first + 2 * cols, :].astype(jnp.float32)
        for ref in pay_refs[1:]:
            both = both + ref[first : first + 2 * cols, :].astype(jnp.float32)
        proj = both[:cols] + both[cols:]
        scale = scale_ref[:, at : at + count]
        weights = scale * scale / ncells
        if count < LANES:
            weights = jnp.concatenate([weights, jnp.zeros((1, LANES - count), jnp.float32)], axis=1)
        c = proj * weights
        turned = [c if n == 0 else pltpu.roll(c, LANES - n * span, 1) for n in range(rows)]
        stacked = jnp.concatenate(turned, axis=0).astype(jnp.bfloat16)
        wide = jnp.dot(stacked, spread, preferred_element_type=jnp.float32)
        for n in range(rows):
            start = (at + n * span) * rows
            if start >= ranks * rows:
                break
            piece = wide[n * cols : (n + 1) * cols, :]
            piece = jnp.broadcast_to(piece[:, None, :], (cols, rows, LANES)).reshape(lines, LANES)
            coef_ref[:, start : start + LANES] = (piece * same).astype(jnp.bfloat16)
    product(coef_ref[...], masks, True, factor_ref, out_ref)


def term_kernel(wanted, after, coef_ref, factor_ref, *refs):
    for (masks, other, _), out_ref in zip(wanted, refs[after:]):
        product(coef_ref[...], masks, other, factor_ref, out_ref)


def pair_kernel(mine_ref, got_ref, *out_refs):
    for n, ref in enumerate(out_refs):
        ref[...] = (mine_ref[n] + got_ref[n].astype(jnp.float32)).astype(ref.dtype)


def local_kernel(rows, cols, halve, b_ref, x_ref, amp_ref, along_ref, *refs):
    pay_refs, base_ref = refs[:-1], refs[-1]
    lines = cols * rows
    head = pay_refs[0].shape[0] - lines
    me = lax.axis_index("grp")
    low = jnp.zeros((lines, LANES), jnp.float32)
    high = low
    for n, ref in enumerate(pay_refs, 1):
        mask = (1 << n) - 1
        part = ref[head:, :].astype(jnp.float32)
        low = jnp.where((me ^ mask) == me - 1, part, low)
        high = jnp.where((me ^ mask) == me + 1, part, high)
    low = low.reshape(cols, rows, LANES)
    high = high.reshape(cols, rows, LANES)
    own = along_ref[...].reshape(cols, rows, LANES)
    conv = stencil(low, own, high, ROW_TAPS, 1)
    x = 0.5 * x_ref[...] if halve else x_ref[...]
    scaled = (amp_ref[...][None] * conv).reshape(lines, LANES)
    base_ref[...] = b_ref[...] - (x + scaled)


def update_kernel(near, halve, x_ref, base_ref, *refs):
    term_refs, out_refs = refs[:near], refs[near:]
    rank_sum = term_refs[0][...]
    for ref in term_refs[1:]:
        rank_sum = rank_sum + ref[...].astype(jnp.float32)
    x = 0.5 * x_ref[...] if halve else x_ref[...]
    residual = base_ref[...] - rank_sum
    new = x + 0.5 * residual
    out_refs[0][...] = new
    if len(out_refs) > 1:
        out_refs[1][...] = residual if out_refs[1].dtype == jnp.float32 else new.astype(jnp.bfloat16)


def on_device(right_side, amplitude, factor, scale):
    cols, rows, width = right_side.shape
    ranks = factor.shape[0]
    tiles = lax.axis_size("tile")
    groups = lax.axis_size("grp")
    near = tiles // 2
    lines = cols * rows
    ncells_all = rows * width * groups * tiles
    blocks = -(-ranks // LANES)
    flat = factor.reshape(ranks * rows, tiles * width)
    b = right_side.reshape(lines, width)
    scale = scale.reshape(1, ranks)
    x = b
    short = (0.5 * b).astype(jnp.bfloat16)
    pay_rows = blocks * 2 * cols + lines

    f32, bf16 = jnp.float32, jnp.bfloat16

    def shape(dtype, *dims):
        return jax.ShapeDtypeStruct(dims, dtype)

    def call(kernel, out_shape, flops=0, moved=1 << 18, **options):
        return pl.pallas_call(
            kernel,
            out_shape=out_shape,
            compiler_params=pltpu.CompilerParams(vmem_limit_bytes=32 * 1024 * 1024),
            cost_estimate=pl.CostEstimate(flops=flops, bytes_accessed=moved, transcendentals=0),
            **options,
        )

    work = lines * ranks * rows * tiles * width
    held = call(
        load_kernel,
        shape(bf16, *flat.shape),
        moved=4 * flat.size,
        in_specs=[pl.BlockSpec(memory_space=pltpu.HBM)],
        out_specs=pl.BlockSpec(memory_space=pltpu.VMEM),
        scratch_shapes=[pltpu.SemaphoreType.DMA((8,))],
        name="load",
    )(flat)
    for step in range(ITERS):
        halve = step == 0
        order = list(range(1, near))
        if step == 0:
            order.sort(key=lambda mask: (mask == near // 2, mask))
        parts = {mask: swap(short, "tile", 2 * mask) for mask in order}
        whole = [pl.BlockSpec(memory_space=pl.ANY)] + [pl.BlockSpec(memory_space=pltpu.VMEM)] * near
        own = call(
            partial(gather_kernel, [0] + order), shape(bf16, near, lines, width), in_specs=whole, name="order"
        )(held, short, *[parts[mask] for mask in order])
        across = swap(own, "tile", 1)
        diag = call(
            partial(first_kernel, rows),
            shape(f32, blocks * LANES, lines),
            flops=work,
            moved=flat.size,
            name="project_own",
        )(own, held)
        pay, part, along = call(
            partial(second_kernel, rows, cols, halve),
            (
                shape(bf16, pay_rows, width),
                shape(bf16, pay_rows - lines, width),
                shape(f32, lines, width),
            ),
            flops=work,
            moved=flat.size,
            scratch_shapes=[pltpu.VMEM((blocks * LANES, lines), f32)],
            name="project_across",
        )(x, across, held, diag)
        pays = [swap(part if mask & (mask + 1) else pay, "grp", mask) for mask in range(1, groups)]
        half = near // 2
        close, away = list(range(half)), list(range(near - 1, half - 1, -1))
        coef, far = call(
            partial(far_kernel, rows, cols, groups, ncells_all, away),
            (shape(bf16, lines, ranks * rows), shape(bf16, half, lines, width)),
            flops=work // 2,
            moved=flat.size,
            name="term_first",
        )(scale, held, part, *pays)
        got = swap(far, "tile", 1)

        def term(*wanted, after=()):
            return call(
                partial(term_kernel, wanted, len(after)),
                in_specs=[pl.BlockSpec(memory_space=pltpu.VMEM)] * 2
                + [pl.BlockSpec(memory_space=pl.ANY)] * len(after),
                out_shape=[shape(dtype, len(masks), lines, width) for masks, _, dtype in wanted],
                flops=work // 2 * len(wanted),
                moved=flat.size,
                name="term",
            )(coef, held, *after)

        def pair(mine, got, masks):
            return call(
                pair_kernel,
                [shape(bf16 if mask else f32, lines, width) for mask in masks],
                name="pair",
            )(mine, got)

        mine, far = term((away, False, f32), (close, True, bf16))
        sends = pair(mine, got, away)
        terms = [swap(send, "tile", 2 * mask) for send, mask in zip(sends, away)]
        got = swap(far, "tile", 1)
        (mine,) = term((close, False, f32), after=sends)
        kept, *sends = pair(mine, got, close)
        terms += [swap(send, "tile", 2 * mask) for send, mask in zip(sends, close[1:])]
        rims = [pay for mask, pay in enumerate(pays, 1) if not mask & (mask + 1)]
        base = call(
            partial(local_kernel, rows, cols, halve), shape(f32, lines, width), name="local"
        )(b, x, amplitude, along, *rims)
        last = step == ITERS - 1
        x, residual = call(
            partial(update_kernel, near, halve),
            (shape(f32, lines, width), shape(f32 if last else bf16, lines, width)),
            name="update",
        )(x, base, kept, *terms)
        short = residual
    return x.reshape(cols, rows, width), residual.reshape(cols, rows, width)


def solution(mesh):
    in_specs = (P(None, "grp", "tile"), P("grp", "tile"), P("tile", "grp", None), P("tile"))
    out_specs = (P(None, "grp", "tile"), P(None, "grp", "tile"))
    return jax.shard_map(
        on_device, mesh=mesh, in_specs=in_specs, out_specs=out_specs, check_vma=False
    )
```

```python
import math
from functools import partial

import jax
import jax.numpy as jnp
import numpy as np
from jax import lax
from jax.experimental import pallas as pl
from jax.experimental.pallas import tpu as pltpu
from jax.sharding import PartitionSpec as P

REACH = 8
ITERS = 2
LANES = 128


def taper(sigma):
    offsets = np.arange(-REACH, REACH + 1).astype(np.float64)
    values = np.exp(-offsets * offsets / (2.0 * sigma * sigma))
    values = values * np.cos(np.pi * offsets / (2.0 * REACH + 2.0)) ** 2
    return [float(v) for v in (values / values.sum()).astype(np.float32)]


ROW_TAPS = taper(3.0)
COL_TAPS = taper(5.0)


def stencil(low, own, high, taps, axis):
    size = own.shape[axis]
    place = lax.broadcasted_iota(jnp.int32, own.shape, axis)
    total = taps[REACH] * own
    for shift in range(1, REACH + 1):
        after = pltpu.roll(jnp.where(place < shift, high, own), size - shift, axis)
        before = pltpu.roll(jnp.where(place >= size - shift, low, own), shift, axis)
        total = total + taps[REACH + shift] * after + taps[REACH - shift] * before
    return total


def swap(value, axis, mask):
    return lax.ppermute(value, axis, [(i, i ^ mask) for i in range(lax.axis_size(axis))])


def place_of(spot):
    mask, other = spot
    me = lax.axis_index("tile")
    core = lax.rem(me, 2)
    return 2 * (lax.div(me, 2) ^ mask) + (1 - core if other else core)


def columns_of(spots):
    return [pl.multiple_of(place_of(spot) * LANES, LANES) for spot in spots]


def join_kernel(*refs):
    part_refs, out_ref = refs[1:-1], refs[-1]
    at = 0
    for ref in part_refs:
        out_ref[at : at + ref.shape[0]] = ref[...]
        at += ref.shape[0]


def load_kernel(source_ref, out_ref, sems):
    chunks = sems.shape[0]
    count = source_ref.shape[0] // chunks
    copies = [
        pltpu.make_async_copy(
            source_ref.at[pl.ds(n * count, count)], out_ref.at[pl.ds(n * count, count)], sems.at[n]
        )
        for n in range(chunks)
    ]
    for copy in copies:
        copy.start()
    for copy in copies:
        copy.wait()


def diagonal(rows, spots, fields, factor_ref, store):
    lines = fields[0].shape[0]
    count = factor_ref.shape[0]
    field = jnp.concatenate(fields, axis=1)
    step = min(1024, count)
    row_of = lax.broadcasted_iota(jnp.int32, (rows, lines), 0)
    lane_of = lax.broadcasted_iota(jnp.int32, (rows, lines), 1)
    same = (lax.rem(lane_of, rows) == row_of).astype(jnp.float32)
    starts = columns_of(spots)
    for at in range(0, count, step):
        left = jnp.concatenate(
            [factor_ref[at : at + step, pl.ds(start, LANES)] for start in starts], axis=1
        )
        part = lax.dot_general(
            left, field, (((1,), (1,)), ((), ())), preferred_element_type=jnp.float32
        )
        part = part.reshape(step // rows, rows, lines) * same[None]
        store(at // rows, (at + step) // rows, jnp.sum(part, axis=1))


def blocks_of(refs):
    return [ref[n] for ref in refs for n in range(ref.shape[0])]


def first_kernel(rows, spots, added, factor_ref, *refs):
    diag_ref = refs[-1]
    field_refs = refs[: len(refs) - 1 - added]
    ranks = factor_ref.shape[0] // rows
    if diag_ref.shape[0] > ranks:
        diag_ref[...] = jnp.zeros_like(diag_ref)

    def store(start, end, value):
        diag_ref[start:end, :] = refs[-2][start:end, :] + value if added else value

    diagonal(rows, spots, blocks_of(field_refs), factor_ref, store)


def second_kernel(rows, cols, halve, spots, known, x_ref, factor_ref, diag_ref, fields_ref, *refs):
    other_refs, (pay_ref, part_ref, along_ref, total) = refs[:-4], refs[-4:]
    lines = cols * rows
    if total.shape[0] > factor_ref.shape[0] // rows:
        total[...] = jnp.zeros_like(total)

    def store(start, end, value):
        total[start:end, :] = diag_ref[start:end, :] + value

    diagonal(rows, spots, blocks_of([fields_ref]), factor_ref, store)
    pick = (
        lax.broadcasted_iota(jnp.int32, (cols, lines), 1) // rows
        == lax.broadcasted_iota(jnp.int32, (cols, lines), 0)
    ).astype(jnp.bfloat16)
    for at in range(0, total.shape[0], LANES):
        part = total[at : at + LANES, :]
        upper = part.astype(jnp.bfloat16)
        lower = (part - upper.astype(jnp.float32)).astype(jnp.bfloat16)
        dims = (((1,), (1,)), ((), ()))
        proj = lax.dot_general(pick, upper, dims, preferred_element_type=jnp.float32)
        proj = proj + lax.dot_general(pick, lower, dims, preferred_element_type=jnp.float32)
        first = at // LANES * 2 * cols
        upper = proj.astype(jnp.bfloat16)
        lower = (proj - upper.astype(jnp.float32)).astype(jnp.bfloat16)
        for ref in (pay_ref, part_ref):
            ref[first : first + cols, :] = upper
            ref[first + cols : first + 2 * cols, :] = lower

    head = total.shape[0] // LANES * 2 * cols
    me = lax.axis_index("tile")
    low = jnp.zeros((lines, LANES), jnp.float32)
    high = low
    for spot, block in zip(spots + known, blocks_of((fields_ref,) + other_refs)):
        part, place = block.astype(jnp.float32), place_of(spot)
        low = jnp.where(place == me - 1, part, low)
        high = jnp.where(place == me + 1, part, high)
    own = 0.5 * x_ref[...] if halve else x_ref[...]
    along = stencil(low, own, high, COL_TAPS, 1)
    along_ref[...] = along
    pay_ref[head:, :] = along.astype(jnp.bfloat16)


def product(coef, spots, factor_ref, out_ref):
    starts = columns_of(spots)
    for n in range(0, len(starts), 2):
        pair = starts[n : n + 2]
        right = jnp.concatenate([factor_ref[:, pl.ds(start, LANES)] for start in pair], axis=1)
        term = jnp.dot(coef, right, preferred_element_type=jnp.float32)
        for m in range(len(pair)):
            out_ref[n + m] = term[:, m * LANES : (m + 1) * LANES].astype(out_ref.dtype)


def far_kernel(rows, cols, groups, ncells, spots, scale_ref, factor_ref, *refs):
    pay_refs, (coef_ref, out_ref) = refs[:groups], refs[groups:]
    ranks = factor_ref.shape[0] // rows
    lines = cols * rows
    span = LANES // rows

    spread = (
        lax.broadcasted_iota(jnp.int32, (LANES, LANES), 1) // rows
        == lax.broadcasted_iota(jnp.int32, (LANES, LANES), 0)
    ).astype(jnp.bfloat16)
    same = (
        lax.rem(lax.broadcasted_iota(jnp.int32, (lines, LANES), 1), rows)
        == lax.rem(lax.broadcasted_iota(jnp.int32, (lines, LANES), 0), rows)
    ).astype(jnp.float32)
    for at in range(0, ranks, LANES):
        count = min(LANES, ranks - at)
        first = at // LANES * 2 * cols
        both = pay_refs[0][first : first + 2 * cols, :].astype(jnp.float32)
        for ref in pay_refs[1:]:
            both = both + ref[first : first + 2 * cols, :].astype(jnp.float32)
        proj = both[:cols] + both[cols:]
        scale = scale_ref[:, at : at + count]
        weights = scale * scale / ncells
        if count < LANES:
            weights = jnp.concatenate([weights, jnp.zeros((1, LANES - count), jnp.float32)], axis=1)
        c = proj * weights
        turned = [c if n == 0 else pltpu.roll(c, LANES - n * span, 1) for n in range(rows)]
        stacked = jnp.concatenate(turned, axis=0).astype(jnp.bfloat16)
        wide = jnp.dot(stacked, spread, preferred_element_type=jnp.float32)
        for n in range(rows):
            start = (at + n * span) * rows
            if start >= ranks * rows:
                break
            piece = wide[n * cols : (n + 1) * cols, :]
            piece = jnp.broadcast_to(piece[:, None, :], (cols, rows, LANES)).reshape(lines, LANES)
            coef_ref[:, start : start + LANES] = (piece * same).astype(jnp.bfloat16)
    product(coef_ref[...], spots, factor_ref, out_ref)


def term_kernel(wanted, after, coef_ref, factor_ref, *refs):
    for (spots, _), out_ref in zip(wanted, refs[after:]):
        product(coef_ref[...], spots, factor_ref, out_ref)


def pair_kernel(mine_ref, got_ref, *out_refs):
    at = 0
    for ref in out_refs:
        end = at + ref.shape[0]
        ref[...] = (mine_ref[at:end] + got_ref[at:end].astype(jnp.float32)).astype(ref.dtype)
        at = end


def local_kernel(rows, cols, halve, b_ref, x_ref, amp_ref, along_ref, *refs):
    pay_refs, base_ref = refs[:-1], refs[-1]
    lines = cols * rows
    head = pay_refs[0].shape[0] - lines
    me = lax.axis_index("grp")
    low = jnp.zeros((lines, LANES), jnp.float32)
    high = low
    for n, ref in enumerate(pay_refs, 1):
        mask = (1 << n) - 1
        part = ref[head:, :].astype(jnp.float32)
        low = jnp.where((me ^ mask) == me - 1, part, low)
        high = jnp.where((me ^ mask) == me + 1, part, high)
    low = low.reshape(cols, rows, LANES)
    high = high.reshape(cols, rows, LANES)
    own = along_ref[...].reshape(cols, rows, LANES)
    conv = stencil(low, own, high, ROW_TAPS, 1)
    x = 0.5 * x_ref[...] if halve else x_ref[...]
    scaled = (amp_ref[...][None] * conv).reshape(lines, LANES)
    base_ref[...] = b_ref[...] - (x + scaled)


def update_kernel(halve, last, x_ref, base_ref, *refs):
    part_refs, (new_ref, other_ref) = refs[:-2], refs[-2:]
    rank_sum = part_refs[0][0]
    for ref in part_refs[1:]:
        rank_sum = rank_sum + ref[0].astype(jnp.float32)
    x = 0.5 * x_ref[...] if halve else x_ref[...]
    residual = base_ref[...] - rank_sum
    new = x + 0.5 * residual
    new_ref[...] = new
    if last:
        other_ref[...] = residual
    else:
        other_ref[0] = new.astype(jnp.bfloat16)


def on_device(right_side, amplitude, factor, scale):
    cols, rows, width = right_side.shape
    ranks = factor.shape[0]
    tiles = lax.axis_size("tile")
    groups = lax.axis_size("grp")
    near = tiles // 2
    lines = cols * rows
    ncells_all = rows * width * groups * tiles
    blocks = -(-ranks // LANES)
    flat = factor.reshape(ranks * rows, tiles * width)
    b = right_side.reshape(lines, width)
    scale = scale.reshape(1, ranks)
    x = b
    short = (0.5 * b).astype(jnp.bfloat16)[None]
    pay_rows = blocks * 2 * cols + lines

    f32, bf16 = jnp.float32, jnp.bfloat16

    def shape(dtype, *dims):
        return jax.ShapeDtypeStruct(dims, dtype)

    def call(kernel, out_shape, flops=0, moved=1 << 18, **options):
        return pl.pallas_call(
            kernel,
            out_shape=out_shape,
            compiler_params=pltpu.CompilerParams(vmem_limit_bytes=32 * 1024 * 1024),
            cost_estimate=pl.CostEstimate(flops=flops, bytes_accessed=moved, transcendentals=0),
            **options,
        )

    work = lines * ranks * rows * tiles * width
    held = call(
        load_kernel,
        shape(bf16, *flat.shape),
        moved=4 * flat.size,
        in_specs=[pl.BlockSpec(memory_space=pltpu.HBM)],
        out_specs=pl.BlockSpec(memory_space=pltpu.VMEM),
        scratch_shapes=[pltpu.SemaphoreType.DMA((8,))],
        name="load",
    )(flat)
    half = near // 2
    close, away = list(range(half)), list(range(near - 1, half - 1, -1))

    def spots_of(masks, other):
        return [(mask, other != (mask > 0)) for mask in masks]

    def cross(value, mask):
        return swap(value, "tile", 2 * mask + 1)

    def first(fields, spots, *before):
        return call(
            partial(first_kernel, rows, spots, len(before)),
            shape(f32, blocks * LANES, lines),
            flops=work,
            moved=flat.size,
            name="project_own",
        )(held, *fields, *before)

    for step in range(ITERS):
        halve = step == 0
        order = list(range(1, near))
        if step == 0:
            order.sort(key=lambda mask: (mask == near // 2, mask))
        parts = [cross(short, mask) for mask in order]
        bundle = call(
            join_kernel,
            shape(bf16, near, lines, width),
            in_specs=[pl.BlockSpec(memory_space=pl.ANY)]
            + [pl.BlockSpec(memory_space=pltpu.VMEM)] * near,
            name="join",
        )(held, short, *parts)
        across = swap(bundle, "tile", 1)
        known = spots_of([0] + order, False)
        diag = first([bundle], known)
        spots = spots_of([0] + order, True)
        pay, part, along = call(
            partial(second_kernel, rows, cols, halve, spots, known),
            (
                shape(bf16, pay_rows, width),
                shape(bf16, pay_rows - lines, width),
                shape(f32, lines, width),
            ),
            flops=work,
            moved=flat.size,
            scratch_shapes=[pltpu.VMEM((blocks * LANES, lines), f32)],
            name="project_across",
        )(x, held, diag, across, bundle)
        pays = [swap(part if mask & (mask + 1) else pay, "grp", mask) for mask in range(1, groups)]
        coef, far = call(
            partial(far_kernel, rows, cols, groups, ncells_all, spots_of(away, True)),
            (shape(bf16, lines, ranks * rows), shape(bf16, half, lines, width)),
            flops=work // 2,
            moved=flat.size,
            name="term_first",
        )(scale, held, part, *pays)
        got = swap(far, "tile", 1)

        def term(*wanted, after=()):
            return call(
                partial(term_kernel, wanted, len(after)),
                in_specs=[pl.BlockSpec(memory_space=pltpu.VMEM)] * 2
                + [pl.BlockSpec(memory_space=pl.ANY)] * len(after),
                out_shape=[shape(dtype, len(spots), lines, width) for spots, dtype in wanted],
                flops=work // 2 * len(wanted),
                moved=flat.size,
                name="term",
            )(coef, held, *after)

        def pair(mine, got, masks):
            return call(
                pair_kernel,
                [shape(bf16 if mask else f32, 1, lines, width) for mask in masks],
                name="pair",
            )(mine, got)

        mine, far = term((spots_of(away, False), f32), (spots_of(close, True), bf16))
        sends = pair(mine, got, away)
        terms = [cross(send, mask) for send, mask in zip(sends, away)]
        got = swap(far, "tile", 1)
        (mine,) = term((spots_of(close, False), f32), after=sends)
        kept, *sends = pair(mine, got, close)
        terms += [cross(send, mask) for send, mask in zip(sends, close[1:])]
        rims = [pay for mask, pay in enumerate(pays, 1) if not mask & (mask + 1)]
        base = call(
            partial(local_kernel, rows, cols, halve), shape(f32, lines, width), name="local"
        )(b, x, amplitude, along, *rims)
        last = step == ITERS - 1
        x, short = call(
            partial(update_kernel, halve, last),
            (
                shape(f32, lines, width),
                shape(f32, lines, width) if last else shape(bf16, 1, lines, width),
            ),
            name="update",
        )(x, base, kept, *terms)
    return x.reshape(cols, rows, width), short.reshape(cols, rows, width)


def solution(mesh):
    in_specs = (P(None, "grp", "tile"), P("grp", "tile"), P("tile", "grp", None), P("tile"))
    out_specs = (P(None, "grp", "tile"), P(None, "grp", "tile"))
    return jax.shard_map(
        on_device, mesh=mesh, in_specs=in_specs, out_specs=out_specs, check_vma=False
    )
```

```python
import math
from functools import partial

import jax
import jax.numpy as jnp
import numpy as np
from jax import lax
from jax.experimental import pallas as pl
from jax.experimental.pallas import tpu as pltpu
from jax.sharding import PartitionSpec as P

REACH = 8
ITERS = 2
LANES = 128


def taper(sigma):
    offsets = np.arange(-REACH, REACH + 1).astype(np.float64)
    values = np.exp(-offsets * offsets / (2.0 * sigma * sigma))
    values = values * np.cos(np.pi * offsets / (2.0 * REACH + 2.0)) ** 2
    return [float(v) for v in (values / values.sum()).astype(np.float32)]


ROW_TAPS = taper(3.0)
COL_TAPS = taper(5.0)


def stencil(low, own, high, taps, axis):
    size = own.shape[axis]
    place = lax.broadcasted_iota(jnp.int32, own.shape, axis)
    total = taps[REACH] * own
    for shift in range(1, REACH + 1):
        after = pltpu.roll(jnp.where(place < shift, high, own), size - shift, axis)
        before = pltpu.roll(jnp.where(place >= size - shift, low, own), shift, axis)
        total = total + taps[REACH + shift] * after + taps[REACH - shift] * before
    return total


def swap(value, axis, mask):
    return lax.ppermute(value, axis, [(i, i ^ mask) for i in range(lax.axis_size(axis))])


def place_of(spot):
    mask, other = spot
    me = lax.axis_index("tile")
    core = lax.rem(me, 2)
    return 2 * (lax.div(me, 2) ^ mask) + (1 - core if other else core)


def columns_of(spots):
    return [pl.multiple_of(place_of(spot) * LANES, LANES) for spot in spots]


def join_kernel(*refs):
    part_refs, out_ref = refs[1:-1], refs[-1]
    at = 0
    for ref in part_refs:
        out_ref[at : at + ref.shape[0]] = ref[...]
        at += ref.shape[0]


def load_kernel(source_ref, out_ref, sems):
    chunks = sems.shape[0]
    count = source_ref.shape[0] // chunks
    copies = [
        pltpu.make_async_copy(
            source_ref.at[pl.ds(n * count, count)], out_ref.at[pl.ds(n * count, count)], sems.at[n]
        )
        for n in range(chunks)
    ]
    for copy in copies:
        copy.start()
    for copy in copies:
        copy.wait()


def diagonal(rows, spots, fields, factor_ref, store):
    lines = fields[0].shape[0]
    count = factor_ref.shape[0]
    field = jnp.concatenate(fields, axis=1)
    step = min(1024, count)
    row_of = lax.broadcasted_iota(jnp.int32, (rows, lines), 0)
    lane_of = lax.broadcasted_iota(jnp.int32, (rows, lines), 1)
    same = (lax.rem(lane_of, rows) == row_of).astype(jnp.float32)
    starts = columns_of(spots)
    for at in range(0, count, step):
        left = jnp.concatenate(
            [factor_ref[at : at + step, pl.ds(start, LANES)] for start in starts], axis=1
        )
        part = lax.dot_general(
            left, field, (((1,), (1,)), ((), ())), preferred_element_type=jnp.float32
        )
        part = part.reshape(step // rows, rows, lines) * same[None]
        store(at // rows, (at + step) // rows, jnp.sum(part, axis=1))


def blocks_of(refs):
    return [ref[n] for ref in refs for n in range(ref.shape[0])]


def first_kernel(rows, spots, added, factor_ref, *refs):
    diag_ref = refs[-1]
    field_refs = refs[: len(refs) - 1 - added]
    ranks = factor_ref.shape[0] // rows
    if diag_ref.shape[0] > ranks:
        diag_ref[...] = jnp.zeros_like(diag_ref)

    def store(start, end, value):
        diag_ref[start:end, :] = refs[-2][start:end, :] + value if added else value

    diagonal(rows, spots, blocks_of(field_refs), factor_ref, store)


def second_kernel(rows, cols, halve, spots, known, x_ref, factor_ref, diag_ref, fields_ref, *refs):
    other_refs, (pay_ref, part_ref, along_ref, total) = refs[:-4], refs[-4:]
    lines = cols * rows
    if total.shape[0] > factor_ref.shape[0] // rows:
        total[...] = jnp.zeros_like(total)

    def store(start, end, value):
        total[start:end, :] = diag_ref[start:end, :] + value

    diagonal(rows, spots, blocks_of([fields_ref]), factor_ref, store)
    pick = (
        lax.broadcasted_iota(jnp.int32, (cols, lines), 1) // rows
        == lax.broadcasted_iota(jnp.int32, (cols, lines), 0)
    ).astype(jnp.bfloat16)
    for at in range(0, total.shape[0], LANES):
        part = total[at : at + LANES, :]
        upper = part.astype(jnp.bfloat16)
        lower = (part - upper.astype(jnp.float32)).astype(jnp.bfloat16)
        dims = (((1,), (1,)), ((), ()))
        proj = lax.dot_general(pick, upper, dims, preferred_element_type=jnp.float32)
        proj = proj + lax.dot_general(pick, lower, dims, preferred_element_type=jnp.float32)
        first = at // LANES * 2 * cols
        upper = proj.astype(jnp.bfloat16)
        lower = (proj - upper.astype(jnp.float32)).astype(jnp.bfloat16)
        for ref in (pay_ref, part_ref):
            ref[first : first + cols, :] = upper
            ref[first + cols : first + 2 * cols, :] = lower

    head = total.shape[0] // LANES * 2 * cols
    me = lax.axis_index("tile")
    low = jnp.zeros((lines, LANES), jnp.float32)
    high = low
    for spot, block in zip(spots + known, blocks_of((fields_ref,) + other_refs)):
        part, place = block.astype(jnp.float32), place_of(spot)
        low = jnp.where(place == me - 1, part, low)
        high = jnp.where(place == me + 1, part, high)
    own = 0.5 * x_ref[...] if halve else x_ref[...]
    along = stencil(low, own, high, COL_TAPS, 1)
    along_ref[...] = along
    pay_ref[head:, :] = along.astype(jnp.bfloat16)


def product(coef, spots, factor_ref, out_ref):
    starts = columns_of(spots)
    for n in range(0, len(starts), 2):
        pair = starts[n : n + 2]
        right = jnp.concatenate([factor_ref[:, pl.ds(start, LANES)] for start in pair], axis=1)
        term = jnp.dot(coef, right, preferred_element_type=jnp.float32)
        for m in range(len(pair)):
            out_ref[n + m] = term[:, m * LANES : (m + 1) * LANES].astype(out_ref.dtype)


def far_kernel(rows, cols, groups, ncells, spots, scale_ref, factor_ref, *refs):
    pay_refs, (coef_ref, out_ref) = refs[:groups], refs[groups:]
    ranks = factor_ref.shape[0] // rows
    lines = cols * rows
    span = LANES // rows

    spread = (
        lax.broadcasted_iota(jnp.int32, (LANES, LANES), 1) // rows
        == lax.broadcasted_iota(jnp.int32, (LANES, LANES), 0)
    ).astype(jnp.bfloat16)
    same = (
        lax.rem(lax.broadcasted_iota(jnp.int32, (lines, LANES), 1), rows)
        == lax.rem(lax.broadcasted_iota(jnp.int32, (lines, LANES), 0), rows)
    ).astype(jnp.float32)
    for at in range(0, ranks, LANES):
        count = min(LANES, ranks - at)
        first = at // LANES * 2 * cols
        both = pay_refs[0][first : first + 2 * cols, :].astype(jnp.float32)
        for ref in pay_refs[1:]:
            both = both + ref[first : first + 2 * cols, :].astype(jnp.float32)
        proj = both[:cols] + both[cols:]
        scale = scale_ref[:, at : at + count]
        weights = scale * scale / ncells
        if count < LANES:
            weights = jnp.concatenate([weights, jnp.zeros((1, LANES - count), jnp.float32)], axis=1)
        c = proj * weights
        turned = [c if n == 0 else pltpu.roll(c, LANES - n * span, 1) for n in range(rows)]
        stacked = jnp.concatenate(turned, axis=0).astype(jnp.bfloat16)
        wide = jnp.dot(stacked, spread, preferred_element_type=jnp.float32)
        for n in range(rows):
            start = (at + n * span) * rows
            if start >= ranks * rows:
                break
            piece = wide[n * cols : (n + 1) * cols, :]
            piece = jnp.broadcast_to(piece[:, None, :], (cols, rows, LANES)).reshape(lines, LANES)
            coef_ref[:, start : start + LANES] = (piece * same).astype(jnp.bfloat16)
    product(coef_ref[...], spots, factor_ref, out_ref)


def term_kernel(wanted, after, coef_ref, factor_ref, *refs):
    for (spots, _), out_ref in zip(wanted, refs[after:]):
        product(coef_ref[...], spots, factor_ref, out_ref)


def pair_kernel(mine_ref, got_ref, *out_refs):
    at = 0
    for ref in out_refs:
        end = at + ref.shape[0]
        ref[...] = (mine_ref[at:end] + got_ref[at:end].astype(jnp.float32)).astype(ref.dtype)
        at = end


def local_kernel(rows, cols, halve, b_ref, x_ref, amp_ref, along_ref, *refs):
    pay_refs, base_ref = refs[:-1], refs[-1]
    lines = cols * rows
    head = pay_refs[0].shape[0] - lines
    me = lax.axis_index("grp")
    low = jnp.zeros((lines, LANES), jnp.float32)
    high = low
    for n, ref in enumerate(pay_refs, 1):
        mask = (1 << n) - 1
        part = ref[head:, :].astype(jnp.float32)
        low = jnp.where((me ^ mask) == me - 1, part, low)
        high = jnp.where((me ^ mask) == me + 1, part, high)
    low = low.reshape(cols, rows, LANES)
    high = high.reshape(cols, rows, LANES)
    own = along_ref[...].reshape(cols, rows, LANES)
    conv = stencil(low, own, high, ROW_TAPS, 1)
    x = 0.5 * x_ref[...] if halve else x_ref[...]
    scaled = (amp_ref[...][None] * conv).reshape(lines, LANES)
    base_ref[...] = b_ref[...] - (x + scaled)


def update_kernel(halve, last, x_ref, base_ref, *refs):
    part_refs, (new_ref, other_ref) = refs[:-2], refs[-2:]
    rank_sum = part_refs[0][0]
    for ref in part_refs[1:]:
        rank_sum = rank_sum + ref[0].astype(jnp.float32)
    x = 0.5 * x_ref[...] if halve else x_ref[...]
    residual = base_ref[...] - rank_sum
    new = x + 0.5 * residual
    new_ref[...] = new
    if last:
        other_ref[...] = residual
    else:
        other_ref[0] = new.astype(jnp.bfloat16)


def on_device(right_side, amplitude, factor, scale):
    cols, rows, width = right_side.shape
    ranks = factor.shape[0]
    tiles = lax.axis_size("tile")
    groups = lax.axis_size("grp")
    near = tiles // 2
    lines = cols * rows
    ncells_all = rows * width * groups * tiles
    blocks = -(-ranks // LANES)
    flat = factor.reshape(ranks * rows, tiles * width)
    b = right_side.reshape(lines, width)
    scale = scale.reshape(1, ranks)
    x = b
    short = (0.5 * b).astype(jnp.bfloat16)[None]
    pay_rows = blocks * 2 * cols + lines

    f32, bf16 = jnp.float32, jnp.bfloat16

    def shape(dtype, *dims):
        return jax.ShapeDtypeStruct(dims, dtype)

    def call(kernel, out_shape, flops=0, moved=1 << 18, **options):
        return pl.pallas_call(
            kernel,
            out_shape=out_shape,
            compiler_params=pltpu.CompilerParams(vmem_limit_bytes=32 * 1024 * 1024),
            cost_estimate=pl.CostEstimate(flops=flops, bytes_accessed=moved, transcendentals=0),
            **options,
        )

    work = lines * ranks * rows * tiles * width
    held = call(
        load_kernel,
        shape(bf16, *flat.shape),
        moved=4 * flat.size,
        in_specs=[pl.BlockSpec(memory_space=pltpu.HBM)],
        out_specs=pl.BlockSpec(memory_space=pltpu.VMEM),
        scratch_shapes=[pltpu.SemaphoreType.DMA((8,))],
        name="load",
    )(flat)
    half = near // 2
    close, away = list(range(half)), list(range(half, near))

    def spots_of(masks, other):
        return [(mask, other != (mask > 0)) for mask in masks]

    def cross(value, mask):
        return swap(value, "tile", 2 * mask + 1)

    def first(fields, spots, *before):
        return call(
            partial(first_kernel, rows, spots, len(before)),
            shape(f32, blocks * LANES, lines),
            flops=work,
            moved=flat.size,
            name="project_own",
        )(held, *fields, *before)

    for step in range(ITERS):
        halve = step == 0
        order = list(range(1, near))
        order.sort(key=lambda mask: (mask == half, mask))
        parts = [cross(short, mask) for mask in order]
        bundle = call(
            join_kernel,
            shape(bf16, near, lines, width),
            in_specs=[pl.BlockSpec(memory_space=pl.ANY)]
            + [pl.BlockSpec(memory_space=pltpu.VMEM)] * near,
            name="join",
        )(held, short, *parts)
        across = swap(bundle, "tile", 1)
        known = spots_of([0] + order, False)
        diag = first([bundle], known)
        spots = spots_of([0] + order, True)
        pay, part, along = call(
            partial(second_kernel, rows, cols, halve, spots, known),
            (
                shape(bf16, pay_rows, width),
                shape(bf16, pay_rows - lines, width),
                shape(f32, lines, width),
            ),
            flops=work,
            moved=flat.size,
            scratch_shapes=[pltpu.VMEM((blocks * LANES, lines), f32)],
            name="project_across",
        )(x, held, diag, across, bundle)
        pays = [swap(part if mask & (mask + 1) else pay, "grp", mask) for mask in range(1, groups)]
        coef, far = call(
            partial(far_kernel, rows, cols, groups, ncells_all, spots_of(away, True)),
            (shape(bf16, lines, ranks * rows), shape(bf16, half, lines, width)),
            flops=work // 2,
            moved=flat.size,
            name="term_first",
        )(scale, held, part, *pays)
        got = swap(far, "tile", 1)

        def term(*wanted, after=()):
            return call(
                partial(term_kernel, wanted, len(after)),
                in_specs=[pl.BlockSpec(memory_space=pltpu.VMEM)] * 2
                + [pl.BlockSpec(memory_space=pl.ANY)] * len(after),
                out_shape=[shape(dtype, len(spots), lines, width) for spots, dtype in wanted],
                flops=work // 2 * len(wanted),
                moved=flat.size,
                name="term",
            )(coef, held, *after)

        def pair(mine, got, masks):
            return call(
                pair_kernel,
                [shape(bf16 if mask else f32, 1, lines, width) for mask in masks],
                name="pair",
            )(mine, got)

        mine, far = term((spots_of(away, False), f32), (spots_of(close, True), bf16))
        sends = pair(mine, got, away)
        terms = [cross(send, mask) for send, mask in zip(sends, away)]
        got = swap(far, "tile", 1)
        (mine,) = term((spots_of(close, False), f32), after=sends)
        kept, *sends = pair(mine, got, close)
        terms += [cross(send, mask) for send, mask in zip(sends, close[1:])]
        rims = [pay for mask, pay in enumerate(pays, 1) if not mask & (mask + 1)]
        base = call(
            partial(local_kernel, rows, cols, halve), shape(f32, lines, width), name="local"
        )(b, x, amplitude, along, *rims)
        last = step == ITERS - 1
        x, short = call(
            partial(update_kernel, halve, last),
            (
                shape(f32, lines, width),
                shape(f32, lines, width) if last else shape(bf16, 1, lines, width),
            ),
            name="update",
        )(x, base, kept, *terms)
    return x.reshape(cols, rows, width), short.reshape(cols, rows, width)


def solution(mesh):
    in_specs = (P(None, "grp", "tile"), P("grp", "tile"), P("tile", "grp", None), P("tile"))
    out_specs = (P(None, "grp", "tile"), P(None, "grp", "tile"))
    return jax.shard_map(
        on_device, mesh=mesh, in_specs=in_specs, out_specs=out_specs, check_vma=False
    )
```

```python
import math
from functools import partial

import jax
import jax.numpy as jnp
import numpy as np
from jax import lax
from jax.experimental import pallas as pl
from jax.experimental.pallas import tpu as pltpu
from jax.sharding import PartitionSpec as P

REACH = 8
ITERS = 2
LANES = 128


def taper(sigma):
    offsets = np.arange(-REACH, REACH + 1).astype(np.float64)
    values = np.exp(-offsets * offsets / (2.0 * sigma * sigma))
    values = values * np.cos(np.pi * offsets / (2.0 * REACH + 2.0)) ** 2
    return [float(v) for v in (values / values.sum()).astype(np.float32)]


ROW_TAPS = taper(3.0)
COL_TAPS = taper(5.0)


def stencil(low, own, high, taps, axis):
    size = own.shape[axis]
    place = lax.broadcasted_iota(jnp.int32, own.shape, axis)
    total = taps[REACH] * own
    for shift in range(1, REACH + 1):
        after = pltpu.roll(jnp.where(place < shift, high, own), size - shift, axis)
        before = pltpu.roll(jnp.where(place >= size - shift, low, own), shift, axis)
        total = total + taps[REACH + shift] * after + taps[REACH - shift] * before
    return total


def swap(value, axis, mask):
    return lax.ppermute(value, axis, [(i, i ^ mask) for i in range(lax.axis_size(axis))])


def place_of(spot):
    mask, other = spot
    me = lax.axis_index("tile")
    core = lax.rem(me, 2)
    return 2 * (lax.div(me, 2) ^ mask) + (1 - core if other else core)


def columns_of(spots):
    return [pl.multiple_of(place_of(spot) * LANES, LANES) for spot in spots]


def join_kernel(*refs):
    part_refs, out_ref = refs[1:-1], refs[-1]
    at = 0
    for ref in part_refs:
        out_ref[at : at + ref.shape[0]] = ref[...]
        at += ref.shape[0]


def load_kernel(source_ref, out_ref, sems):
    chunks = sems.shape[0]
    count = source_ref.shape[0] // chunks
    copies = [
        pltpu.make_async_copy(
            source_ref.at[pl.ds(n * count, count)], out_ref.at[pl.ds(n * count, count)], sems.at[n]
        )
        for n in range(chunks)
    ]
    for copy in copies:
        copy.start()
    for copy in copies:
        copy.wait()


def diagonal(rows, spots, fields, factor_ref, store):
    lines = fields[0].shape[0]
    count = factor_ref.shape[0]
    field = jnp.concatenate(fields, axis=1)
    step = min(1024, count)
    row_of = lax.broadcasted_iota(jnp.int32, (rows, lines), 0)
    lane_of = lax.broadcasted_iota(jnp.int32, (rows, lines), 1)
    same = (lax.rem(lane_of, rows) == row_of).astype(jnp.float32)
    starts = columns_of(spots)
    for at in range(0, count, step):
        left = jnp.concatenate(
            [factor_ref[at : at + step, pl.ds(start, LANES)] for start in starts], axis=1
        )
        part = lax.dot_general(
            left, field, (((1,), (1,)), ((), ())), preferred_element_type=jnp.float32
        )
        part = part.reshape(step // rows, rows, lines) * same[None]
        store(at // rows, (at + step) // rows, jnp.sum(part, axis=1))


def blocks_of(refs):
    return [ref[n] for ref in refs for n in range(ref.shape[0])]


def first_kernel(rows, spots, added, factor_ref, *refs):
    diag_ref = refs[-1]
    field_refs = refs[: len(refs) - 1 - added]
    ranks = factor_ref.shape[0] // rows
    if diag_ref.shape[0] > ranks:
        diag_ref[...] = jnp.zeros_like(diag_ref)

    def store(start, end, value):
        diag_ref[start:end, :] = refs[-2][start:end, :] + value if added else value

    diagonal(rows, spots, blocks_of(field_refs), factor_ref, store)


def second_kernel(rows, cols, halve, spots, known, x_ref, factor_ref, diag_ref, fields_ref, *refs):
    other_refs, (pay_ref, part_ref, along_ref, total) = refs[:-4], refs[-4:]
    lines = cols * rows
    if total.shape[0] > factor_ref.shape[0] // rows:
        total[...] = jnp.zeros_like(total)

    def store(start, end, value):
        total[start:end, :] = diag_ref[start:end, :] + value

    diagonal(rows, spots, blocks_of([fields_ref]), factor_ref, store)
    pick = (
        lax.broadcasted_iota(jnp.int32, (cols, lines), 1) // rows
        == lax.broadcasted_iota(jnp.int32, (cols, lines), 0)
    ).astype(jnp.bfloat16)
    for at in range(0, total.shape[0], LANES):
        part = total[at : at + LANES, :]
        upper = part.astype(jnp.bfloat16)
        lower = (part - upper.astype(jnp.float32)).astype(jnp.bfloat16)
        dims = (((1,), (1,)), ((), ()))
        proj = lax.dot_general(pick, upper, dims, preferred_element_type=jnp.float32)
        proj = proj + lax.dot_general(pick, lower, dims, preferred_element_type=jnp.float32)
        first = at // LANES * 2 * cols
        upper = proj.astype(jnp.bfloat16)
        lower = (proj - upper.astype(jnp.float32)).astype(jnp.bfloat16)
        for ref in (pay_ref, part_ref):
            ref[first : first + cols, :] = upper
            ref[first + cols : first + 2 * cols, :] = lower

    head = total.shape[0] // LANES * 2 * cols
    me = lax.axis_index("tile")
    low = jnp.zeros((lines, LANES), jnp.float32)
    high = low
    for spot, block in zip(spots + known, blocks_of((fields_ref,) + other_refs)):
        part, place = block.astype(jnp.float32), place_of(spot)
        low = jnp.where(place == me - 1, part, low)
        high = jnp.where(place == me + 1, part, high)
    own = 0.5 * x_ref[...] if halve else x_ref[...]
    along = stencil(low, own, high, COL_TAPS, 1)
    along_ref[...] = along
    pay_ref[head:, :] = along.astype(jnp.bfloat16)


def product(coef, spots, factor_ref, out_ref):
    starts = columns_of(spots)
    for n in range(0, len(starts), 2):
        pair = starts[n : n + 2]
        right = jnp.concatenate([factor_ref[:, pl.ds(start, LANES)] for start in pair], axis=1)
        term = jnp.dot(coef, right, preferred_element_type=jnp.float32)
        for m in range(len(pair)):
            out_ref[n + m] = term[:, m * LANES : (m + 1) * LANES].astype(out_ref.dtype)


def far_kernel(rows, cols, groups, ncells, spots, scale_ref, factor_ref, *refs):
    pay_refs, (coef_ref, out_ref) = refs[:groups], refs[groups:]
    ranks = factor_ref.shape[0] // rows
    lines = cols * rows
    span = LANES // rows

    spread = (
        lax.broadcasted_iota(jnp.int32, (LANES, LANES), 1) // rows
        == lax.broadcasted_iota(jnp.int32, (LANES, LANES), 0)
    ).astype(jnp.bfloat16)
    same = (
        lax.rem(lax.broadcasted_iota(jnp.int32, (lines, LANES), 1), rows)
        == lax.rem(lax.broadcasted_iota(jnp.int32, (lines, LANES), 0), rows)
    ).astype(jnp.float32)
    for at in range(0, ranks, LANES):
        count = min(LANES, ranks - at)
        first = at // LANES * 2 * cols
        both = pay_refs[0][first : first + 2 * cols, :].astype(jnp.float32)
        for ref in pay_refs[1:]:
            both = both + ref[first : first + 2 * cols, :].astype(jnp.float32)
        proj = both[:cols] + both[cols:]
        scale = scale_ref[:, at : at + count]
        weights = scale * scale / ncells
        if count < LANES:
            weights = jnp.concatenate([weights, jnp.zeros((1, LANES - count), jnp.float32)], axis=1)
        c = proj * weights
        turned = [c if n == 0 else pltpu.roll(c, LANES - n * span, 1) for n in range(rows)]
        stacked = jnp.concatenate(turned, axis=0).astype(jnp.bfloat16)
        wide = jnp.dot(stacked, spread, preferred_element_type=jnp.float32)
        for n in range(rows):
            start = (at + n * span) * rows
            if start >= ranks * rows:
                break
            piece = wide[n * cols : (n + 1) * cols, :]
            piece = jnp.broadcast_to(piece[:, None, :], (cols, rows, LANES)).reshape(lines, LANES)
            coef_ref[:, start : start + LANES] = (piece * same).astype(jnp.bfloat16)
    product(coef_ref[...], spots, factor_ref, out_ref)


def term_kernel(wanted, after, coef_ref, factor_ref, *refs):
    for (spots, _), out_ref in zip(wanted, refs[after:]):
        product(coef_ref[...], spots, factor_ref, out_ref)


def pair_kernel(mine_ref, got_ref, *out_refs):
    at = 0
    for ref in out_refs:
        end = at + ref.shape[0]
        ref[...] = (mine_ref[at:end] + got_ref[at:end].astype(jnp.float32)).astype(ref.dtype)
        at = end


def local_kernel(rows, cols, halve, b_ref, x_ref, amp_ref, along_ref, *refs):
    pay_refs, base_ref = refs[:-1], refs[-1]
    lines = cols * rows
    head = pay_refs[0].shape[0] - lines
    me = lax.axis_index("grp")
    low = jnp.zeros((lines, LANES), jnp.float32)
    high = low
    for n, ref in enumerate(pay_refs, 1):
        mask = (1 << n) - 1
        part = ref[head:, :].astype(jnp.float32)
        low = jnp.where((me ^ mask) == me - 1, part, low)
        high = jnp.where((me ^ mask) == me + 1, part, high)
    low = low.reshape(cols, rows, LANES)
    high = high.reshape(cols, rows, LANES)
    own = along_ref[...].reshape(cols, rows, LANES)
    conv = stencil(low, own, high, ROW_TAPS, 1)
    x = 0.5 * x_ref[...] if halve else x_ref[...]
    scaled = (amp_ref[...][None] * conv).reshape(lines, LANES)
    base_ref[...] = b_ref[...] - (x + scaled)


def update_kernel(halve, last, x_ref, base_ref, *refs):
    part_refs, (new_ref, other_ref) = refs[:-2], refs[-2:]
    rank_sum = part_refs[0][0]
    for ref in part_refs[1:]:
        rank_sum = rank_sum + ref[0].astype(jnp.float32)
    x = 0.5 * x_ref[...] if halve else x_ref[...]
    residual = base_ref[...] - rank_sum
    new = x + 0.5 * residual
    new_ref[...] = new
    if last:
        other_ref[...] = residual
    else:
        other_ref[0] = new.astype(jnp.bfloat16)


def on_device(right_side, amplitude, factor, scale):
    cols, rows, width = right_side.shape
    ranks = factor.shape[0]
    tiles = lax.axis_size("tile")
    groups = lax.axis_size("grp")
    near = tiles // 2
    lines = cols * rows
    ncells_all = rows * width * groups * tiles
    blocks = -(-ranks // LANES)
    flat = factor.reshape(ranks * rows, tiles * width)
    b = right_side.reshape(lines, width)
    scale = scale.reshape(1, ranks)
    x = b
    short = (0.5 * b).astype(jnp.bfloat16)[None]
    pay_rows = blocks * 2 * cols + lines

    f32, bf16 = jnp.float32, jnp.bfloat16

    def shape(dtype, *dims):
        return jax.ShapeDtypeStruct(dims, dtype)

    def call(kernel, out_shape, flops=0, moved=1 << 18, **options):
        return pl.pallas_call(
            kernel,
            out_shape=out_shape,
            compiler_params=pltpu.CompilerParams(vmem_limit_bytes=32 * 1024 * 1024),
            cost_estimate=pl.CostEstimate(flops=flops, bytes_accessed=moved, transcendentals=0),
            **options,
        )

    work = lines * ranks * rows * tiles * width
    held = call(
        load_kernel,
        shape(bf16, *flat.shape),
        moved=4 * flat.size,
        in_specs=[pl.BlockSpec(memory_space=pltpu.HBM)],
        out_specs=pl.BlockSpec(memory_space=pltpu.VMEM),
        scratch_shapes=[pltpu.SemaphoreType.DMA((8,))],
        name="load",
    )(flat)
    half = near // 2
    close, away = list(range(half)), list(range(near - 1, half - 1, -1))

    def spots_of(masks, other):
        return [(mask, other != (mask > 0)) for mask in masks]

    def cross(value, mask):
        return swap(value, "tile", 2 * mask + 1)

    def first(fields, spots, *before):
        return call(
            partial(first_kernel, rows, spots, len(before)),
            shape(f32, blocks * LANES, lines),
            flops=work,
            moved=flat.size,
            name="project_own",
        )(held, *fields, *before)

    for step in range(ITERS):
        halve = step == 0
        order = list(range(1, near))
        order.sort(key=lambda mask: (mask == half, mask))
        parts = [cross(short, mask) for mask in order]
        bundle = call(
            join_kernel,
            shape(bf16, near, lines, width),
            in_specs=[pl.BlockSpec(memory_space=pl.ANY)]
            + [pl.BlockSpec(memory_space=pltpu.VMEM)] * near,
            name="join",
        )(held, short, *parts)
        across = swap(bundle, "tile", 1)
        known = spots_of([0] + order, False)
        diag = first([bundle], known)
        spots = spots_of([0] + order, True)
        pay, part, along = call(
            partial(second_kernel, rows, cols, halve, spots, known),
            (
                shape(bf16, pay_rows, width),
                shape(bf16, pay_rows - lines, width),
                shape(f32, lines, width),
            ),
            flops=work,
            moved=flat.size,
            scratch_shapes=[pltpu.VMEM((blocks * LANES, lines), f32)],
            name="project_across",
        )(x, held, diag, across, bundle)
        pays = [swap(part if mask & (mask + 1) else pay, "grp", mask) for mask in range(1, groups)]
        coef, far = call(
            partial(far_kernel, rows, cols, groups, ncells_all, spots_of(away, True)),
            (shape(bf16, lines, ranks * rows), shape(bf16, half, lines, width)),
            flops=work // 2,
            moved=flat.size,
            name="term_first",
        )(scale, held, part, *pays)
        got = swap(far, "tile", 1)

        def term(*wanted, after=()):
            return call(
                partial(term_kernel, wanted, len(after)),
                in_specs=[pl.BlockSpec(memory_space=pltpu.VMEM)] * 2
                + [pl.BlockSpec(memory_space=pl.ANY)] * len(after),
                out_shape=[shape(dtype, len(spots), lines, width) for spots, dtype in wanted],
                flops=work // 2 * len(wanted),
                moved=flat.size,
                name="term",
            )(coef, held, *after)

        def pair(mine, got, masks):
            return call(
                pair_kernel,
                [shape(bf16 if mask else f32, 1, lines, width) for mask in masks],
                name="pair",
            )(mine, got)

        mine, far = term((spots_of(away, False), f32), (spots_of(close, True), bf16))
        sends = pair(mine, got, away)
        terms = [cross(send, mask) for send, mask in zip(sends, away)]
        got = swap(far, "tile", 1)
        (mine,) = term((spots_of(close, False), f32), after=sends)
        kept, *sends = pair(mine, got, close)
        terms += [cross(send, mask) for send, mask in zip(sends, close[1:])]
        rims = [pay for mask, pay in enumerate(pays, 1) if not mask & (mask + 1)]
        base = call(
            partial(local_kernel, rows, cols, halve), shape(f32, lines, width), name="local"
        )(b, x, amplitude, along, *rims)
        last = step == ITERS - 1
        x, short = call(
            partial(update_kernel, halve, last),
            (
                shape(f32, lines, width),
                shape(f32, lines, width) if last else shape(bf16, 1, lines, width),
            ),
            name="update",
        )(x, base, kept, *terms)
    return x.reshape(cols, rows, width), short.reshape(cols, rows, width)


def solution(mesh):
    in_specs = (P(None, "grp", "tile"), P("grp", "tile"), P("tile", "grp", None), P("tile"))
    out_specs = (P(None, "grp", "tile"), P(None, "grp", "tile"))
    return jax.shard_map(
        on_device, mesh=mesh, in_specs=in_specs, out_specs=out_specs, check_vma=False
    )
```

```python
import math
from functools import partial

import jax
import jax.numpy as jnp
import numpy as np
from jax import lax
from jax.experimental import pallas as pl
from jax.experimental.pallas import tpu as pltpu
from jax.sharding import PartitionSpec as P

REACH = 8
ITERS = 2
LANES = 128


def taper(sigma):
    offsets = np.arange(-REACH, REACH + 1).astype(np.float64)
    values = np.exp(-offsets * offsets / (2.0 * sigma * sigma))
    values = values * np.cos(np.pi * offsets / (2.0 * REACH + 2.0)) ** 2
    return [float(v) for v in (values / values.sum()).astype(np.float32)]


ROW_TAPS = taper(3.0)
COL_TAPS = taper(5.0)


def stencil(low, own, high, taps, axis):
    size = own.shape[axis]
    place = lax.broadcasted_iota(jnp.int32, own.shape, axis)
    total = taps[REACH] * own
    for shift in range(1, REACH + 1):
        after = pltpu.roll(jnp.where(place < shift, high, own), size - shift, axis)
        before = pltpu.roll(jnp.where(place >= size - shift, low, own), shift, axis)
        total = total + taps[REACH + shift] * after + taps[REACH - shift] * before
    return total


def swap(value, axis, mask):
    return lax.ppermute(value, axis, [(i, i ^ mask) for i in range(lax.axis_size(axis))])


def place_of(spot):
    mask, other = spot
    me = lax.axis_index("tile")
    core = lax.rem(me, 2)
    return 2 * (lax.div(me, 2) ^ mask) + (1 - core if other else core)


def columns_of(spots):
    return [pl.multiple_of(place_of(spot) * LANES, LANES) for spot in spots]


def join_kernel(*refs):
    part_refs, out_ref = refs[2:-1], refs[-1]
    at = 0
    for ref in part_refs:
        out_ref[at : at + ref.shape[0]] = ref[...]
        at += ref.shape[0]


def load_kernel(source_ref, out_ref, sems):
    chunks = sems.shape[0]
    count = source_ref.shape[0] // chunks
    copies = [
        pltpu.make_async_copy(
            source_ref.at[pl.ds(n * count, count)], out_ref.at[pl.ds(n * count, count)], sems.at[n]
        )
        for n in range(chunks)
    ]
    for copy in copies:
        copy.start()
    for copy in copies:
        copy.wait()


def diagonal(rows, spots, fields, factor_ref, store):
    lines = fields[0].shape[0]
    count = factor_ref.shape[0]
    field = jnp.concatenate(fields, axis=1)
    step = min(2048, count)
    row_of = lax.broadcasted_iota(jnp.int32, (rows, lines), 0)
    lane_of = lax.broadcasted_iota(jnp.int32, (rows, lines), 1)
    same = (lax.rem(lane_of, rows) == row_of).astype(jnp.float32)
    starts = columns_of(spots)
    for at in range(0, count, step):
        left = jnp.concatenate(
            [factor_ref[at : at + step, pl.ds(start, LANES)] for start in starts], axis=1
        )
        part = lax.dot_general(
            left, field, (((1,), (1,)), ((), ())), preferred_element_type=jnp.float32
        )
        part = part.reshape(step // rows, rows, lines) * same[None]
        store(at // rows, (at + step) // rows, jnp.sum(part, axis=1))


def blocks_of(refs):
    return [ref[n] for ref in refs for n in range(ref.shape[0])]


def first_kernel(rows, spots, added, factor_ref, *refs):
    diag_ref = refs[-1]
    field_refs = refs[: len(refs) - 1 - added]
    ranks = factor_ref.shape[0] // rows
    if diag_ref.shape[0] > ranks:
        diag_ref[...] = jnp.zeros_like(diag_ref)

    def store(start, end, value):
        diag_ref[start:end, :] = refs[-2][start:end, :] + value if added else value

    diagonal(rows, spots, blocks_of(field_refs), factor_ref, store)


def columns_kernel(halve, spots, x_ref, bundle_ref, twin_ref, along_ref, short_ref):
    me = lax.axis_index("tile")
    low = jnp.zeros(x_ref.shape, jnp.float32)
    high = low
    for spot, block in zip(spots, blocks_of([bundle_ref, twin_ref])):
        part, place = block.astype(jnp.float32), place_of(spot)
        low = jnp.where(place == me - 1, part, low)
        high = jnp.where(place == me + 1, part, high)
    own = 0.5 * x_ref[...] if halve else x_ref[...]
    along = stencil(low, own, high, COL_TAPS, 1)
    along_ref[...] = along
    short_ref[...] = along.astype(jnp.bfloat16)


def second_kernel(
    rows, cols, spots, factor_ref, diag_ref, fields_ref, short_ref, pay_ref, part_ref, total
):
    lines = cols * rows
    if total.shape[0] > factor_ref.shape[0] // rows:
        total[...] = jnp.zeros_like(total)

    def store(start, end, value):
        total[start:end, :] = diag_ref[start:end, :] + value

    diagonal(rows, spots, blocks_of([fields_ref]), factor_ref, store)
    pick = (
        lax.broadcasted_iota(jnp.int32, (cols, lines), 1) // rows
        == lax.broadcasted_iota(jnp.int32, (cols, lines), 0)
    ).astype(jnp.bfloat16)
    for at in range(0, total.shape[0], LANES):
        part = total[at : at + LANES, :]
        upper = part.astype(jnp.bfloat16)
        lower = (part - upper.astype(jnp.float32)).astype(jnp.bfloat16)
        dims = (((1,), (1,)), ((), ()))
        proj = lax.dot_general(pick, upper, dims, preferred_element_type=jnp.float32)
        proj = proj + lax.dot_general(pick, lower, dims, preferred_element_type=jnp.float32)
        first = at // LANES * 2 * cols
        upper = proj.astype(jnp.bfloat16)
        lower = (proj - upper.astype(jnp.float32)).astype(jnp.bfloat16)
        for ref in (pay_ref, part_ref):
            ref[first : first + cols, :] = upper
            ref[first + cols : first + 2 * cols, :] = lower

    head = total.shape[0] // LANES * 2 * cols
    pay_ref[head:, :] = short_ref[...]


def product(coef, spots, factor_ref, out_ref):
    starts = columns_of(spots)
    for n in range(0, len(starts), 2):
        pair = starts[n : n + 2]
        right = jnp.concatenate([factor_ref[:, pl.ds(start, LANES)] for start in pair], axis=1)
        term = jnp.dot(coef, right, preferred_element_type=jnp.float32)
        for m in range(len(pair)):
            out_ref[n + m] = term[:, m * LANES : (m + 1) * LANES].astype(out_ref.dtype)


def far_kernel(rows, cols, groups, ncells, spots, scale_ref, factor_ref, *refs):
    pay_refs, (coef_ref, out_ref) = refs[:groups], refs[groups:]
    ranks = factor_ref.shape[0] // rows
    lines = cols * rows
    span = LANES // rows

    spread = (
        lax.broadcasted_iota(jnp.int32, (LANES, LANES), 1) // rows
        == lax.broadcasted_iota(jnp.int32, (LANES, LANES), 0)
    ).astype(jnp.bfloat16)
    same = (
        lax.rem(lax.broadcasted_iota(jnp.int32, (lines, LANES), 1), rows)
        == lax.rem(lax.broadcasted_iota(jnp.int32, (lines, LANES), 0), rows)
    ).astype(jnp.float32)
    for at in range(0, ranks, LANES):
        count = min(LANES, ranks - at)
        first = at // LANES * 2 * cols
        both = pay_refs[0][first : first + 2 * cols, :].astype(jnp.float32)
        for ref in pay_refs[1:]:
            both = both + ref[first : first + 2 * cols, :].astype(jnp.float32)
        proj = both[:cols] + both[cols:]
        scale = scale_ref[:, at : at + count]
        weights = scale * scale / ncells
        if count < LANES:
            weights = jnp.concatenate([weights, jnp.zeros((1, LANES - count), jnp.float32)], axis=1)
        c = proj * weights
        turned = [c if n == 0 else pltpu.roll(c, LANES - n * span, 1) for n in range(rows)]
        stacked = jnp.concatenate(turned, axis=0).astype(jnp.bfloat16)
        wide = jnp.dot(stacked, spread, preferred_element_type=jnp.float32)
        for n in range(rows):
            start = (at + n * span) * rows
            if start >= ranks * rows:
                break
            piece = wide[n * cols : (n + 1) * cols, :]
            piece = jnp.broadcast_to(piece[:, None, :], (cols, rows, LANES)).reshape(lines, LANES)
            coef_ref[:, start : start + LANES] = (piece * same).astype(jnp.bfloat16)
    product(coef_ref[...], spots, factor_ref, out_ref)


def term_kernel(wanted, after, coef_ref, factor_ref, *refs):
    for (spots, _), out_ref in zip(wanted, refs[after:]):
        product(coef_ref[...], spots, factor_ref, out_ref)


def pair_kernel(mine_ref, got_ref, *out_refs):
    at = 0
    for ref in out_refs:
        end = at + ref.shape[0]
        ref[...] = (mine_ref[at:end] + got_ref[at:end].astype(jnp.float32)).astype(ref.dtype)
        at = end


def local_kernel(rows, cols, halve, b_ref, x_ref, amp_ref, along_ref, *refs):
    pay_refs, base_ref = refs[:-1], refs[-1]
    lines = cols * rows
    head = pay_refs[0].shape[0] - lines
    me = lax.axis_index("grp")
    low = jnp.zeros((lines, LANES), jnp.float32)
    high = low
    for n, ref in enumerate(pay_refs, 1):
        mask = (1 << n) - 1
        part = ref[head:, :].astype(jnp.float32)
        low = jnp.where((me ^ mask) == me - 1, part, low)
        high = jnp.where((me ^ mask) == me + 1, part, high)
    low = low.reshape(cols, rows, LANES)
    high = high.reshape(cols, rows, LANES)
    own = along_ref[...].reshape(cols, rows, LANES)
    conv = stencil(low, own, high, ROW_TAPS, 1)
    x = 0.5 * x_ref[...] if halve else x_ref[...]
    scaled = (amp_ref[...][None] * conv).reshape(lines, LANES)
    base_ref[...] = b_ref[...] - (x + scaled)


def update_kernel(halve, last, x_ref, base_ref, *refs):
    part_refs, (new_ref, other_ref) = refs[:-2], refs[-2:]
    rank_sum = part_refs[0][0]
    for ref in part_refs[1:]:
        rank_sum = rank_sum + ref[0].astype(jnp.float32)
    x = 0.5 * x_ref[...] if halve else x_ref[...]
    residual = base_ref[...] - rank_sum
    new = x + 0.5 * residual
    new_ref[...] = new
    if last:
        other_ref[...] = residual
    else:
        other_ref[0] = new.astype(jnp.bfloat16)


def on_device(right_side, amplitude, factor, scale):
    cols, rows, width = right_side.shape
    ranks = factor.shape[0]
    tiles = lax.axis_size("tile")
    groups = lax.axis_size("grp")
    near = tiles // 2
    lines = cols * rows
    ncells_all = rows * width * groups * tiles
    blocks = -(-ranks // LANES)
    flat = factor.reshape(ranks * rows, tiles * width)
    b = right_side.reshape(lines, width)
    scale = scale.reshape(1, ranks)
    x = b
    short = (0.5 * b).astype(jnp.bfloat16)[None]
    pay_rows = blocks * 2 * cols + lines

    f32, bf16 = jnp.float32, jnp.bfloat16

    def shape(dtype, *dims):
        return jax.ShapeDtypeStruct(dims, dtype)

    def call(kernel, out_shape, flops=0, moved=1 << 18, **options):
        return pl.pallas_call(
            kernel,
            out_shape=out_shape,
            compiler_params=pltpu.CompilerParams(vmem_limit_bytes=32 * 1024 * 1024),
            cost_estimate=pl.CostEstimate(flops=flops, bytes_accessed=moved, transcendentals=0),
            **options,
        )

    work = lines * ranks * rows * tiles * width
    held = call(
        load_kernel,
        shape(bf16, *flat.shape),
        moved=4 * flat.size,
        in_specs=[pl.BlockSpec(memory_space=pltpu.HBM)],
        out_specs=pl.BlockSpec(memory_space=pltpu.VMEM),
        scratch_shapes=[pltpu.SemaphoreType.DMA((8,))],
        name="load",
    )(flat)
    half = near // 2
    close = list(range(half))

    def spots_of(masks, other):
        return [(mask, other != (mask > 0)) for mask in masks]

    def cross(value, mask):
        return swap(value, "tile", 2 * mask + 1)

    def first(fields, spots, *before):
        return call(
            partial(first_kernel, rows, spots, len(before)),
            shape(f32, blocks * LANES, lines),
            flops=work,
            moved=flat.size,
            name="project_own",
        )(held, *fields, *before)

    for step in range(ITERS):
        halve = step == 0
        last = step == ITERS - 1
        away = sorted(range(half, near), reverse=last)
        order = list(range(1, near))
        order.sort(key=lambda mask: (mask == half, mask))
        parts = [cross(short, mask) for mask in order]
        twin = swap(short, "tile", 1)
        bundle = call(
            join_kernel,
            shape(bf16, near - 1, lines, width),
            in_specs=[pl.BlockSpec(memory_space=pl.ANY)] * 2
            + [pl.BlockSpec(memory_space=pltpu.VMEM)] * (near - 1),
            name="join",
        )(held, twin, *parts)
        across = swap(bundle, "tile", 1)
        known = spots_of(order, False) + [(0, True)]
        diag = first([bundle, twin, short], known + [(0, False)])
        spots = spots_of(order, True)
        along, along_short = call(
            partial(columns_kernel, halve, known),
            (shape(f32, lines, width), shape(bf16, lines, width)),
            name="columns",
        )(x, bundle, twin)
        pay, part = call(
            partial(second_kernel, rows, cols, spots),
            (shape(bf16, pay_rows, width), shape(bf16, pay_rows - lines, width)),
            flops=work,
            moved=flat.size,
            scratch_shapes=[pltpu.VMEM((blocks * LANES, lines), f32)],
            name="project_across",
        )(held, diag, across, along_short)
        pays = [swap(part if mask & (mask + 1) else pay, "grp", mask) for mask in range(1, groups)]
        coef, far = call(
            partial(far_kernel, rows, cols, groups, ncells_all, spots_of(away, True)),
            (shape(bf16, lines, ranks * rows), shape(bf16, half, lines, width)),
            flops=work // 2,
            moved=flat.size,
            name="term_first",
        )(scale, held, part, *pays)
        got = swap(far, "tile", 1)

        def term(*wanted, after=()):
            return call(
                partial(term_kernel, wanted, len(after)),
                in_specs=[pl.BlockSpec(memory_space=pltpu.VMEM)] * 2
                + [pl.BlockSpec(memory_space=pl.ANY)] * len(after),
                out_shape=[shape(dtype, len(spots), lines, width) for spots, dtype in wanted],
                flops=work // 2 * len(wanted),
                moved=flat.size,
                name="term",
            )(coef, held, *after)

        def pair(mine, got, masks):
            return call(
                pair_kernel,
                [shape(bf16 if mask else f32, 1, lines, width) for mask in masks],
                name="pair",
            )(mine, got)

        mine, far = term((spots_of(away, False), f32), (spots_of(close, True), bf16))
        sends = pair(mine, got, away)
        terms = [cross(send, mask) for send, mask in zip(sends, away)]
        got = swap(far, "tile", 1)
        (mine,) = term((spots_of(close, False), f32), after=sends)
        kept, *sends = pair(mine, got, close)
        terms += [cross(send, mask) for send, mask in zip(sends, close[1:])]
        rims = [pay for mask, pay in enumerate(pays, 1) if not mask & (mask + 1)]
        base = call(
            partial(local_kernel, rows, cols, halve), shape(f32, lines, width), name="local"
        )(b, x, amplitude, along, *rims)
        x, short = call(
            partial(update_kernel, halve, last),
            (
                shape(f32, lines, width),
                shape(f32, lines, width) if last else shape(bf16, 1, lines, width),
            ),
            name="update",
        )(x, base, kept, *terms)
    return x.reshape(cols, rows, width), short.reshape(cols, rows, width)


def solution(mesh):
    in_specs = (P(None, "grp", "tile"), P("grp", "tile"), P("tile", "grp", None), P("tile"))
    out_specs = (P(None, "grp", "tile"), P(None, "grp", "tile"))
    return jax.shard_map(
        on_device, mesh=mesh, in_specs=in_specs, out_specs=out_specs, check_vma=False
    )
```

```python
import math
from functools import partial

import jax
import jax.numpy as jnp
import numpy as np
from jax import lax
from jax.experimental import pallas as pl
from jax.experimental.pallas import tpu as pltpu
from jax.sharding import PartitionSpec as P

REACH = 8
ITERS = 2
LANES = 128


def taper(sigma):
    offsets = np.arange(-REACH, REACH + 1).astype(np.float64)
    values = np.exp(-offsets * offsets / (2.0 * sigma * sigma))
    values = values * np.cos(np.pi * offsets / (2.0 * REACH + 2.0)) ** 2
    return [float(v) for v in (values / values.sum()).astype(np.float32)]


ROW_TAPS = taper(3.0)
COL_TAPS = taper(5.0)


def stencil(low, own, high, taps, axis):
    size = own.shape[axis]
    place = lax.broadcasted_iota(jnp.int32, own.shape, axis)
    total = taps[REACH] * own
    for shift in range(1, REACH + 1):
        after = pltpu.roll(jnp.where(place < shift, high, own), size - shift, axis)
        before = pltpu.roll(jnp.where(place >= size - shift, low, own), shift, axis)
        total = total + taps[REACH + shift] * after + taps[REACH - shift] * before
    return total


def swap(value, axis, mask):
    return lax.ppermute(value, axis, [(i, i ^ mask) for i in range(lax.axis_size(axis))])


def place_of(spot):
    mask, other = spot
    me = lax.axis_index("tile")
    core = lax.rem(me, 2)
    return 2 * (lax.div(me, 2) ^ mask) + (1 - core if other else core)


def columns_of(spots):
    return [pl.multiple_of(place_of(spot) * LANES, LANES) for spot in spots]


def join_kernel(*refs):
    part_refs, out_ref = refs[2:-1], refs[-1]
    at = 0
    for ref in part_refs:
        out_ref[at : at + ref.shape[0]] = ref[...]
        at += ref.shape[0]


def load_kernel(source_ref, out_ref, sems):
    chunks = sems.shape[0]
    count = source_ref.shape[0] // chunks
    copies = [
        pltpu.make_async_copy(
            source_ref.at[pl.ds(n * count, count)], out_ref.at[pl.ds(n * count, count)], sems.at[n]
        )
        for n in range(chunks)
    ]
    for copy in copies:
        copy.start()
    for copy in copies:
        copy.wait()


def diagonal(rows, spots, fields, factor_ref, store):
    lines = fields[0].shape[0]
    count = factor_ref.shape[0]
    field = jnp.concatenate(fields, axis=1)
    step = min(2048, count)
    row_of = lax.broadcasted_iota(jnp.int32, (rows, lines), 0)
    lane_of = lax.broadcasted_iota(jnp.int32, (rows, lines), 1)
    same = (lax.rem(lane_of, rows) == row_of).astype(jnp.float32)
    starts = columns_of(spots)
    for at in range(0, count, step):
        left = jnp.concatenate(
            [factor_ref[at : at + step, pl.ds(start, LANES)] for start in starts], axis=1
        )
        part = lax.dot_general(
            left, field, (((1,), (1,)), ((), ())), preferred_element_type=jnp.float32
        )
        part = part.reshape(step // rows, rows, lines) * same[None]
        store(at // rows, (at + step) // rows, jnp.sum(part, axis=1))


def blocks_of(refs):
    return [ref[n] for ref in refs for n in range(ref.shape[0])]


def first_kernel(rows, spots, added, factor_ref, *refs):
    diag_ref = refs[-1]
    field_refs = refs[: len(refs) - 1 - added]
    ranks = factor_ref.shape[0] // rows
    if diag_ref.shape[0] > ranks:
        diag_ref[...] = jnp.zeros_like(diag_ref)

    def store(start, end, value):
        diag_ref[start:end, :] = refs[-2][start:end, :] + value if added else value

    diagonal(rows, spots, blocks_of(field_refs), factor_ref, store)


def columns_kernel(halve, spots, x_ref, bundle_ref, twin_ref, along_ref, short_ref):
    me = lax.axis_index("tile")
    low = jnp.zeros(x_ref.shape, jnp.float32)
    high = low
    for spot, block in zip(spots, blocks_of([bundle_ref, twin_ref])):
        part, place = block.astype(jnp.float32), place_of(spot)
        low = jnp.where(place == me - 1, part, low)
        high = jnp.where(place == me + 1, part, high)
    own = 0.5 * x_ref[...] if halve else x_ref[...]
    along = stencil(low, own, high, COL_TAPS, 1)
    along_ref[...] = along
    short_ref[...] = along.astype(jnp.bfloat16)


def second_kernel(
    rows, cols, spots, factor_ref, diag_ref, fields_ref, short_ref, pay_ref, part_ref, total
):
    lines = cols * rows
    if total.shape[0] > factor_ref.shape[0] // rows:
        total[...] = jnp.zeros_like(total)

    def store(start, end, value):
        total[start:end, :] = diag_ref[start:end, :] + value

    diagonal(rows, spots, blocks_of([fields_ref]), factor_ref, store)
    pick = (
        lax.broadcasted_iota(jnp.int32, (cols, lines), 1) // rows
        == lax.broadcasted_iota(jnp.int32, (cols, lines), 0)
    ).astype(jnp.bfloat16)
    for at in range(0, total.shape[0], LANES):
        part = total[at : at + LANES, :]
        upper = part.astype(jnp.bfloat16)
        lower = (part - upper.astype(jnp.float32)).astype(jnp.bfloat16)
        dims = (((1,), (1,)), ((), ()))
        proj = lax.dot_general(pick, upper, dims, preferred_element_type=jnp.float32)
        proj = proj + lax.dot_general(pick, lower, dims, preferred_element_type=jnp.float32)
        first = at // LANES * 2 * cols
        upper = proj.astype(jnp.bfloat16)
        lower = (proj - upper.astype(jnp.float32)).astype(jnp.bfloat16)
        for ref in (pay_ref, part_ref):
            ref[first : first + cols, :] = upper
            ref[first + cols : first + 2 * cols, :] = lower

    head = total.shape[0] // LANES * 2 * cols
    pay_ref[head:, :] = short_ref[...]


def product(coef, spots, factor_ref, out_ref):
    starts = columns_of(spots)
    for n in range(0, len(starts), 2):
        pair = starts[n : n + 2]
        right = jnp.concatenate([factor_ref[:, pl.ds(start, LANES)] for start in pair], axis=1)
        term = jnp.dot(coef, right, preferred_element_type=jnp.float32)
        for m in range(len(pair)):
            out_ref[n + m] = term[:, m * LANES : (m + 1) * LANES].astype(out_ref.dtype)


def far_kernel(rows, cols, groups, ncells, spots, scale_ref, factor_ref, *refs):
    pay_refs, (coef_ref, out_ref) = refs[:groups], refs[groups:]
    ranks = factor_ref.shape[0] // rows
    lines = cols * rows
    span = LANES // rows

    spread = (
        lax.broadcasted_iota(jnp.int32, (LANES, LANES), 1) // rows
        == lax.broadcasted_iota(jnp.int32, (LANES, LANES), 0)
    ).astype(jnp.bfloat16)
    same = (
        lax.rem(lax.broadcasted_iota(jnp.int32, (lines, LANES), 1), rows)
        == lax.rem(lax.broadcasted_iota(jnp.int32, (lines, LANES), 0), rows)
    ).astype(jnp.float32)
    for at in range(0, ranks, LANES):
        count = min(LANES, ranks - at)
        first = at // LANES * 2 * cols
        both = pay_refs[0][first : first + 2 * cols, :].astype(jnp.float32)
        for ref in pay_refs[1:]:
            both = both + ref[first : first + 2 * cols, :].astype(jnp.float32)
        proj = both[:cols] + both[cols:]
        scale = scale_ref[:, at : at + count]
        weights = scale * scale / ncells
        if count < LANES:
            weights = jnp.concatenate([weights, jnp.zeros((1, LANES - count), jnp.float32)], axis=1)
        c = proj * weights
        turned = [c if n == 0 else pltpu.roll(c, LANES - n * span, 1) for n in range(rows)]
        stacked = jnp.concatenate(turned, axis=0).astype(jnp.bfloat16)
        wide = jnp.dot(stacked, spread, preferred_element_type=jnp.float32)
        for n in range(rows):
            start = (at + n * span) * rows
            if start >= ranks * rows:
                break
            piece = wide[n * cols : (n + 1) * cols, :]
            piece = jnp.broadcast_to(piece[:, None, :], (cols, rows, LANES)).reshape(lines, LANES)
            coef_ref[:, start : start + LANES] = (piece * same).astype(jnp.bfloat16)
    product(coef_ref[...], spots, factor_ref, out_ref)


def term_kernel(wanted, after, coef_ref, factor_ref, *refs):
    for (spots, _), out_ref in zip(wanted, refs[after:]):
        product(coef_ref[...], spots, factor_ref, out_ref)


def pair_kernel(mine_ref, got_ref, *out_refs):
    at = 0
    for ref in out_refs:
        end = at + ref.shape[0]
        ref[...] = (mine_ref[at:end] + got_ref[at:end].astype(jnp.float32)).astype(ref.dtype)
        at = end


def local_kernel(rows, cols, halve, b_ref, x_ref, amp_ref, along_ref, *refs):
    pay_refs, base_ref = refs[:-1], refs[-1]
    lines = cols * rows
    head = pay_refs[0].shape[0] - lines
    me = lax.axis_index("grp")
    low = jnp.zeros((lines, LANES), jnp.float32)
    high = low
    for n, ref in enumerate(pay_refs, 1):
        mask = (1 << n) - 1
        part = ref[head:, :].astype(jnp.float32)
        low = jnp.where((me ^ mask) == me - 1, part, low)
        high = jnp.where((me ^ mask) == me + 1, part, high)
    low = low.reshape(cols, rows, LANES)
    high = high.reshape(cols, rows, LANES)
    own = along_ref[...].reshape(cols, rows, LANES)
    conv = stencil(low, own, high, ROW_TAPS, 1)
    x = 0.5 * x_ref[...] if halve else x_ref[...]
    scaled = (amp_ref[...][None] * conv).reshape(lines, LANES)
    base_ref[...] = b_ref[...] - (x + scaled)


def update_kernel(halve, last, x_ref, base_ref, *refs):
    part_refs, (new_ref, other_ref) = refs[:-2], refs[-2:]
    rank_sum = part_refs[0][0]
    for ref in part_refs[1:]:
        rank_sum = rank_sum + ref[0].astype(jnp.float32)
    x = 0.5 * x_ref[...] if halve else x_ref[...]
    residual = base_ref[...] - rank_sum
    new = x + 0.5 * residual
    new_ref[...] = new
    if last:
        other_ref[...] = residual
    else:
        other_ref[0] = new.astype(jnp.bfloat16)


def on_device(right_side, amplitude, factor, scale):
    cols, rows, width = right_side.shape
    ranks = factor.shape[0]
    tiles = lax.axis_size("tile")
    groups = lax.axis_size("grp")
    near = tiles // 2
    lines = cols * rows
    ncells_all = rows * width * groups * tiles
    blocks = -(-ranks // LANES)
    flat = factor.reshape(ranks * rows, tiles * width)
    b = right_side.reshape(lines, width)
    scale = scale.reshape(1, ranks)
    x = b
    short = (0.5 * b).astype(jnp.bfloat16)[None]
    pay_rows = blocks * 2 * cols + lines

    f32, bf16 = jnp.float32, jnp.bfloat16

    def shape(dtype, *dims):
        return jax.ShapeDtypeStruct(dims, dtype)

    def call(kernel, out_shape, flops=0, moved=1 << 18, **options):
        return pl.pallas_call(
            kernel,
            out_shape=out_shape,
            compiler_params=pltpu.CompilerParams(vmem_limit_bytes=32 * 1024 * 1024),
            cost_estimate=pl.CostEstimate(flops=flops, bytes_accessed=moved, transcendentals=0),
            **options,
        )

    work = lines * ranks * rows * tiles * width
    held = call(
        load_kernel,
        shape(bf16, *flat.shape),
        moved=4 * flat.size,
        in_specs=[pl.BlockSpec(memory_space=pltpu.HBM)],
        out_specs=pl.BlockSpec(memory_space=pltpu.VMEM),
        scratch_shapes=[pltpu.SemaphoreType.DMA((8,))],
        name="load",
    )(flat)
    half = near // 2
    close = list(range(half))

    def spots_of(masks, other):
        return [(mask, other != (mask > 0)) for mask in masks]

    def cross(value, mask):
        return swap(value, "tile", 2 * mask + 1)

    def first(fields, spots, *before):
        return call(
            partial(first_kernel, rows, spots, len(before)),
            shape(f32, blocks * LANES, lines),
            flops=work,
            moved=flat.size,
            name="project_own",
        )(held, *fields, *before)

    for step in range(ITERS):
        halve = step == 0
        last = step == ITERS - 1
        away = sorted(range(half, near), reverse=last)
        order = list(range(1, near))
        order.sort(key=lambda mask: (mask == half, mask))
        parts = [cross(short, mask) for mask in order]
        twin = swap(short, "tile", 1)
        diag = first([twin, short], [(0, True), (0, False)])
        bundle = call(
            join_kernel,
            shape(bf16, near - 1, lines, width),
            in_specs=[pl.BlockSpec(memory_space=pl.ANY)] * 2
            + [pl.BlockSpec(memory_space=pltpu.VMEM)] * (near - 1),
            name="join",
        )(diag, twin, *parts)
        across = swap(bundle, "tile", 1)
        known = spots_of(order, False) + [(0, True)]
        diag = first([bundle], spots_of(order, False), diag)
        spots = spots_of(order, True)
        along, along_short = call(
            partial(columns_kernel, halve, known),
            (shape(f32, lines, width), shape(bf16, lines, width)),
            name="columns",
        )(x, bundle, twin)
        pay, part = call(
            partial(second_kernel, rows, cols, spots),
            (shape(bf16, pay_rows, width), shape(bf16, pay_rows - lines, width)),
            flops=work,
            moved=flat.size,
            scratch_shapes=[pltpu.VMEM((blocks * LANES, lines), f32)],
            name="project_across",
        )(held, diag, across, along_short)
        pays = [swap(part if mask & (mask + 1) else pay, "grp", mask) for mask in range(1, groups)]
        coef, far = call(
            partial(far_kernel, rows, cols, groups, ncells_all, spots_of(away, True)),
            (shape(bf16, lines, ranks * rows), shape(bf16, half, lines, width)),
            flops=work // 2,
            moved=flat.size,
            name="term_first",
        )(scale, held, part, *pays)
        got = swap(far, "tile", 1)

        def term(*wanted, after=()):
            return call(
                partial(term_kernel, wanted, len(after)),
                in_specs=[pl.BlockSpec(memory_space=pltpu.VMEM)] * 2
                + [pl.BlockSpec(memory_space=pl.ANY)] * len(after),
                out_shape=[shape(dtype, len(spots), lines, width) for spots, dtype in wanted],
                flops=work // 2 * len(wanted),
                moved=flat.size,
                name="term",
            )(coef, held, *after)

        def pair(mine, got, masks):
            return call(
                pair_kernel,
                [shape(bf16 if mask else f32, 1, lines, width) for mask in masks],
                name="pair",
            )(mine, got)

        mine, far = term((spots_of(away, False), f32), (spots_of(close, True), bf16))
        sends = pair(mine, got, away)
        terms = [cross(send, mask) for send, mask in zip(sends, away)]
        got = swap(far, "tile", 1)
        (mine,) = term((spots_of(close, False), f32), after=sends)
        kept, *sends = pair(mine, got, close)
        terms += [cross(send, mask) for send, mask in zip(sends, close[1:])]
        rims = [pay for mask, pay in enumerate(pays, 1) if not mask & (mask + 1)]
        base = call(
            partial(local_kernel, rows, cols, halve), shape(f32, lines, width), name="local"
        )(b, x, amplitude, along, *rims)
        x, short = call(
            partial(update_kernel, halve, last),
            (
                shape(f32, lines, width),
                shape(f32, lines, width) if last else shape(bf16, 1, lines, width),
            ),
            name="update",
        )(x, base, kept, *terms)
    return x.reshape(cols, rows, width), short.reshape(cols, rows, width)


def solution(mesh):
    in_specs = (P(None, "grp", "tile"), P("grp", "tile"), P("tile", "grp", None), P("tile"))
    out_specs = (P(None, "grp", "tile"), P(None, "grp", "tile"))
    return jax.shard_map(
        on_device, mesh=mesh, in_specs=in_specs, out_specs=out_specs, check_vma=False
    )
```

```python
import math
from functools import partial

import jax
import jax.numpy as jnp
import numpy as np
from jax import lax
from jax.experimental import pallas as pl
from jax.experimental.pallas import tpu as pltpu
from jax.sharding import PartitionSpec as P

REACH = 8
ITERS = 2
LANES = 128


def taper(sigma):
    offsets = np.arange(-REACH, REACH + 1).astype(np.float64)
    values = np.exp(-offsets * offsets / (2.0 * sigma * sigma))
    values = values * np.cos(np.pi * offsets / (2.0 * REACH + 2.0)) ** 2
    return [float(v) for v in (values / values.sum()).astype(np.float32)]


ROW_TAPS = taper(3.0)
COL_TAPS = taper(5.0)


def stencil(low, own, high, taps, axis):
    size = own.shape[axis]
    place = lax.broadcasted_iota(jnp.int32, own.shape, axis)
    total = taps[REACH] * own
    for shift in range(1, REACH + 1):
        after = pltpu.roll(jnp.where(place < shift, high, own), size - shift, axis)
        before = pltpu.roll(jnp.where(place >= size - shift, low, own), shift, axis)
        total = total + taps[REACH + shift] * after + taps[REACH - shift] * before
    return total


def swap(value, axis, mask):
    return lax.ppermute(value, axis, [(i, i ^ mask) for i in range(lax.axis_size(axis))])


def place_of(spot):
    mask, other = spot
    me = lax.axis_index("tile")
    core = lax.rem(me, 2)
    return 2 * (lax.div(me, 2) ^ mask) + (1 - core if other else core)


def columns_of(spots):
    return [pl.multiple_of(place_of(spot) * LANES, LANES) for spot in spots]


def join_kernel(*refs):
    part_refs, out_ref = refs[2:-1], refs[-1]
    at = 0
    for ref in part_refs:
        out_ref[at : at + ref.shape[0]] = ref[...]
        at += ref.shape[0]


def load_kernel(source_ref, out_ref, sems):
    chunks = sems.shape[0]
    count = source_ref.shape[0] // chunks
    copies = [
        pltpu.make_async_copy(
            source_ref.at[pl.ds(n * count, count)], out_ref.at[pl.ds(n * count, count)], sems.at[n]
        )
        for n in range(chunks)
    ]
    for copy in copies:
        copy.start()
    for copy in copies:
        copy.wait()


def diagonal(rows, spots, fields, factor_ref, store):
    lines = fields[0].shape[0]
    count = factor_ref.shape[0]
    field = jnp.concatenate(fields, axis=1)
    step = min(2048, count)
    row_of = lax.broadcasted_iota(jnp.int32, (rows, lines), 0)
    lane_of = lax.broadcasted_iota(jnp.int32, (rows, lines), 1)
    same = (lax.rem(lane_of, rows) == row_of).astype(jnp.float32)
    starts = columns_of(spots)
    for at in range(0, count, step):
        left = jnp.concatenate(
            [factor_ref[at : at + step, pl.ds(start, LANES)] for start in starts], axis=1
        )
        part = lax.dot_general(
            left, field, (((1,), (1,)), ((), ())), preferred_element_type=jnp.float32
        )
        part = part.reshape(step // rows, rows, lines) * same[None]
        store(at // rows, (at + step) // rows, jnp.sum(part, axis=1))


def blocks_of(refs):
    return [ref[n] for ref in refs for n in range(ref.shape[0])]


def first_kernel(rows, spots, added, factor_ref, *refs):
    diag_ref = refs[-1]
    field_refs = refs[: len(refs) - 1 - added]
    ranks = factor_ref.shape[0] // rows
    if diag_ref.shape[0] > ranks:
        diag_ref[...] = jnp.zeros_like(diag_ref)

    def store(start, end, value):
        diag_ref[start:end, :] = refs[-2][start:end, :] + value if added else value

    diagonal(rows, spots, blocks_of(field_refs), factor_ref, store)


def columns_kernel(halve, masks, x_ref, bundle_ref, twin_ref, along_ref, short_ref):
    me = lax.axis_index("tile")
    chip, core = lax.div(me, 2), lax.rem(me, 2)
    near = bundle_ref.shape[0] + 1
    beside = chip + 2 * core - 1
    slot = 0
    for n, mask in enumerate(masks):
        slot = jnp.where((chip ^ beside) == mask, n, slot)
    far = bundle_ref[slot].astype(jnp.float32)
    far = jnp.where((beside >= 0) & (beside < near), far, 0.0)
    twin = twin_ref[0].astype(jnp.float32)
    low = jnp.where(core == 0, far, twin)
    high = jnp.where(core == 0, twin, far)
    own = 0.5 * x_ref[...] if halve else x_ref[...]
    along = stencil(low, own, high, COL_TAPS, 1)
    along_ref[...] = along
    short_ref[...] = along.astype(jnp.bfloat16)


def second_kernel(
    rows, cols, spots, factor_ref, diag_ref, fields_ref, short_ref, pay_ref, part_ref, total
):
    lines = cols * rows
    if total.shape[0] > factor_ref.shape[0] // rows:
        total[...] = jnp.zeros_like(total)

    def store(start, end, value):
        total[start:end, :] = diag_ref[start:end, :] + value

    diagonal(rows, spots, blocks_of([fields_ref]), factor_ref, store)
    pick = (
        lax.broadcasted_iota(jnp.int32, (cols, lines), 1) // rows
        == lax.broadcasted_iota(jnp.int32, (cols, lines), 0)
    ).astype(jnp.bfloat16)
    for at in range(0, total.shape[0], LANES):
        part = total[at : at + LANES, :]
        upper = part.astype(jnp.bfloat16)
        lower = (part - upper.astype(jnp.float32)).astype(jnp.bfloat16)
        dims = (((1,), (1,)), ((), ()))
        proj = lax.dot_general(pick, upper, dims, preferred_element_type=jnp.float32)
        proj = proj + lax.dot_general(pick, lower, dims, preferred_element_type=jnp.float32)
        first = at // LANES * 2 * cols
        upper = proj.astype(jnp.bfloat16)
        lower = (proj - upper.astype(jnp.float32)).astype(jnp.bfloat16)
        for ref in (pay_ref, part_ref):
            ref[first : first + cols, :] = upper
            ref[first + cols : first + 2 * cols, :] = lower

    head = total.shape[0] // LANES * 2 * cols
    pay_ref[head:, :] = short_ref[...]


def product(coef, spots, factor_ref, out_ref):
    starts = columns_of(spots)
    for n in range(0, len(starts), 2):
        pair = starts[n : n + 2]
        right = jnp.concatenate([factor_ref[:, pl.ds(start, LANES)] for start in pair], axis=1)
        term = jnp.dot(coef, right, preferred_element_type=jnp.float32)
        for m in range(len(pair)):
            out_ref[n + m] = term[:, m * LANES : (m + 1) * LANES].astype(out_ref.dtype)


def far_kernel(rows, cols, groups, ncells, spots, scale_ref, factor_ref, *refs):
    pay_refs, (coef_ref, out_ref) = refs[:groups], refs[groups:]
    ranks = factor_ref.shape[0] // rows
    lines = cols * rows
    span = LANES // rows

    spread = (
        lax.broadcasted_iota(jnp.int32, (LANES, LANES), 1) // rows
        == lax.broadcasted_iota(jnp.int32, (LANES, LANES), 0)
    ).astype(jnp.bfloat16)
    same = (
        lax.rem(lax.broadcasted_iota(jnp.int32, (lines, LANES), 1), rows)
        == lax.rem(lax.broadcasted_iota(jnp.int32, (lines, LANES), 0), rows)
    ).astype(jnp.float32)
    for at in range(0, ranks, LANES):
        count = min(LANES, ranks - at)
        first = at // LANES * 2 * cols
        both = pay_refs[0][first : first + 2 * cols, :].astype(jnp.float32)
        for ref in pay_refs[1:]:
            both = both + ref[first : first + 2 * cols, :].astype(jnp.float32)
        proj = both[:cols] + both[cols:]
        scale = scale_ref[:, at : at + count]
        weights = scale * scale / ncells
        if count < LANES:
            weights = jnp.concatenate([weights, jnp.zeros((1, LANES - count), jnp.float32)], axis=1)
        c = proj * weights
        turned = [c if n == 0 else pltpu.roll(c, LANES - n * span, 1) for n in range(rows)]
        stacked = jnp.concatenate(turned, axis=0).astype(jnp.bfloat16)
        wide = jnp.dot(stacked, spread, preferred_element_type=jnp.float32)
        for n in range(rows):
            start = (at + n * span) * rows
            if start >= ranks * rows:
                break
            piece = wide[n * cols : (n + 1) * cols, :]
            piece = jnp.broadcast_to(piece[:, None, :], (cols, rows, LANES)).reshape(lines, LANES)
            coef_ref[:, start : start + LANES] = (piece * same).astype(jnp.bfloat16)
    product(coef_ref[...], spots, factor_ref, out_ref)


def term_kernel(wanted, after, coef_ref, factor_ref, *refs):
    for (spots, _), out_ref in zip(wanted, refs[after:]):
        product(coef_ref[...], spots, factor_ref, out_ref)


def pair_kernel(mine_ref, got_ref, *out_refs):
    at = 0
    for ref in out_refs:
        end = at + ref.shape[0]
        ref[...] = (mine_ref[at:end] + got_ref[at:end].astype(jnp.float32)).astype(ref.dtype)
        at = end


def local_kernel(rows, cols, halve, b_ref, x_ref, amp_ref, along_ref, *refs):
    pay_refs, base_ref = refs[:-1], refs[-1]
    lines = cols * rows
    head = pay_refs[0].shape[0] - lines
    me = lax.axis_index("grp")
    low = jnp.zeros((lines, LANES), jnp.float32)
    high = low
    for n, ref in enumerate(pay_refs, 1):
        mask = (1 << n) - 1
        part = ref[head:, :].astype(jnp.float32)
        low = jnp.where((me ^ mask) == me - 1, part, low)
        high = jnp.where((me ^ mask) == me + 1, part, high)
    low = low.reshape(cols, rows, LANES)
    high = high.reshape(cols, rows, LANES)
    own = along_ref[...].reshape(cols, rows, LANES)
    conv = stencil(low, own, high, ROW_TAPS, 1)
    x = 0.5 * x_ref[...] if halve else x_ref[...]
    scaled = (amp_ref[...][None] * conv).reshape(lines, LANES)
    base_ref[...] = b_ref[...] - (x + scaled)


def update_kernel(halve, last, x_ref, base_ref, *refs):
    part_refs, (new_ref, other_ref) = refs[:-2], refs[-2:]
    rank_sum = part_refs[0][0]
    for ref in part_refs[1:]:
        rank_sum = rank_sum + ref[0].astype(jnp.float32)
    x = 0.5 * x_ref[...] if halve else x_ref[...]
    residual = base_ref[...] - rank_sum
    new = x + 0.5 * residual
    new_ref[...] = new
    if last:
        other_ref[...] = residual
    else:
        other_ref[0] = new.astype(jnp.bfloat16)


def on_device(right_side, amplitude, factor, scale):
    cols, rows, width = right_side.shape
    ranks = factor.shape[0]
    tiles = lax.axis_size("tile")
    groups = lax.axis_size("grp")
    near = tiles // 2
    lines = cols * rows
    ncells_all = rows * width * groups * tiles
    blocks = -(-ranks // LANES)
    flat = factor.reshape(ranks * rows, tiles * width)
    b = right_side.reshape(lines, width)
    scale = scale.reshape(1, ranks)
    x = b
    short = (0.5 * b).astype(jnp.bfloat16)[None]
    pay_rows = blocks * 2 * cols + lines

    f32, bf16 = jnp.float32, jnp.bfloat16

    def shape(dtype, *dims):
        return jax.ShapeDtypeStruct(dims, dtype)

    def call(kernel, out_shape, flops=0, moved=1 << 18, **options):
        return pl.pallas_call(
            kernel,
            out_shape=out_shape,
            compiler_params=pltpu.CompilerParams(vmem_limit_bytes=32 * 1024 * 1024),
            cost_estimate=pl.CostEstimate(flops=flops, bytes_accessed=moved, transcendentals=0),
            **options,
        )

    work = lines * ranks * rows * tiles * width
    held = call(
        load_kernel,
        shape(bf16, *flat.shape),
        moved=4 * flat.size,
        in_specs=[pl.BlockSpec(memory_space=pltpu.HBM)],
        out_specs=pl.BlockSpec(memory_space=pltpu.VMEM),
        scratch_shapes=[pltpu.SemaphoreType.DMA((8,))],
        name="load",
    )(flat)
    half = near // 2
    close = list(range(half))

    def spots_of(masks, other):
        return [(mask, other != (mask > 0)) for mask in masks]

    def cross(value, mask):
        return swap(value, "tile", 2 * mask + 1)

    def first(fields, spots, *before):
        return call(
            partial(first_kernel, rows, spots, len(before)),
            shape(f32, blocks * LANES, lines),
            flops=work,
            moved=flat.size,
            name="project_own",
        )(held, *fields, *before)

    for step in range(ITERS):
        halve = step == 0
        last = step == ITERS - 1
        away = sorted(range(half, near), reverse=last)
        order = list(range(1, near))
        order.sort(key=lambda mask: (mask == half, mask))
        parts = [cross(short, mask) for mask in order]
        twin = swap(short, "tile", 1)
        diag = first([short], [(0, False)])
        bundle = call(
            join_kernel,
            shape(bf16, near - 1, lines, width),
            in_specs=[pl.BlockSpec(memory_space=pl.ANY)] * 2
            + [pl.BlockSpec(memory_space=pltpu.VMEM)] * (near - 1),
            name="join",
        )(diag, twin, *parts)
        across = swap(bundle, "tile", 1)
        known = spots_of(order, False) + [(0, True)]
        diag = first([bundle, twin], known, diag)
        spots = spots_of(order, True)
        along, along_short = call(
            partial(columns_kernel, halve, order),
            (shape(f32, lines, width), shape(bf16, lines, width)),
            name="columns",
        )(x, bundle, twin)
        pay, part = call(
            partial(second_kernel, rows, cols, spots),
            (shape(bf16, pay_rows, width), shape(bf16, pay_rows - lines, width)),
            flops=work,
            moved=flat.size,
            scratch_shapes=[pltpu.VMEM((blocks * LANES, lines), f32)],
            name="project_across",
        )(held, diag, across, along_short)
        pays = [swap(part if mask & (mask + 1) else pay, "grp", mask) for mask in range(1, groups)]
        coef, far = call(
            partial(far_kernel, rows, cols, groups, ncells_all, spots_of(away, True)),
            (shape(bf16, lines, ranks * rows), shape(bf16, half, lines, width)),
            flops=work // 2,
            moved=flat.size,
            name="term_first",
        )(scale, held, part, *pays)
        got = swap(far, "tile", 1)

        def term(*wanted, after=()):
            return call(
                partial(term_kernel, wanted, len(after)),
                in_specs=[pl.BlockSpec(memory_space=pltpu.VMEM)] * 2
                + [pl.BlockSpec(memory_space=pl.ANY)] * len(after),
                out_shape=[shape(dtype, len(spots), lines, width) for spots, dtype in wanted],
                flops=work // 2 * len(wanted),
                moved=flat.size,
                name="term",
            )(coef, held, *after)

        def pair(mine, got, masks):
            return call(
                pair_kernel,
                [shape(bf16 if mask else f32, 1, lines, width) for mask in masks],
                name="pair",
            )(mine, got)

        mine, far = term((spots_of(away, False), f32), (spots_of(close, True), bf16))
        sends = pair(mine, got, away)
        terms = [cross(send, mask) for send, mask in zip(sends, away)]
        got = swap(far, "tile", 1)
        (mine,) = term((spots_of(close, False), f32), after=sends)
        kept, *sends = pair(mine, got, close)
        terms += [cross(send, mask) for send, mask in zip(sends, close[1:])]
        rims = [pay for mask, pay in enumerate(pays, 1) if not mask & (mask + 1)]
        base = call(
            partial(local_kernel, rows, cols, halve), shape(f32, lines, width), name="local"
        )(b, x, amplitude, along, *rims)
        x, short = call(
            partial(update_kernel, halve, last),
            (
                shape(f32, lines, width),
                shape(f32, lines, width) if last else shape(bf16, 1, lines, width),
            ),
            name="update",
        )(x, base, kept, *terms)
    return x.reshape(cols, rows, width), short.reshape(cols, rows, width)


def solution(mesh):
    in_specs = (P(None, "grp", "tile"), P("grp", "tile"), P("tile", "grp", None), P("tile"))
    out_specs = (P(None, "grp", "tile"), P(None, "grp", "tile"))
    return jax.shard_map(
        on_device, mesh=mesh, in_specs=in_specs, out_specs=out_specs, check_vma=False
    )
```

```python
import math
from functools import partial

import jax
import jax.numpy as jnp
import numpy as np
from jax import lax
from jax.experimental import pallas as pl
from jax.experimental.pallas import tpu as pltpu
from jax.sharding import PartitionSpec as P

REACH = 8
ITERS = 2
LANES = 128


def taper(sigma):
    offsets = np.arange(-REACH, REACH + 1).astype(np.float64)
    values = np.exp(-offsets * offsets / (2.0 * sigma * sigma))
    values = values * np.cos(np.pi * offsets / (2.0 * REACH + 2.0)) ** 2
    return [float(v) for v in (values / values.sum()).astype(np.float32)]


ROW_TAPS = taper(3.0)
COL_TAPS = taper(5.0)


def stencil(low, own, high, taps, axis):
    size = own.shape[axis]
    place = lax.broadcasted_iota(jnp.int32, own.shape, axis)
    total = taps[REACH] * own
    for shift in range(1, REACH + 1):
        after = pltpu.roll(jnp.where(place < shift, high, own), size - shift, axis)
        before = pltpu.roll(jnp.where(place >= size - shift, low, own), shift, axis)
        total = total + taps[REACH + shift] * after + taps[REACH - shift] * before
    return total


def swap(value, axis, mask):
    return lax.ppermute(value, axis, [(i, i ^ mask) for i in range(lax.axis_size(axis))])


def place_of(spot):
    mask, other = spot
    me = lax.axis_index("tile")
    core = lax.rem(me, 2)
    return 2 * (lax.div(me, 2) ^ mask) + (1 - core if other else core)


def columns_of(spots):
    return [pl.multiple_of(place_of(spot) * LANES, LANES) for spot in spots]


def join_kernel(*refs):
    part_refs, out_ref = refs[2:-1], refs[-1]
    at = 0
    for ref in part_refs:
        out_ref[at : at + ref.shape[0]] = ref[...]
        at += ref.shape[0]


def load_kernel(source_ref, out_ref, sems):
    chunks = sems.shape[0]
    count = source_ref.shape[0] // chunks
    copies = [
        pltpu.make_async_copy(
            source_ref.at[pl.ds(n * count, count)], out_ref.at[pl.ds(n * count, count)], sems.at[n]
        )
        for n in range(chunks)
    ]
    for copy in copies:
        copy.start()
    for copy in copies:
        copy.wait()


def diagonal(rows, spots, fields, factor_ref, store):
    lines = fields[0].shape[0]
    count = factor_ref.shape[0]
    field = jnp.concatenate(fields, axis=1)
    step = min(2048, count)
    row_of = lax.broadcasted_iota(jnp.int32, (rows, lines), 0)
    lane_of = lax.broadcasted_iota(jnp.int32, (rows, lines), 1)
    same = (lax.rem(lane_of, rows) == row_of).astype(jnp.float32)
    starts = columns_of(spots)
    for at in range(0, count, step):
        left = jnp.concatenate(
            [factor_ref[at : at + step, pl.ds(start, LANES)] for start in starts], axis=1
        )
        part = lax.dot_general(
            left, field, (((1,), (1,)), ((), ())), preferred_element_type=jnp.float32
        )
        part = part.reshape(step // rows, rows, lines) * same[None]
        store(at // rows, (at + step) // rows, jnp.sum(part, axis=1))


def blocks_of(refs):
    return [ref[n] for ref in refs for n in range(ref.shape[0])]


def first_kernel(rows, spots, added, factor_ref, *refs):
    diag_ref = refs[-1]
    field_refs = refs[: len(refs) - 1 - added]
    ranks = factor_ref.shape[0] // rows
    if diag_ref.shape[0] > ranks:
        diag_ref[...] = jnp.zeros_like(diag_ref)

    def store(start, end, value):
        diag_ref[start:end, :] = refs[-2][start:end, :] + value if added else value

    diagonal(rows, spots, blocks_of(field_refs), factor_ref, store)


def columns_kernel(halve, masks, x_ref, bundle_ref, twin_ref, along_ref, short_ref):
    me = lax.axis_index("tile")
    chip, core = lax.div(me, 2), lax.rem(me, 2)
    near = bundle_ref.shape[0] + 1
    beside = chip + 2 * core - 1
    slot = 0
    for n, mask in enumerate(masks):
        slot = jnp.where((chip ^ beside) == mask, n, slot)
    far = bundle_ref[slot].astype(jnp.float32)
    far = jnp.where((beside >= 0) & (beside < near), far, 0.0)
    twin = twin_ref[0].astype(jnp.float32)
    low = jnp.where(core == 0, far, twin)
    high = jnp.where(core == 0, twin, far)
    own = 0.5 * x_ref[...] if halve else x_ref[...]
    along = stencil(low, own, high, COL_TAPS, 1)
    along_ref[...] = along
    short_ref[...] = along.astype(jnp.bfloat16)


def second_kernel(
    rows, cols, spots, factor_ref, diag_ref, fields_ref, short_ref, pay_ref, part_ref, total
):
    lines = cols * rows
    if total.shape[0] > factor_ref.shape[0] // rows:
        total[...] = jnp.zeros_like(total)

    def store(start, end, value):
        total[start:end, :] = diag_ref[start:end, :] + value

    diagonal(rows, spots, blocks_of([fields_ref]), factor_ref, store)
    pick = (
        lax.broadcasted_iota(jnp.int32, (cols, lines), 1) // rows
        == lax.broadcasted_iota(jnp.int32, (cols, lines), 0)
    ).astype(jnp.bfloat16)
    value = total[...]
    upper = value.astype(jnp.bfloat16)
    lower = (value - upper.astype(jnp.float32)).astype(jnp.bfloat16)
    both = lax.dot_general(
        pick,
        jnp.concatenate([upper, lower], axis=0),
        (((1,), (1,)), ((), ())),
        preferred_element_type=jnp.float32,
    )
    proj = both[:, : total.shape[0]] + both[:, total.shape[0] :]
    for at in range(0, total.shape[0], LANES):
        upper = proj[:, at : at + LANES].astype(jnp.bfloat16)
        lower = (proj[:, at : at + LANES] - upper.astype(jnp.float32)).astype(jnp.bfloat16)
        first = at // LANES * 2 * cols
        for ref in (pay_ref, part_ref):
            ref[first : first + cols, :] = upper
            ref[first + cols : first + 2 * cols, :] = lower

    head = total.shape[0] // LANES * 2 * cols
    pay_ref[head:, :] = short_ref[...]


def product(coef, spots, factor_ref, out_ref):
    starts = columns_of(spots)
    for n in range(0, len(starts), 2):
        pair = starts[n : n + 2]
        right = jnp.concatenate([factor_ref[:, pl.ds(start, LANES)] for start in pair], axis=1)
        term = jnp.dot(coef, right, preferred_element_type=jnp.float32)
        for m in range(len(pair)):
            out_ref[n + m] = term[:, m * LANES : (m + 1) * LANES].astype(out_ref.dtype)


def far_kernel(rows, cols, groups, ncells, spots, scale_ref, factor_ref, *refs):
    pay_refs, (coef_ref, out_ref) = refs[:groups], refs[groups:]
    ranks = factor_ref.shape[0] // rows
    lines = cols * rows
    span = LANES // rows

    spread = (
        lax.broadcasted_iota(jnp.int32, (LANES, LANES), 1) // rows
        == lax.broadcasted_iota(jnp.int32, (LANES, LANES), 0)
    ).astype(jnp.bfloat16)
    same = (
        lax.rem(lax.broadcasted_iota(jnp.int32, (lines, LANES), 1), rows)
        == lax.rem(lax.broadcasted_iota(jnp.int32, (lines, LANES), 0), rows)
    ).astype(jnp.float32)
    turned = []
    for at in range(0, ranks, LANES):
        count = min(LANES, ranks - at)
        first = at // LANES * 2 * cols
        both = pay_refs[0][first : first + 2 * cols, :].astype(jnp.float32)
        for ref in pay_refs[1:]:
            both = both + ref[first : first + 2 * cols, :].astype(jnp.float32)
        proj = both[:cols] + both[cols:]
        scale = scale_ref[:, at : at + count]
        weights = scale * scale / ncells
        if count < LANES:
            weights = jnp.concatenate([weights, jnp.zeros((1, LANES - count), jnp.float32)], axis=1)
        c = proj * weights
        turned += [c if n == 0 else pltpu.roll(c, LANES - n * span, 1) for n in range(rows)]
    stacked = jnp.concatenate(turned, axis=0).astype(jnp.bfloat16)
    wide = jnp.dot(stacked, spread, preferred_element_type=jnp.float32)
    for n in range(ranks * rows // LANES):
        piece = wide[n * cols : (n + 1) * cols, :]
        piece = jnp.broadcast_to(piece[:, None, :], (cols, rows, LANES)).reshape(lines, LANES)
        coef_ref[:, n * LANES : (n + 1) * LANES] = (piece * same).astype(jnp.bfloat16)
    product(coef_ref[...], spots, factor_ref, out_ref)


def term_kernel(wanted, after, coef_ref, factor_ref, *refs):
    for (spots, _), out_ref in zip(wanted, refs[after:]):
        product(coef_ref[...], spots, factor_ref, out_ref)


def pair_kernel(mine_ref, got_ref, *out_refs):
    at = 0
    for ref in out_refs:
        end = at + ref.shape[0]
        ref[...] = (mine_ref[at:end] + got_ref[at:end].astype(jnp.float32)).astype(ref.dtype)
        at = end


def local_kernel(rows, cols, halve, b_ref, x_ref, amp_ref, along_ref, *refs):
    pay_refs, base_ref = refs[:-1], refs[-1]
    lines = cols * rows
    head = pay_refs[0].shape[0] - lines
    me = lax.axis_index("grp")
    low = jnp.zeros((lines, LANES), jnp.float32)
    high = low
    for n, ref in enumerate(pay_refs, 1):
        mask = (1 << n) - 1
        part = ref[head:, :].astype(jnp.float32)
        low = jnp.where((me ^ mask) == me - 1, part, low)
        high = jnp.where((me ^ mask) == me + 1, part, high)
    low = low.reshape(cols, rows, LANES)
    high = high.reshape(cols, rows, LANES)
    own = along_ref[...].reshape(cols, rows, LANES)
    conv = stencil(low, own, high, ROW_TAPS, 1)
    x = 0.5 * x_ref[...] if halve else x_ref[...]
    scaled = (amp_ref[...][None] * conv).reshape(lines, LANES)
    base_ref[...] = b_ref[...] - (x + scaled)


def update_kernel(halve, last, x_ref, base_ref, *refs):
    part_refs, (new_ref, other_ref) = refs[:-2], refs[-2:]
    rank_sum = part_refs[0][0]
    for ref in part_refs[1:]:
        rank_sum = rank_sum + ref[0].astype(jnp.float32)
    x = 0.5 * x_ref[...] if halve else x_ref[...]
    residual = base_ref[...] - rank_sum
    new = x + 0.5 * residual
    new_ref[...] = new
    if last:
        other_ref[...] = residual
    else:
        other_ref[0] = new.astype(jnp.bfloat16)


def on_device(right_side, amplitude, factor, scale):
    cols, rows, width = right_side.shape
    ranks = factor.shape[0]
    tiles = lax.axis_size("tile")
    groups = lax.axis_size("grp")
    near = tiles // 2
    lines = cols * rows
    ncells_all = rows * width * groups * tiles
    blocks = -(-ranks // LANES)
    flat = factor.reshape(ranks * rows, tiles * width)
    b = right_side.reshape(lines, width)
    scale = scale.reshape(1, ranks)
    x = b
    short = (0.5 * b).astype(jnp.bfloat16)[None]
    pay_rows = blocks * 2 * cols + lines

    f32, bf16 = jnp.float32, jnp.bfloat16

    def shape(dtype, *dims):
        return jax.ShapeDtypeStruct(dims, dtype)

    def call(kernel, out_shape, flops=0, moved=1 << 18, **options):
        return pl.pallas_call(
            kernel,
            out_shape=out_shape,
            compiler_params=pltpu.CompilerParams(vmem_limit_bytes=32 * 1024 * 1024),
            cost_estimate=pl.CostEstimate(flops=flops, bytes_accessed=moved, transcendentals=0),
            **options,
        )

    work = lines * ranks * rows * tiles * width
    held = call(
        load_kernel,
        shape(bf16, *flat.shape),
        moved=4 * flat.size,
        in_specs=[pl.BlockSpec(memory_space=pltpu.HBM)],
        out_specs=pl.BlockSpec(memory_space=pltpu.VMEM),
        scratch_shapes=[pltpu.SemaphoreType.DMA((8,))],
        name="load",
    )(flat)
    half = near // 2
    close = list(range(half))

    def spots_of(masks, other):
        return [(mask, other != (mask > 0)) for mask in masks]

    def cross(value, mask):
        return swap(value, "tile", 2 * mask + 1)

    def first(fields, spots, *before):
        return call(
            partial(first_kernel, rows, spots, len(before)),
            shape(f32, blocks * LANES, lines),
            flops=work,
            moved=flat.size,
            name="project_own",
        )(held, *fields, *before)

    for step in range(ITERS):
        halve = step == 0
        last = step == ITERS - 1
        away = sorted(range(half, near), reverse=last)
        order = list(range(1, near))
        order.sort(key=lambda mask: (mask == half, mask))
        parts = [cross(short, mask) for mask in order]
        twin = swap(short, "tile", 1)
        diag = first([short], [(0, False)])
        bundle = call(
            join_kernel,
            shape(bf16, near - 1, lines, width),
            in_specs=[pl.BlockSpec(memory_space=pl.ANY)] * 2
            + [pl.BlockSpec(memory_space=pltpu.VMEM)] * (near - 1),
            name="join",
        )(diag, twin, *parts)
        across = swap(bundle, "tile", 1)
        known = spots_of(order, False) + [(0, True)]
        diag = first([bundle, twin], known, diag)
        spots = spots_of(order, True)
        along, along_short = call(
            partial(columns_kernel, halve, order),
            (shape(f32, lines, width), shape(bf16, lines, width)),
            name="columns",
        )(x, bundle, twin)
        pay, part = call(
            partial(second_kernel, rows, cols, spots),
            (shape(bf16, pay_rows, width), shape(bf16, pay_rows - lines, width)),
            flops=work,
            moved=flat.size,
            scratch_shapes=[pltpu.VMEM((blocks * LANES, lines), f32)],
            name="project_across",
        )(held, diag, across, along_short)
        pays = [swap(part if mask & (mask + 1) else pay, "grp", mask) for mask in range(1, groups)]
        coef, far = call(
            partial(far_kernel, rows, cols, groups, ncells_all, spots_of(away, True)),
            (shape(bf16, lines, ranks * rows), shape(bf16, half, lines, width)),
            flops=work // 2,
            moved=flat.size,
            name="term_first",
        )(scale, held, part, *pays)
        got = swap(far, "tile", 1)

        def term(*wanted, after=()):
            return call(
                partial(term_kernel, wanted, len(after)),
                in_specs=[pl.BlockSpec(memory_space=pltpu.VMEM)] * 2
                + [pl.BlockSpec(memory_space=pl.ANY)] * len(after),
                out_shape=[shape(dtype, len(spots), lines, width) for spots, dtype in wanted],
                flops=work // 2 * len(wanted),
                moved=flat.size,
                name="term",
            )(coef, held, *after)

        def pair(mine, got, masks):
            return call(
                pair_kernel,
                [shape(bf16 if mask else f32, 1, lines, width) for mask in masks],
                name="pair",
            )(mine, got)

        mine, far = term((spots_of(away, False), f32), (spots_of(close, True), bf16))
        sends = pair(mine, got, away)
        terms = [cross(send, mask) for send, mask in zip(sends, away)]
        got = swap(far, "tile", 1)
        (mine,) = term((spots_of(close, False), f32), after=sends)
        kept, *sends = pair(mine, got, close)
        terms += [cross(send, mask) for send, mask in zip(sends, close[1:])]
        rims = [pay for mask, pay in enumerate(pays, 1) if not mask & (mask + 1)]
        base = call(
            partial(local_kernel, rows, cols, halve), shape(f32, lines, width), name="local"
        )(b, x, amplitude, along, *rims)
        x, short = call(
            partial(update_kernel, halve, last),
            (
                shape(f32, lines, width),
                shape(f32, lines, width) if last else shape(bf16, 1, lines, width),
            ),
            name="update",
        )(x, base, kept, *terms)
    return x.reshape(cols, rows, width), short.reshape(cols, rows, width)


def solution(mesh):
    in_specs = (P(None, "grp", "tile"), P("grp", "tile"), P("tile", "grp", None), P("tile"))
    out_specs = (P(None, "grp", "tile"), P(None, "grp", "tile"))
    return jax.shard_map(
        on_device, mesh=mesh, in_specs=in_specs, out_specs=out_specs, check_vma=False
    )
```

```python
import math
from functools import partial

import jax
import jax.numpy as jnp
import numpy as np
from jax import lax
from jax.experimental import pallas as pl
from jax.experimental.pallas import tpu as pltpu
from jax.sharding import PartitionSpec as P

REACH = 8
ITERS = 2
LANES = 128


def taper(sigma):
    offsets = np.arange(-REACH, REACH + 1).astype(np.float64)
    values = np.exp(-offsets * offsets / (2.0 * sigma * sigma))
    values = values * np.cos(np.pi * offsets / (2.0 * REACH + 2.0)) ** 2
    return [float(v) for v in (values / values.sum()).astype(np.float32)]


ROW_TAPS = taper(3.0)
COL_TAPS = taper(5.0)


def stencil(low, own, high, taps, axis):
    size = own.shape[axis]
    place = lax.broadcasted_iota(jnp.int32, own.shape, axis)
    total = taps[REACH] * own
    for shift in range(1, REACH + 1):
        after = pltpu.roll(jnp.where(place < shift, high, own), size - shift, axis)
        before = pltpu.roll(jnp.where(place >= size - shift, low, own), shift, axis)
        total = total + taps[REACH + shift] * after + taps[REACH - shift] * before
    return total


def swap(value, axis, mask):
    return lax.ppermute(value, axis, [(i, i ^ mask) for i in range(lax.axis_size(axis))])


def place_of(spot):
    mask, other = spot
    me = lax.axis_index("tile")
    core = lax.rem(me, 2)
    return 2 * (lax.div(me, 2) ^ mask) + (1 - core if other else core)


def columns_of(spots):
    return [pl.multiple_of(place_of(spot) * LANES, LANES) for spot in spots]


def join_kernel(*refs):
    part_refs, out_ref = refs[2:-1], refs[-1]
    at = 0
    for ref in part_refs:
        out_ref[at : at + ref.shape[0]] = ref[...]
        at += ref.shape[0]


def load_kernel(source_ref, out_ref, sems):
    chunks = sems.shape[0]
    count = source_ref.shape[0] // chunks
    copies = [
        pltpu.make_async_copy(
            source_ref.at[pl.ds(n * count, count)], out_ref.at[pl.ds(n * count, count)], sems.at[n]
        )
        for n in range(chunks)
    ]
    for copy in copies:
        copy.start()
    for copy in copies:
        copy.wait()


def diagonal(rows, spots, fields, factor_ref, store):
    lines = fields[0].shape[0]
    count = factor_ref.shape[0]
    field = jnp.concatenate(fields, axis=1)
    step = min(2048, count)
    row_of = lax.broadcasted_iota(jnp.int32, (rows, lines), 0)
    lane_of = lax.broadcasted_iota(jnp.int32, (rows, lines), 1)
    same = (lax.rem(lane_of, rows) == row_of).astype(jnp.float32)
    starts = columns_of(spots)
    for at in range(0, count, step):
        left = jnp.concatenate(
            [factor_ref[at : at + step, pl.ds(start, LANES)] for start in starts], axis=1
        )
        part = lax.dot_general(
            left, field, (((1,), (1,)), ((), ())), preferred_element_type=jnp.float32
        )
        part = part.reshape(step // rows, rows, lines) * same[None]
        store(at // rows, (at + step) // rows, jnp.sum(part, axis=1))


def blocks_of(refs):
    return [ref[n] for ref in refs for n in range(ref.shape[0])]


def first_kernel(rows, spots, added, factor_ref, *refs):
    diag_ref = refs[-1]
    field_refs = refs[: len(refs) - 1 - added]
    ranks = factor_ref.shape[0] // rows
    if diag_ref.shape[0] > ranks:
        diag_ref[...] = jnp.zeros_like(diag_ref)

    def store(start, end, value):
        diag_ref[start:end, :] = refs[-2][start:end, :] + value if added else value

    diagonal(rows, spots, blocks_of(field_refs), factor_ref, store)


def columns_kernel(halve, masks, x_ref, bundle_ref, twin_ref, along_ref, short_ref):
    me = lax.axis_index("tile")
    chip, core = lax.div(me, 2), lax.rem(me, 2)
    near = bundle_ref.shape[0] + 1
    beside = chip + 2 * core - 1
    slot = 0
    for n, mask in enumerate(masks):
        slot = jnp.where((chip ^ beside) == mask, n, slot)
    far = bundle_ref[slot].astype(jnp.float32)
    far = jnp.where((beside >= 0) & (beside < near), far, 0.0)
    twin = twin_ref[0].astype(jnp.float32)
    low = jnp.where(core == 0, far, twin)
    high = jnp.where(core == 0, twin, far)
    own = 0.5 * x_ref[...] if halve else x_ref[...]
    along = stencil(low, own, high, COL_TAPS, 1)
    along_ref[...] = along
    short_ref[...] = along.astype(jnp.bfloat16)


def second_kernel(
    rows, cols, spots, factor_ref, diag_ref, fields_ref, short_ref, pay_ref, part_ref, total
):
    lines = cols * rows
    if total.shape[0] > factor_ref.shape[0] // rows:
        total[...] = jnp.zeros_like(total)

    def store(start, end, value):
        total[start:end, :] = diag_ref[start:end, :] + value

    diagonal(rows, spots, blocks_of([fields_ref]), factor_ref, store)
    pick = (
        lax.broadcasted_iota(jnp.int32, (cols, lines), 1) // rows
        == lax.broadcasted_iota(jnp.int32, (cols, lines), 0)
    ).astype(jnp.bfloat16)
    value = total[...]
    upper = value.astype(jnp.bfloat16)
    lower = (value - upper.astype(jnp.float32)).astype(jnp.bfloat16)
    both = lax.dot_general(
        pick,
        jnp.concatenate([upper, lower], axis=0),
        (((1,), (1,)), ((), ())),
        preferred_element_type=jnp.float32,
    )
    proj = both[:, : total.shape[0]] + both[:, total.shape[0] :]
    for at in range(0, total.shape[0], LANES):
        upper = proj[:, at : at + LANES].astype(jnp.bfloat16)
        lower = (proj[:, at : at + LANES] - upper.astype(jnp.float32)).astype(jnp.bfloat16)
        first = at // LANES * 2 * cols
        for ref in (pay_ref, part_ref):
            ref[first : first + cols, :] = upper
            ref[first + cols : first + 2 * cols, :] = lower

    head = total.shape[0] // LANES * 2 * cols
    pay_ref[head:, :] = short_ref[...]


def product(coef, spots, factor_ref, out_ref):
    starts = columns_of(spots)
    for n in range(0, len(starts), 2):
        pair = starts[n : n + 2]
        right = jnp.concatenate([factor_ref[:, pl.ds(start, LANES)] for start in pair], axis=1)
        term = jnp.dot(coef, right, preferred_element_type=jnp.float32)
        for m in range(len(pair)):
            out_ref[n + m] = term[:, m * LANES : (m + 1) * LANES].astype(out_ref.dtype)


def far_kernel(rows, cols, groups, ncells, spots, scale_ref, factor_ref, *refs):
    pay_refs, (coef_ref, out_ref) = refs[:groups], refs[groups:]
    ranks = factor_ref.shape[0] // rows
    lines = cols * rows
    span = LANES // rows

    spread = (
        lax.broadcasted_iota(jnp.int32, (LANES, LANES), 1) // rows
        == lax.broadcasted_iota(jnp.int32, (LANES, LANES), 0)
    ).astype(jnp.bfloat16)
    same = (
        lax.rem(lax.broadcasted_iota(jnp.int32, (lines, LANES), 1), rows)
        == lax.rem(lax.broadcasted_iota(jnp.int32, (lines, LANES), 0), rows)
    ).astype(jnp.float32)
    turned = []
    for at in range(0, ranks, LANES):
        count = min(LANES, ranks - at)
        first = at // LANES * 2 * cols
        both = pay_refs[0][first : first + 2 * cols, :].astype(jnp.float32)
        for ref in pay_refs[1:]:
            both = both + ref[first : first + 2 * cols, :].astype(jnp.float32)
        proj = both[:cols] + both[cols:]
        scale = scale_ref[:, at : at + count]
        weights = scale * scale / ncells
        if count < LANES:
            weights = jnp.concatenate([weights, jnp.zeros((1, LANES - count), jnp.float32)], axis=1)
        c = proj * weights
        turned += [c if n == 0 else pltpu.roll(c, LANES - n * span, 1) for n in range(rows)]
    stacked = jnp.concatenate(turned, axis=0).astype(jnp.bfloat16)
    wide = jnp.dot(stacked, spread, preferred_element_type=jnp.float32)
    for n in range(ranks * rows // LANES):
        piece = wide[n * cols : (n + 1) * cols, :]
        piece = jnp.broadcast_to(piece[:, None, :], (cols, rows, LANES)).reshape(lines, LANES)
        coef_ref[:, n * LANES : (n + 1) * LANES] = (piece * same).astype(jnp.bfloat16)
    product(coef_ref[...], spots, factor_ref, out_ref)


def term_kernel(wanted, after, coef_ref, factor_ref, *refs):
    for (spots, _), out_ref in zip(wanted, refs[after:]):
        product(coef_ref[...], spots, factor_ref, out_ref)


def pair_kernel(mine_ref, got_ref, *out_refs):
    at = 0
    for ref in out_refs:
        end = at + ref.shape[0]
        ref[...] = (mine_ref[at:end] + got_ref[at:end].astype(jnp.float32)).astype(ref.dtype)
        at = end


def local_kernel(rows, cols, halve, masks, b_ref, x_ref, amp_ref, along_ref, *refs):
    pay_refs, base_ref = refs[:-1], refs[-1]
    lines = cols * rows
    head = pay_refs[0].shape[0] - lines
    me = lax.axis_index("grp")
    low = jnp.zeros((lines, LANES), jnp.float32)
    high = low
    for mask, ref in zip(masks, pay_refs):
        part = ref[head:, :].astype(jnp.float32)
        low = jnp.where((me ^ mask) == me - 1, part, low)
        high = jnp.where((me ^ mask) == me + 1, part, high)
    low = low.reshape(cols, rows, LANES)
    high = high.reshape(cols, rows, LANES)
    own = along_ref[...].reshape(cols, rows, LANES)
    conv = stencil(low, own, high, ROW_TAPS, 1)
    x = 0.5 * x_ref[...] if halve else x_ref[...]
    scaled = (amp_ref[...][None] * conv).reshape(lines, LANES)
    base_ref[...] = b_ref[...] - (x + scaled)


def update_kernel(halve, last, x_ref, base_ref, *refs):
    part_refs, (new_ref, other_ref) = refs[:-2], refs[-2:]
    rank_sum = part_refs[0][0]
    for ref in part_refs[1:]:
        rank_sum = rank_sum + ref[0].astype(jnp.float32)
    x = 0.5 * x_ref[...] if halve else x_ref[...]
    residual = base_ref[...] - rank_sum
    new = x + 0.5 * residual
    new_ref[...] = new
    if last:
        other_ref[...] = residual
    else:
        other_ref[0] = new.astype(jnp.bfloat16)


def on_device(right_side, amplitude, factor, scale):
    cols, rows, width = right_side.shape
    ranks = factor.shape[0]
    tiles = lax.axis_size("tile")
    groups = lax.axis_size("grp")
    near = tiles // 2
    lines = cols * rows
    ncells_all = rows * width * groups * tiles
    blocks = -(-ranks // LANES)
    flat = factor.reshape(ranks * rows, tiles * width)
    b = right_side.reshape(lines, width)
    scale = scale.reshape(1, ranks)
    x = b
    short = (0.5 * b).astype(jnp.bfloat16)[None]
    pay_rows = blocks * 2 * cols + lines

    f32, bf16 = jnp.float32, jnp.bfloat16

    def shape(dtype, *dims):
        return jax.ShapeDtypeStruct(dims, dtype)

    def call(kernel, out_shape, flops=0, moved=1 << 18, **options):
        return pl.pallas_call(
            kernel,
            out_shape=out_shape,
            compiler_params=pltpu.CompilerParams(vmem_limit_bytes=32 * 1024 * 1024),
            cost_estimate=pl.CostEstimate(flops=flops, bytes_accessed=moved, transcendentals=0),
            **options,
        )

    work = lines * ranks * rows * tiles * width
    held = call(
        load_kernel,
        shape(bf16, *flat.shape),
        moved=4 * flat.size,
        in_specs=[pl.BlockSpec(memory_space=pltpu.HBM)],
        out_specs=pl.BlockSpec(memory_space=pltpu.VMEM),
        scratch_shapes=[pltpu.SemaphoreType.DMA((8,))],
        name="load",
    )(flat)
    half = near // 2
    close = list(range(half))

    def spots_of(masks, other):
        return [(mask, other != (mask > 0)) for mask in masks]

    def cross(value, mask):
        return swap(value, "tile", 2 * mask + 1)

    def first(fields, spots, *before):
        return call(
            partial(first_kernel, rows, spots, len(before)),
            shape(f32, blocks * LANES, lines),
            flops=work,
            moved=flat.size,
            name="project_own",
        )(held, *fields, *before)

    for step in range(ITERS):
        halve = step == 0
        last = step == ITERS - 1
        away = sorted(range(half, near), reverse=last)
        order = list(range(1, near))
        order.sort(key=lambda mask: (mask == half, mask))
        parts = [cross(short, mask) for mask in order]
        twin = swap(short, "tile", 1)
        diag = first([short], [(0, False)])
        bundle = call(
            join_kernel,
            shape(bf16, near - 1, lines, width),
            in_specs=[pl.BlockSpec(memory_space=pl.ANY)] * 2
            + [pl.BlockSpec(memory_space=pltpu.VMEM)] * (near - 1),
            name="join",
        )(diag, twin, *parts)
        across = swap(bundle, "tile", 1)
        known = spots_of(order, False) + [(0, True)]
        diag = first([bundle, twin], known, diag)
        spots = spots_of(order, True)
        along, along_short = call(
            partial(columns_kernel, halve, order),
            (shape(f32, lines, width), shape(bf16, lines, width)),
            name="columns",
        )(x, bundle, twin)
        pay, part = call(
            partial(second_kernel, rows, cols, spots),
            (shape(bf16, pay_rows, width), shape(bf16, pay_rows - lines, width)),
            flops=work,
            moved=flat.size,
            scratch_shapes=[pltpu.VMEM((blocks * LANES, lines), f32)],
            name="project_across",
        )(held, diag, across, along_short)
        pays = {
            mask: swap(part if mask & (mask + 1) else pay, "grp", mask)
            for mask in reversed(range(1, groups))
        }
        coef, far = call(
            partial(far_kernel, rows, cols, groups, ncells_all, spots_of(away, True)),
            (shape(bf16, lines, ranks * rows), shape(bf16, half, lines, width)),
            flops=work // 2,
            moved=flat.size,
            name="term_first",
        )(scale, held, part, *pays.values())
        got = swap(far, "tile", 1)

        def term(*wanted, after=()):
            return call(
                partial(term_kernel, wanted, len(after)),
                in_specs=[pl.BlockSpec(memory_space=pltpu.VMEM)] * 2
                + [pl.BlockSpec(memory_space=pl.ANY)] * len(after),
                out_shape=[shape(dtype, len(spots), lines, width) for spots, dtype in wanted],
                flops=work // 2 * len(wanted),
                moved=flat.size,
                name="term",
            )(coef, held, *after)

        def pair(mine, got, masks):
            return call(
                pair_kernel,
                [shape(bf16 if mask else f32, 1, lines, width) for mask in masks],
                name="pair",
            )(mine, got)

        mine, far = term((spots_of(away, False), f32), (spots_of(close, True), bf16))
        sends = pair(mine, got, away)
        terms = [cross(send, mask) for send, mask in zip(sends, away)]
        got = swap(far, "tile", 1)
        (mine,) = term((spots_of(close, False), f32), after=sends)
        kept, *sends = pair(mine, got, close)
        terms += [cross(send, mask) for send, mask in zip(sends, close[1:])]
        rims = [mask for mask in pays if not mask & (mask + 1)]
        base = call(
            partial(local_kernel, rows, cols, halve, rims), shape(f32, lines, width), name="local"
        )(b, x, amplitude, along, *[pays[mask] for mask in rims])
        x, short = call(
            partial(update_kernel, halve, last),
            (
                shape(f32, lines, width),
                shape(f32, lines, width) if last else shape(bf16, 1, lines, width),
            ),
            name="update",
        )(x, base, kept, *terms)
    return x.reshape(cols, rows, width), short.reshape(cols, rows, width)


def solution(mesh):
    in_specs = (P(None, "grp", "tile"), P("grp", "tile"), P("tile", "grp", None), P("tile"))
    out_specs = (P(None, "grp", "tile"), P(None, "grp", "tile"))
    return jax.shard_map(
        on_device, mesh=mesh, in_specs=in_specs, out_specs=out_specs, check_vma=False
    )
```

```python
import math
from functools import partial

import jax
import jax.numpy as jnp
import numpy as np
from jax import lax
from jax.experimental import pallas as pl
from jax.experimental.pallas import tpu as pltpu
from jax.sharding import PartitionSpec as P

REACH = 8
ITERS = 2
LANES = 128


def taper(sigma):
    offsets = np.arange(-REACH, REACH + 1).astype(np.float64)
    values = np.exp(-offsets * offsets / (2.0 * sigma * sigma))
    values = values * np.cos(np.pi * offsets / (2.0 * REACH + 2.0)) ** 2
    return [float(v) for v in (values / values.sum()).astype(np.float32)]


ROW_TAPS = taper(3.0)
COL_TAPS = taper(5.0)


def stencil(low, own, high, taps, axis):
    size = own.shape[axis]
    place = lax.broadcasted_iota(jnp.int32, own.shape, axis)
    total = taps[REACH] * own
    for shift in range(1, REACH + 1):
        after = pltpu.roll(jnp.where(place < shift, high, own), size - shift, axis)
        before = pltpu.roll(jnp.where(place >= size - shift, low, own), shift, axis)
        total = total + taps[REACH + shift] * after + taps[REACH - shift] * before
    return total


def swap(value, axis, mask):
    return lax.ppermute(value, axis, [(i, i ^ mask) for i in range(lax.axis_size(axis))])


def place_of(spot):
    mask, other = spot
    me = lax.axis_index("tile")
    core = lax.rem(me, 2)
    return 2 * (lax.div(me, 2) ^ mask) + (1 - core if other else core)


def columns_of(spots):
    return [pl.multiple_of(place_of(spot) * LANES, LANES) for spot in spots]


def join_kernel(*refs):
    part_refs, out_ref = refs[2:-1], refs[-1]
    at = 0
    for ref in part_refs:
        out_ref[at : at + ref.shape[0]] = ref[...]
        at += ref.shape[0]


def load_kernel(source_ref, out_ref, sems):
    chunks = sems.shape[0]
    count = source_ref.shape[0] // chunks
    copies = [
        pltpu.make_async_copy(
            source_ref.at[pl.ds(n * count, count)], out_ref.at[pl.ds(n * count, count)], sems.at[n]
        )
        for n in range(chunks)
    ]
    for copy in copies:
        copy.start()
    for copy in copies:
        copy.wait()


def diagonal(rows, spots, fields, factor_ref, store):
    lines = fields[0].shape[0]
    count = factor_ref.shape[0]
    field = jnp.concatenate(fields, axis=1)
    step = min(2048, count)
    row_of = lax.broadcasted_iota(jnp.int32, (rows, lines), 0)
    lane_of = lax.broadcasted_iota(jnp.int32, (rows, lines), 1)
    same = (lax.rem(lane_of, rows) == row_of).astype(jnp.float32)
    starts = columns_of(spots)
    for at in range(0, count, step):
        left = jnp.concatenate(
            [factor_ref[at : at + step, pl.ds(start, LANES)] for start in starts], axis=1
        )
        part = lax.dot_general(
            left, field, (((1,), (1,)), ((), ())), preferred_element_type=jnp.float32
        )
        part = part.reshape(step // rows, rows, lines) * same[None]
        store(at // rows, (at + step) // rows, jnp.sum(part, axis=1))


def blocks_of(refs):
    return [ref[n] for ref in refs for n in range(ref.shape[0])]


def first_kernel(rows, spots, added, factor_ref, *refs):
    diag_ref = refs[-1]
    field_refs = refs[: len(refs) - 1 - added]
    ranks = factor_ref.shape[0] // rows
    if diag_ref.shape[0] > ranks:
        diag_ref[...] = jnp.zeros_like(diag_ref)

    def store(start, end, value):
        diag_ref[start:end, :] = refs[-2][start:end, :] + value if added else value

    diagonal(rows, spots, blocks_of(field_refs), factor_ref, store)


def columns_kernel(halve, masks, x_ref, bundle_ref, twin_ref, along_ref, short_ref):
    me = lax.axis_index("tile")
    chip, core = lax.div(me, 2), lax.rem(me, 2)
    near = bundle_ref.shape[0] + 1
    beside = chip + 2 * core - 1
    slot = 0
    for n, mask in enumerate(masks):
        slot = jnp.where((chip ^ beside) == mask, n, slot)
    far = bundle_ref[slot].astype(jnp.float32)
    far = jnp.where((beside >= 0) & (beside < near), far, 0.0)
    twin = twin_ref[0].astype(jnp.float32)
    low = jnp.where(core == 0, far, twin)
    high = jnp.where(core == 0, twin, far)
    own = 0.5 * x_ref[...] if halve else x_ref[...]
    along = stencil(low, own, high, COL_TAPS, 1)
    along_ref[...] = along
    short_ref[...] = along.astype(jnp.bfloat16)


def second_kernel(
    rows, cols, spots, factor_ref, diag_ref, fields_ref, short_ref, pay_ref, part_ref, total
):
    lines = cols * rows
    if total.shape[0] > factor_ref.shape[0] // rows:
        total[...] = jnp.zeros_like(total)

    def store(start, end, value):
        total[start:end, :] = diag_ref[start:end, :] + value

    diagonal(rows, spots, blocks_of([fields_ref]), factor_ref, store)
    pick = (
        lax.broadcasted_iota(jnp.int32, (cols, lines), 1) // rows
        == lax.broadcasted_iota(jnp.int32, (cols, lines), 0)
    ).astype(jnp.bfloat16)
    for at in range(0, total.shape[0], LANES):
        part = total[at : at + LANES, :]
        upper = part.astype(jnp.bfloat16)
        lower = (part - upper.astype(jnp.float32)).astype(jnp.bfloat16)
        dims = (((1,), (1,)), ((), ()))
        proj = lax.dot_general(pick, upper, dims, preferred_element_type=jnp.float32)
        proj = proj + lax.dot_general(pick, lower, dims, preferred_element_type=jnp.float32)
        first = at // LANES * 2 * cols
        upper = proj.astype(jnp.bfloat16)
        lower = (proj - upper.astype(jnp.float32)).astype(jnp.bfloat16)
        for ref in (pay_ref, part_ref):
            ref[first : first + cols, :] = upper
            ref[first + cols : first + 2 * cols, :] = lower

    head = total.shape[0] // LANES * 2 * cols
    pay_ref[head:, :] = short_ref[...]


def product(coef, spots, factor_ref, out_ref):
    starts = columns_of(spots)
    for n in range(0, len(starts), 2):
        pair = starts[n : n + 2]
        right = jnp.concatenate([factor_ref[:, pl.ds(start, LANES)] for start in pair], axis=1)
        term = jnp.dot(coef, right, preferred_element_type=jnp.float32)
        for m in range(len(pair)):
            out_ref[n + m] = term[:, m * LANES : (m + 1) * LANES].astype(out_ref.dtype)


def far_kernel(rows, cols, groups, ncells, spots, scale_ref, factor_ref, *refs):
    pay_refs, (coef_ref, out_ref) = refs[:groups], refs[groups:]
    ranks = factor_ref.shape[0] // rows
    lines = cols * rows
    span = LANES // rows

    spread = (
        lax.broadcasted_iota(jnp.int32, (LANES, LANES), 1) // rows
        == lax.broadcasted_iota(jnp.int32, (LANES, LANES), 0)
    ).astype(jnp.bfloat16)
    same = (
        lax.rem(lax.broadcasted_iota(jnp.int32, (lines, LANES), 1), rows)
        == lax.rem(lax.broadcasted_iota(jnp.int32, (lines, LANES), 0), rows)
    ).astype(jnp.float32)
    for at in range(0, ranks, LANES):
        count = min(LANES, ranks - at)
        first = at // LANES * 2 * cols
        both = pay_refs[0][first : first + 2 * cols, :].astype(jnp.float32)
        for ref in pay_refs[1:]:
            both = both + ref[first : first + 2 * cols, :].astype(jnp.float32)
        proj = both[:cols] + both[cols:]
        scale = scale_ref[:, at : at + count]
        weights = scale * scale / ncells
        if count < LANES:
            weights = jnp.concatenate([weights, jnp.zeros((1, LANES - count), jnp.float32)], axis=1)
        c = proj * weights
        turned = [c if n == 0 else pltpu.roll(c, LANES - n * span, 1) for n in range(rows)]
        stacked = jnp.concatenate(turned, axis=0).astype(jnp.bfloat16)
        wide = jnp.dot(stacked, spread, preferred_element_type=jnp.float32)
        for n in range(rows):
            start = (at + n * span) * rows
            if start >= ranks * rows:
                break
            piece = wide[n * cols : (n + 1) * cols, :]
            piece = jnp.broadcast_to(piece[:, None, :], (cols, rows, LANES)).reshape(lines, LANES)
            coef_ref[:, start : start + LANES] = (piece * same).astype(jnp.bfloat16)
    product(coef_ref[...], spots, factor_ref, out_ref)


def term_kernel(wanted, after, coef_ref, factor_ref, *refs):
    for (spots, _), out_ref in zip(wanted, refs[after:]):
        product(coef_ref[...], spots, factor_ref, out_ref)


def pair_kernel(mine_ref, got_ref, *out_refs):
    at = 0
    for ref in out_refs:
        end = at + ref.shape[0]
        ref[...] = (mine_ref[at:end] + got_ref[at:end].astype(jnp.float32)).astype(ref.dtype)
        at = end


def local_kernel(rows, cols, halve, b_ref, x_ref, amp_ref, along_ref, *refs):
    pay_refs, base_ref = refs[:-1], refs[-1]
    lines = cols * rows
    head = pay_refs[0].shape[0] - lines
    me = lax.axis_index("grp")
    low = jnp.zeros((lines, LANES), jnp.float32)
    high = low
    for n, ref in enumerate(pay_refs, 1):
        mask = (1 << n) - 1
        part = ref[head:, :].astype(jnp.float32)
        low = jnp.where((me ^ mask) == me - 1, part, low)
        high = jnp.where((me ^ mask) == me + 1, part, high)
    low = low.reshape(cols, rows, LANES)
    high = high.reshape(cols, rows, LANES)
    own = along_ref[...].reshape(cols, rows, LANES)
    conv = stencil(low, own, high, ROW_TAPS, 1)
    x = 0.5 * x_ref[...] if halve else x_ref[...]
    scaled = (amp_ref[...][None] * conv).reshape(lines, LANES)
    base_ref[...] = b_ref[...] - (x + scaled)


def update_kernel(halve, last, x_ref, base_ref, *refs):
    part_refs, (new_ref, other_ref) = refs[:-2], refs[-2:]
    rank_sum = part_refs[0][0]
    for ref in part_refs[1:]:
        rank_sum = rank_sum + ref[0].astype(jnp.float32)
    x = 0.5 * x_ref[...] if halve else x_ref[...]
    residual = base_ref[...] - rank_sum
    new = x + 0.5 * residual
    new_ref[...] = new
    if last:
        other_ref[...] = residual
    else:
        other_ref[0] = new.astype(jnp.bfloat16)


def on_device(right_side, amplitude, factor, scale):
    cols, rows, width = right_side.shape
    ranks = factor.shape[0]
    tiles = lax.axis_size("tile")
    groups = lax.axis_size("grp")
    near = tiles // 2
    lines = cols * rows
    ncells_all = rows * width * groups * tiles
    blocks = -(-ranks // LANES)
    flat = factor.reshape(ranks * rows, tiles * width)
    b = right_side.reshape(lines, width)
    scale = scale.reshape(1, ranks)
    x = b
    short = (0.5 * b).astype(jnp.bfloat16)[None]
    pay_rows = blocks * 2 * cols + lines

    f32, bf16 = jnp.float32, jnp.bfloat16

    def shape(dtype, *dims):
        return jax.ShapeDtypeStruct(dims, dtype)

    def call(kernel, out_shape, flops=0, moved=1 << 18, **options):
        return pl.pallas_call(
            kernel,
            out_shape=out_shape,
            compiler_params=pltpu.CompilerParams(vmem_limit_bytes=32 * 1024 * 1024),
            cost_estimate=pl.CostEstimate(flops=flops, bytes_accessed=moved, transcendentals=0),
            **options,
        )

    work = lines * ranks * rows * tiles * width
    held = call(
        load_kernel,
        shape(bf16, *flat.shape),
        moved=4 * flat.size,
        in_specs=[pl.BlockSpec(memory_space=pltpu.HBM)],
        out_specs=pl.BlockSpec(memory_space=pltpu.VMEM),
        scratch_shapes=[pltpu.SemaphoreType.DMA((8,))],
        name="load",
    )(flat)
    half = near // 2
    close = list(range(half))

    def spots_of(masks, other):
        return [(mask, other != (mask > 0)) for mask in masks]

    def cross(value, mask):
        return swap(value, "tile", 2 * mask + 1)

    def first(fields, spots, *before):
        return call(
            partial(first_kernel, rows, spots, len(before)),
            shape(f32, blocks * LANES, lines),
            flops=work,
            moved=flat.size,
            name="project_own",
        )(held, *fields, *before)

    for step in range(ITERS):
        halve = step == 0
        last = step == ITERS - 1
        away = sorted(range(half, near), reverse=last)
        order = list(range(1, near))
        if step == 0:
            order.sort(key=lambda mask: (mask == half, mask))
        parts = [cross(short, mask) for mask in order]
        twin = swap(short, "tile", 1)
        diag = first([short], [(0, False)])
        bundle = call(
            join_kernel,
            shape(bf16, near - 1, lines, width),
            in_specs=[pl.BlockSpec(memory_space=pl.ANY)] * 2
            + [pl.BlockSpec(memory_space=pltpu.VMEM)] * (near - 1),
            name="join",
        )(diag, twin, *parts)
        across = swap(bundle, "tile", 1)
        known = spots_of(order, False) + [(0, True)]
        diag = first([bundle, twin], known, diag)
        spots = spots_of(order, True)
        along, along_short = call(
            partial(columns_kernel, halve, order),
            (shape(f32, lines, width), shape(bf16, lines, width)),
            name="columns",
        )(x, bundle, twin)
        pay, part = call(
            partial(second_kernel, rows, cols, spots),
            (shape(bf16, pay_rows, width), shape(bf16, pay_rows - lines, width)),
            flops=work,
            moved=flat.size,
            scratch_shapes=[pltpu.VMEM((blocks * LANES, lines), f32)],
            name="project_across",
        )(held, diag, across, along_short)
        pays = [swap(part if mask & (mask + 1) else pay, "grp", mask) for mask in range(1, groups)]
        coef, far = call(
            partial(far_kernel, rows, cols, groups, ncells_all, spots_of(away, True)),
            (shape(bf16, lines, ranks * rows), shape(bf16, half, lines, width)),
            flops=work // 2,
            moved=flat.size,
            name="term_first",
        )(scale, held, part, *pays)
        got = swap(far, "tile", 1)

        def term(*wanted, after=()):
            return call(
                partial(term_kernel, wanted, len(after)),
                in_specs=[pl.BlockSpec(memory_space=pltpu.VMEM)] * 2
                + [pl.BlockSpec(memory_space=pl.ANY)] * len(after),
                out_shape=[shape(dtype, len(spots), lines, width) for spots, dtype in wanted],
                flops=work // 2 * len(wanted),
                moved=flat.size,
                name="term",
            )(coef, held, *after)

        def pair(mine, got, masks):
            return call(
                pair_kernel,
                [shape(bf16 if mask else f32, 1, lines, width) for mask in masks],
                name="pair",
            )(mine, got)

        mine, far = term((spots_of(away, False), f32), (spots_of(close, True), bf16))
        sends = pair(mine, got, away)
        terms = [cross(send, mask) for send, mask in zip(sends, away)]
        got = swap(far, "tile", 1)
        (mine,) = term((spots_of(close, False), f32), after=sends)
        kept, *sends = pair(mine, got, close)
        terms += [cross(send, mask) for send, mask in zip(sends, close[1:])]
        rims = [pay for mask, pay in enumerate(pays, 1) if not mask & (mask + 1)]
        base = call(
            partial(local_kernel, rows, cols, halve), shape(f32, lines, width), name="local"
        )(b, x, amplitude, along, *rims)
        x, short = call(
            partial(update_kernel, halve, last),
            (
                shape(f32, lines, width),
                shape(f32, lines, width) if last else shape(bf16, 1, lines, width),
            ),
            name="update",
        )(x, base, kept, *terms)
    return x.reshape(cols, rows, width), short.reshape(cols, rows, width)


def solution(mesh):
    in_specs = (P(None, "grp", "tile"), P("grp", "tile"), P("tile", "grp", None), P("tile"))
    out_specs = (P(None, "grp", "tile"), P(None, "grp", "tile"))
    return jax.shard_map(
        on_device, mesh=mesh, in_specs=in_specs, out_specs=out_specs, check_vma=False
    )
```

```python
import math
from functools import partial

import jax
import jax.numpy as jnp
import numpy as np
from jax import lax
from jax.experimental import pallas as pl
from jax.experimental.pallas import tpu as pltpu
from jax.sharding import PartitionSpec as P

REACH = 8
ITERS = 2
LANES = 128


def taper(sigma):
    offsets = np.arange(-REACH, REACH + 1).astype(np.float64)
    values = np.exp(-offsets * offsets / (2.0 * sigma * sigma))
    values = values * np.cos(np.pi * offsets / (2.0 * REACH + 2.0)) ** 2
    return [float(v) for v in (values / values.sum()).astype(np.float32)]


ROW_TAPS = taper(3.0)
COL_TAPS = taper(5.0)


def stencil(low, own, high, taps, axis):
    size = own.shape[axis]
    place = lax.broadcasted_iota(jnp.int32, own.shape, axis)
    total = taps[REACH] * own
    for shift in range(1, REACH + 1):
        after = pltpu.roll(jnp.where(place < shift, high, own), size - shift, axis)
        before = pltpu.roll(jnp.where(place >= size - shift, low, own), shift, axis)
        total = total + taps[REACH + shift] * after + taps[REACH - shift] * before
    return total


def swap(value, axis, mask):
    return lax.ppermute(value, axis, [(i, i ^ mask) for i in range(lax.axis_size(axis))])


def place_of(spot):
    mask, other = spot
    me = lax.axis_index("tile")
    core = lax.rem(me, 2)
    return 2 * (lax.div(me, 2) ^ mask) + (1 - core if other else core)


def columns_of(spots):
    return [pl.multiple_of(place_of(spot) * LANES, LANES) for spot in spots]


def join_kernel(*refs):
    part_refs, out_ref = refs[2:-1], refs[-1]
    at = 0
    for ref in part_refs:
        out_ref[at : at + ref.shape[0]] = ref[...]
        at += ref.shape[0]


def load_kernel(source_ref, out_ref, sems):
    chunks = sems.shape[0]
    count = source_ref.shape[0] // chunks
    copies = [
        pltpu.make_async_copy(
            source_ref.at[pl.ds(n * count, count)], out_ref.at[pl.ds(n * count, count)], sems.at[n]
        )
        for n in range(chunks)
    ]
    for copy in copies:
        copy.start()
    for copy in copies:
        copy.wait()


def diagonal(rows, spots, fields, factor_ref, store):
    lines = fields[0].shape[0]
    count = factor_ref.shape[0]
    field = jnp.concatenate(fields, axis=1)
    step = min(2048, count)
    row_of = lax.broadcasted_iota(jnp.int32, (rows, lines), 0)
    lane_of = lax.broadcasted_iota(jnp.int32, (rows, lines), 1)
    same = (lax.rem(lane_of, rows) == row_of).astype(jnp.float32)
    starts = columns_of(spots)
    for at in range(0, count, step):
        left = jnp.concatenate(
            [factor_ref[at : at + step, pl.ds(start, LANES)] for start in starts], axis=1
        )
        part = lax.dot_general(
            left, field, (((1,), (1,)), ((), ())), preferred_element_type=jnp.float32
        )
        part = part.reshape(step // rows, rows, lines) * same[None]
        store(at // rows, (at + step) // rows, jnp.sum(part, axis=1))


def blocks_of(refs):
    return [ref[n] for ref in refs for n in range(ref.shape[0])]


def first_kernel(rows, spots, added, factor_ref, *refs):
    diag_ref = refs[-1]
    field_refs = refs[: len(refs) - 1 - added]
    ranks = factor_ref.shape[0] // rows
    if diag_ref.shape[0] > ranks:
        diag_ref[...] = jnp.zeros_like(diag_ref)

    def store(start, end, value):
        diag_ref[start:end, :] = refs[-2][start:end, :] + value if added else value

    diagonal(rows, spots, blocks_of(field_refs), factor_ref, store)


def columns_kernel(halve, masks, x_ref, bundle_ref, twin_ref, along_ref, short_ref):
    me = lax.axis_index("tile")
    chip, core = lax.div(me, 2), lax.rem(me, 2)
    near = bundle_ref.shape[0] + 1
    beside = chip + 2 * core - 1
    slot = 0
    for n, mask in enumerate(masks):
        slot = jnp.where((chip ^ beside) == mask, n, slot)
    far = bundle_ref[slot].astype(jnp.float32)
    far = jnp.where((beside >= 0) & (beside < near), far, 0.0)
    twin = twin_ref[0].astype(jnp.float32)
    low = jnp.where(core == 0, far, twin)
    high = jnp.where(core == 0, twin, far)
    own = 0.5 * x_ref[...] if halve else x_ref[...]
    along = stencil(low, own, high, COL_TAPS, 1)
    along_ref[...] = along
    short_ref[...] = along.astype(jnp.bfloat16)


def second_kernel(
    rows, cols, spots, factor_ref, diag_ref, fields_ref, short_ref, pay_ref, part_ref, total
):
    lines = cols * rows
    if total.shape[0] > factor_ref.shape[0] // rows:
        total[...] = jnp.zeros_like(total)

    def store(start, end, value):
        total[start:end, :] = diag_ref[start:end, :] + value

    diagonal(rows, spots, blocks_of([fields_ref]), factor_ref, store)
    pick = (
        lax.broadcasted_iota(jnp.int32, (cols, lines), 1) // rows
        == lax.broadcasted_iota(jnp.int32, (cols, lines), 0)
    ).astype(jnp.bfloat16)
    for at in range(0, total.shape[0], LANES):
        part = total[at : at + LANES, :]
        upper = part.astype(jnp.bfloat16)
        lower = (part - upper.astype(jnp.float32)).astype(jnp.bfloat16)
        dims = (((1,), (1,)), ((), ()))
        proj = lax.dot_general(pick, upper, dims, preferred_element_type=jnp.float32)
        proj = proj + lax.dot_general(pick, lower, dims, preferred_element_type=jnp.float32)
        first = at // LANES * 2 * cols
        upper = proj.astype(jnp.bfloat16)
        lower = (proj - upper.astype(jnp.float32)).astype(jnp.bfloat16)
        for ref in (pay_ref, part_ref):
            ref[first : first + cols, :] = upper
            ref[first + cols : first + 2 * cols, :] = lower

    head = total.shape[0] // LANES * 2 * cols
    pay_ref[head:, :] = short_ref[...]


def product(coef, spots, factor_ref, out_ref):
    starts = columns_of(spots)
    for n in range(0, len(starts), 2):
        pair = starts[n : n + 2]
        right = jnp.concatenate([factor_ref[:, pl.ds(start, LANES)] for start in pair], axis=1)
        term = jnp.dot(coef, right, preferred_element_type=jnp.float32)
        for m in range(len(pair)):
            out_ref[n + m] = term[:, m * LANES : (m + 1) * LANES].astype(out_ref.dtype)


def far_kernel(rows, cols, groups, ncells, spots, scale_ref, factor_ref, *refs):
    pay_refs, (coef_ref, out_ref) = refs[:groups], refs[groups:]
    ranks = factor_ref.shape[0] // rows
    lines = cols * rows
    span = LANES // rows

    spread = (
        lax.broadcasted_iota(jnp.int32, (LANES, LANES), 1) // rows
        == lax.broadcasted_iota(jnp.int32, (LANES, LANES), 0)
    ).astype(jnp.bfloat16)
    same = (
        lax.rem(lax.broadcasted_iota(jnp.int32, (lines, LANES), 1), rows)
        == lax.rem(lax.broadcasted_iota(jnp.int32, (lines, LANES), 0), rows)
    ).astype(jnp.float32)
    for at in range(0, ranks, LANES):
        count = min(LANES, ranks - at)
        first = at // LANES * 2 * cols
        both = pay_refs[0][first : first + 2 * cols, :].astype(jnp.float32)
        for ref in pay_refs[1:]:
            both = both + ref[first : first + 2 * cols, :].astype(jnp.float32)
        proj = both[:cols] + both[cols:]
        scale = scale_ref[:, at : at + count]
        weights = scale * scale / ncells
        if count < LANES:
            weights = jnp.concatenate([weights, jnp.zeros((1, LANES - count), jnp.float32)], axis=1)
        c = proj * weights
        turned = [c if n == 0 else pltpu.roll(c, LANES - n * span, 1) for n in range(rows)]
        stacked = jnp.concatenate(turned, axis=0).astype(jnp.bfloat16)
        wide = jnp.dot(stacked, spread, preferred_element_type=jnp.float32)
        for n in range(rows):
            start = (at + n * span) * rows
            if start >= ranks * rows:
                break
            piece = wide[n * cols : (n + 1) * cols, :]
            piece = jnp.broadcast_to(piece[:, None, :], (cols, rows, LANES)).reshape(lines, LANES)
            coef_ref[:, start : start + LANES] = (piece * same).astype(jnp.bfloat16)
    product(coef_ref[...], spots, factor_ref, out_ref)


def term_kernel(wanted, after, coef_ref, factor_ref, *refs):
    for (spots, _), out_ref in zip(wanted, refs[after:]):
        product(coef_ref[...], spots, factor_ref, out_ref)


def pair_kernel(mine_ref, got_ref, *out_refs):
    at = 0
    for ref in out_refs:
        end = at + ref.shape[0]
        ref[...] = (mine_ref[at:end] + got_ref[at:end].astype(jnp.float32)).astype(ref.dtype)
        at = end


def local_kernel(rows, cols, halve, b_ref, x_ref, amp_ref, along_ref, *refs):
    pay_refs, base_ref = refs[:-1], refs[-1]
    lines = cols * rows
    head = pay_refs[0].shape[0] - lines
    me = lax.axis_index("grp")
    low = jnp.zeros((lines, LANES), jnp.float32)
    high = low
    for n, ref in enumerate(pay_refs, 1):
        mask = (1 << n) - 1
        part = ref[head:, :].astype(jnp.float32)
        low = jnp.where((me ^ mask) == me - 1, part, low)
        high = jnp.where((me ^ mask) == me + 1, part, high)
    low = low.reshape(cols, rows, LANES)
    high = high.reshape(cols, rows, LANES)
    own = along_ref[...].reshape(cols, rows, LANES)
    conv = stencil(low, own, high, ROW_TAPS, 1)
    x = 0.5 * x_ref[...] if halve else x_ref[...]
    scaled = (amp_ref[...][None] * conv).reshape(lines, LANES)
    base_ref[...] = b_ref[...] - (x + scaled)


def update_kernel(halve, last, x_ref, base_ref, *refs):
    part_refs, (new_ref, other_ref) = refs[:-2], refs[-2:]
    rank_sum = part_refs[0][0]
    for ref in part_refs[1:]:
        rank_sum = rank_sum + ref[0].astype(jnp.float32)
    x = 0.5 * x_ref[...] if halve else x_ref[...]
    residual = base_ref[...] - rank_sum
    new = x + 0.5 * residual
    new_ref[...] = new
    if last:
        other_ref[...] = residual
    else:
        other_ref[0] = new.astype(jnp.bfloat16)


def on_device(right_side, amplitude, factor, scale):
    cols, rows, width = right_side.shape
    ranks = factor.shape[0]
    tiles = lax.axis_size("tile")
    groups = lax.axis_size("grp")
    near = tiles // 2
    lines = cols * rows
    ncells_all = rows * width * groups * tiles
    blocks = -(-ranks // LANES)
    flat = factor.reshape(ranks * rows, tiles * width)
    b = right_side.reshape(lines, width)
    scale = scale.reshape(1, ranks)
    x = b
    short = (0.5 * b).astype(jnp.bfloat16)[None]
    pay_rows = blocks * 2 * cols + lines

    f32, bf16 = jnp.float32, jnp.bfloat16

    def shape(dtype, *dims):
        return jax.ShapeDtypeStruct(dims, dtype)

    def call(kernel, out_shape, flops=0, moved=1 << 18, **options):
        return pl.pallas_call(
            kernel,
            out_shape=out_shape,
            compiler_params=pltpu.CompilerParams(vmem_limit_bytes=32 * 1024 * 1024),
            cost_estimate=pl.CostEstimate(flops=flops, bytes_accessed=moved, transcendentals=0),
            **options,
        )

    work = lines * ranks * rows * tiles * width
    held = call(
        load_kernel,
        shape(bf16, *flat.shape),
        moved=4 * flat.size,
        in_specs=[pl.BlockSpec(memory_space=pltpu.HBM)],
        out_specs=pl.BlockSpec(memory_space=pltpu.VMEM),
        scratch_shapes=[pltpu.SemaphoreType.DMA((8,))],
        name="load",
    )(flat)
    half = near // 2

    def spots_of(masks, other):
        return [(mask, other != (mask > 0)) for mask in masks]

    def cross(value, mask):
        return swap(value, "tile", 2 * mask + 1)

    def first(fields, spots, *before):
        return call(
            partial(first_kernel, rows, spots, len(before)),
            shape(f32, blocks * LANES, lines),
            flops=work,
            moved=flat.size,
            name="project_own",
        )(held, *fields, *before)

    for step in range(ITERS):
        halve = step == 0
        last = step == ITERS - 1
        close = list(range(half if last else 1))
        away = sorted(range(half, near), reverse=last) + list(range(len(close), half))
        order = list(range(1, near))
        order.sort(key=lambda mask: (mask == half, mask))
        parts = [cross(short, mask) for mask in order]
        twin = swap(short, "tile", 1)
        diag = first([short], [(0, False)])
        bundle = call(
            join_kernel,
            shape(bf16, near - 1, lines, width),
            in_specs=[pl.BlockSpec(memory_space=pl.ANY)] * 2
            + [pl.BlockSpec(memory_space=pltpu.VMEM)] * (near - 1),
            name="join",
        )(diag, twin, *parts)
        across = swap(bundle, "tile", 1)
        known = spots_of(order, False) + [(0, True)]
        diag = first([bundle, twin], known, diag)
        spots = spots_of(order, True)
        along, along_short = call(
            partial(columns_kernel, halve, order),
            (shape(f32, lines, width), shape(bf16, lines, width)),
            name="columns",
        )(x, bundle, twin)
        pay, part = call(
            partial(second_kernel, rows, cols, spots),
            (shape(bf16, pay_rows, width), shape(bf16, pay_rows - lines, width)),
            flops=work,
            moved=flat.size,
            scratch_shapes=[pltpu.VMEM((blocks * LANES, lines), f32)],
            name="project_across",
        )(held, diag, across, along_short)
        pays = [swap(part if mask & (mask + 1) else pay, "grp", mask) for mask in range(1, groups)]
        coef, far = call(
            partial(far_kernel, rows, cols, groups, ncells_all, spots_of(away, True)),
            (shape(bf16, lines, ranks * rows), shape(bf16, len(away), lines, width)),
            flops=work // 2,
            moved=flat.size,
            name="term_first",
        )(scale, held, part, *pays)
        got = swap(far, "tile", 1)

        def term(*wanted, after=()):
            return call(
                partial(term_kernel, wanted, len(after)),
                in_specs=[pl.BlockSpec(memory_space=pltpu.VMEM)] * 2
                + [pl.BlockSpec(memory_space=pl.ANY)] * len(after),
                out_shape=[shape(dtype, len(spots), lines, width) for spots, dtype in wanted],
                flops=work // 2 * len(wanted),
                moved=flat.size,
                name="term",
            )(coef, held, *after)

        def pair(mine, got, masks):
            return call(
                pair_kernel,
                [shape(bf16 if mask else f32, 1, lines, width) for mask in masks],
                name="pair",
            )(mine, got)

        mine, far = term((spots_of(away, False), f32), (spots_of(close, True), bf16))
        sends = pair(mine, got, away)
        terms = [cross(send, mask) for send, mask in zip(sends, away)]
        got = swap(far, "tile", 1)
        (mine,) = term((spots_of(close, False), f32), after=sends)
        kept, *sends = pair(mine, got, close)
        terms += [cross(send, mask) for send, mask in zip(sends, close[1:])]
        rims = [pay for mask, pay in enumerate(pays, 1) if not mask & (mask + 1)]
        base = call(
            partial(local_kernel, rows, cols, halve), shape(f32, lines, width), name="local"
        )(b, x, amplitude, along, *rims)
        x, short = call(
            partial(update_kernel, halve, last),
            (
                shape(f32, lines, width),
                shape(f32, lines, width) if last else shape(bf16, 1, lines, width),
            ),
            name="update",
        )(x, base, kept, *terms)
    return x.reshape(cols, rows, width), short.reshape(cols, rows, width)


def solution(mesh):
    in_specs = (P(None, "grp", "tile"), P("grp", "tile"), P("tile", "grp", None), P("tile"))
    out_specs = (P(None, "grp", "tile"), P(None, "grp", "tile"))
    return jax.shard_map(
        on_device, mesh=mesh, in_specs=in_specs, out_specs=out_specs, check_vma=False
    )
```

```python
import math
from functools import partial

import jax
import jax.numpy as jnp
import numpy as np
from jax import lax
from jax.experimental import pallas as pl
from jax.experimental.pallas import tpu as pltpu
from jax.sharding import PartitionSpec as P

REACH = 8
ITERS = 2
LANES = 128


def taper(sigma):
    offsets = np.arange(-REACH, REACH + 1).astype(np.float64)
    values = np.exp(-offsets * offsets / (2.0 * sigma * sigma))
    values = values * np.cos(np.pi * offsets / (2.0 * REACH + 2.0)) ** 2
    return [float(v) for v in (values / values.sum()).astype(np.float32)]


ROW_TAPS = taper(3.0)
COL_TAPS = taper(5.0)


def stencil(low, own, high, taps, axis):
    size = own.shape[axis]
    place = lax.broadcasted_iota(jnp.int32, own.shape, axis)
    total = taps[REACH] * own
    for shift in range(1, REACH + 1):
        after = pltpu.roll(jnp.where(place < shift, high, own), size - shift, axis)
        before = pltpu.roll(jnp.where(place >= size - shift, low, own), shift, axis)
        total = total + taps[REACH + shift] * after + taps[REACH - shift] * before
    return total


def swap(value, axis, mask):
    return lax.ppermute(value, axis, [(i, i ^ mask) for i in range(lax.axis_size(axis))])


def place_of(spot):
    mask, other = spot
    me = lax.axis_index("tile")
    core = lax.rem(me, 2)
    return 2 * (lax.div(me, 2) ^ mask) + (1 - core if other else core)


def columns_of(spots):
    return [pl.multiple_of(place_of(spot) * LANES, LANES) for spot in spots]


def join_kernel(*refs):
    part_refs, out_ref = refs[2:-1], refs[-1]
    at = 0
    for ref in part_refs:
        out_ref[at : at + ref.shape[0]] = ref[...]
        at += ref.shape[0]


def load_kernel(source_ref, out_ref, sems):
    chunks = sems.shape[0]
    count = source_ref.shape[0] // chunks
    copies = [
        pltpu.make_async_copy(
            source_ref.at[pl.ds(n * count, count)], out_ref.at[pl.ds(n * count, count)], sems.at[n]
        )
        for n in range(chunks)
    ]
    for copy in copies:
        copy.start()
    for copy in copies:
        copy.wait()


def diagonal(rows, spots, fields, factor_ref, store):
    lines = fields[0].shape[0]
    count = factor_ref.shape[0]
    field = jnp.concatenate(fields, axis=1)
    step = min(2048, count)
    row_of = lax.broadcasted_iota(jnp.int32, (rows, lines), 0)
    lane_of = lax.broadcasted_iota(jnp.int32, (rows, lines), 1)
    same = (lax.rem(lane_of, rows) == row_of).astype(jnp.float32)
    starts = columns_of(spots)
    for at in range(0, count, step):
        left = jnp.concatenate(
            [factor_ref[at : at + step, pl.ds(start, LANES)] for start in starts], axis=1
        )
        part = lax.dot_general(
            left, field, (((1,), (1,)), ((), ())), preferred_element_type=jnp.float32
        )
        part = part.reshape(step // rows, rows, lines) * same[None]
        store(at // rows, (at + step) // rows, jnp.sum(part, axis=1))


def blocks_of(refs):
    return [ref[n] for ref in refs for n in range(ref.shape[0])]


def first_kernel(rows, spots, added, factor_ref, *refs):
    diag_ref = refs[-1]
    field_refs = refs[: len(refs) - 1 - added]
    ranks = factor_ref.shape[0] // rows
    if diag_ref.shape[0] > ranks:
        diag_ref[...] = jnp.zeros_like(diag_ref)

    def store(start, end, value):
        diag_ref[start:end, :] = refs[-2][start:end, :] + value if added else value

    diagonal(rows, spots, blocks_of(field_refs), factor_ref, store)


def columns_kernel(halve, masks, x_ref, bundle_ref, twin_ref, along_ref, short_ref):
    me = lax.axis_index("tile")
    chip, core = lax.div(me, 2), lax.rem(me, 2)
    near = bundle_ref.shape[0] + 1
    beside = chip + 2 * core - 1
    slot = 0
    for n, mask in enumerate(masks):
        slot = jnp.where((chip ^ beside) == mask, n, slot)
    far = bundle_ref[slot].astype(jnp.float32)
    far = jnp.where((beside >= 0) & (beside < near), far, 0.0)
    twin = twin_ref[0].astype(jnp.float32)
    low = jnp.where(core == 0, far, twin)
    high = jnp.where(core == 0, twin, far)
    own = 0.5 * x_ref[...] if halve else x_ref[...]
    along = stencil(low, own, high, COL_TAPS, 1)
    along_ref[...] = along
    short_ref[...] = along.astype(jnp.bfloat16)


def second_kernel(
    rows, cols, spots, factor_ref, diag_ref, fields_ref, short_ref, pay_ref, part_ref, total
):
    lines = cols * rows
    if total.shape[0] > factor_ref.shape[0] // rows:
        total[...] = jnp.zeros_like(total)

    def store(start, end, value):
        total[start:end, :] = diag_ref[start:end, :] + value

    diagonal(rows, spots, blocks_of([fields_ref]), factor_ref, store)
    pick = (
        lax.broadcasted_iota(jnp.int32, (cols, lines), 1) // rows
        == lax.broadcasted_iota(jnp.int32, (cols, lines), 0)
    ).astype(jnp.bfloat16)
    value = total[...]
    upper = value.astype(jnp.bfloat16)
    lower = (value - upper.astype(jnp.float32)).astype(jnp.bfloat16)
    both = lax.dot_general(
        pick,
        jnp.concatenate([upper, lower], axis=0),
        (((1,), (1,)), ((), ())),
        preferred_element_type=jnp.float32,
    )
    proj = both[:, : total.shape[0]] + both[:, total.shape[0] :]
    for at in range(0, total.shape[0], LANES):
        upper = proj[:, at : at + LANES].astype(jnp.bfloat16)
        lower = (proj[:, at : at + LANES] - upper.astype(jnp.float32)).astype(jnp.bfloat16)
        first = at // LANES * 2 * cols
        for ref in (pay_ref, part_ref):
            ref[first : first + cols, :] = upper
            ref[first + cols : first + 2 * cols, :] = lower

    head = total.shape[0] // LANES * 2 * cols
    pay_ref[head:, :] = short_ref[...]


def product(coef, spots, factor_ref, out_ref):
    starts = columns_of(spots)
    for n in range(0, len(starts), 2):
        pair = starts[n : n + 2]
        right = jnp.concatenate([factor_ref[:, pl.ds(start, LANES)] for start in pair], axis=1)
        term = jnp.dot(coef, right, preferred_element_type=jnp.float32)
        for m in range(len(pair)):
            out_ref[n + m] = term[:, m * LANES : (m + 1) * LANES].astype(out_ref.dtype)


def far_kernel(rows, cols, groups, ncells, spots, scale_ref, factor_ref, *refs):
    pay_refs, (coef_ref, out_ref) = refs[:groups], refs[groups:]
    ranks = factor_ref.shape[0] // rows
    lines = cols * rows
    span = LANES // rows

    spread = (
        lax.broadcasted_iota(jnp.int32, (LANES, LANES), 1) // rows
        == lax.broadcasted_iota(jnp.int32, (LANES, LANES), 0)
    ).astype(jnp.bfloat16)
    same = (
        lax.rem(lax.broadcasted_iota(jnp.int32, (lines, LANES), 1), rows)
        == lax.rem(lax.broadcasted_iota(jnp.int32, (lines, LANES), 0), rows)
    ).astype(jnp.float32)
    turned = []
    for at in range(0, ranks, LANES):
        count = min(LANES, ranks - at)
        first = at // LANES * 2 * cols
        both = pay_refs[0][first : first + 2 * cols, :].astype(jnp.float32)
        for ref in pay_refs[1:]:
            both = both + ref[first : first + 2 * cols, :].astype(jnp.float32)
        proj = both[:cols] + both[cols:]
        scale = scale_ref[:, at : at + count]
        weights = scale * scale / ncells
        if count < LANES:
            weights = jnp.concatenate([weights, jnp.zeros((1, LANES - count), jnp.float32)], axis=1)
        c = proj * weights
        turned += [c if n == 0 else pltpu.roll(c, LANES - n * span, 1) for n in range(rows)]
    stacked = jnp.concatenate(turned, axis=0).astype(jnp.bfloat16)
    wide = jnp.dot(stacked, spread, preferred_element_type=jnp.float32)
    for n in range(ranks * rows // LANES):
        piece = wide[n * cols : (n + 1) * cols, :]
        piece = jnp.broadcast_to(piece[:, None, :], (cols, rows, LANES)).reshape(lines, LANES)
        coef_ref[:, n * LANES : (n + 1) * LANES] = (piece * same).astype(jnp.bfloat16)
    product(coef_ref[...], spots, factor_ref, out_ref)


def term_kernel(wanted, after, coef_ref, factor_ref, *refs):
    for (spots, _), out_ref in zip(wanted, refs[after:]):
        product(coef_ref[...], spots, factor_ref, out_ref)


def pair_kernel(mine_ref, got_ref, *out_refs):
    at = 0
    for ref in out_refs:
        end = at + ref.shape[0]
        ref[...] = (mine_ref[at:end] + got_ref[at:end].astype(jnp.float32)).astype(ref.dtype)
        at = end


def local_kernel(rows, cols, halve, b_ref, x_ref, amp_ref, along_ref, *refs):
    pay_refs, base_ref = refs[:-1], refs[-1]
    lines = cols * rows
    head = pay_refs[0].shape[0] - lines
    me = lax.axis_index("grp")
    low = jnp.zeros((lines, LANES), jnp.float32)
    high = low
    for n, ref in enumerate(pay_refs, 1):
        mask = (1 << n) - 1
        part = ref[head:, :].astype(jnp.float32)
        low = jnp.where((me ^ mask) == me - 1, part, low)
        high = jnp.where((me ^ mask) == me + 1, part, high)
    low = low.reshape(cols, rows, LANES)
    high = high.reshape(cols, rows, LANES)
    own = along_ref[...].reshape(cols, rows, LANES)
    conv = stencil(low, own, high, ROW_TAPS, 1)
    x = 0.5 * x_ref[...] if halve else x_ref[...]
    scaled = (amp_ref[...][None] * conv).reshape(lines, LANES)
    base_ref[...] = b_ref[...] - (x + scaled)


def update_kernel(halve, last, x_ref, base_ref, *refs):
    part_refs, (new_ref, other_ref) = refs[:-2], refs[-2:]
    rank_sum = part_refs[0][0]
    for ref in part_refs[1:]:
        rank_sum = rank_sum + ref[0].astype(jnp.float32)
    x = 0.5 * x_ref[...] if halve else x_ref[...]
    residual = base_ref[...] - rank_sum
    new = x + 0.5 * residual
    new_ref[...] = new
    if last:
        other_ref[...] = residual
    else:
        other_ref[0] = new.astype(jnp.bfloat16)


def on_device(right_side, amplitude, factor, scale):
    cols, rows, width = right_side.shape
    ranks = factor.shape[0]
    tiles = lax.axis_size("tile")
    groups = lax.axis_size("grp")
    near = tiles // 2
    lines = cols * rows
    ncells_all = rows * width * groups * tiles
    blocks = -(-ranks // LANES)
    flat = factor.reshape(ranks * rows, tiles * width)
    b = right_side.reshape(lines, width)
    scale = scale.reshape(1, ranks)
    x = b
    short = (0.5 * b).astype(jnp.bfloat16)[None]
    pay_rows = blocks * 2 * cols + lines

    f32, bf16 = jnp.float32, jnp.bfloat16

    def shape(dtype, *dims):
        return jax.ShapeDtypeStruct(dims, dtype)

    def call(kernel, out_shape, flops=0, moved=1 << 18, **options):
        return pl.pallas_call(
            kernel,
            out_shape=out_shape,
            compiler_params=pltpu.CompilerParams(vmem_limit_bytes=32 * 1024 * 1024),
            cost_estimate=pl.CostEstimate(flops=flops, bytes_accessed=moved, transcendentals=0),
            **options,
        )

    work = lines * ranks * rows * tiles * width
    held = call(
        load_kernel,
        shape(bf16, *flat.shape),
        moved=4 * flat.size,
        in_specs=[pl.BlockSpec(memory_space=pltpu.HBM)],
        out_specs=pl.BlockSpec(memory_space=pltpu.VMEM),
        scratch_shapes=[pltpu.SemaphoreType.DMA((8,))],
        name="load",
    )(flat)
    half = near // 2

    def spots_of(masks, other):
        return [(mask, other != (mask > 0)) for mask in masks]

    def cross(value, mask):
        return swap(value, "tile", 2 * mask + 1)

    def first(fields, spots, *before):
        return call(
            partial(first_kernel, rows, spots, len(before)),
            shape(f32, blocks * LANES, lines),
            flops=work,
            moved=flat.size,
            name="project_own",
        )(held, *fields, *before)

    for step in range(ITERS):
        halve = step == 0
        last = step == ITERS - 1
        close = list(range(half if last else 1))
        away = sorted(range(half, near), reverse=last) + list(range(len(close), half))
        order = list(range(1, near))
        order.sort(key=lambda mask: (mask == half, mask))
        parts = [cross(short, mask) for mask in order]
        twin = swap(short, "tile", 1)
        diag = first([short], [(0, False)])
        bundle = call(
            join_kernel,
            shape(bf16, near - 1, lines, width),
            in_specs=[pl.BlockSpec(memory_space=pl.ANY)] * 2
            + [pl.BlockSpec(memory_space=pltpu.VMEM)] * (near - 1),
            name="join",
        )(diag, twin, *parts)
        across = swap(bundle, "tile", 1)
        known = spots_of(order, False) + [(0, True)]
        diag = first([bundle, twin], known, diag)
        spots = spots_of(order, True)
        along, along_short = call(
            partial(columns_kernel, halve, order),
            (shape(f32, lines, width), shape(bf16, lines, width)),
            name="columns",
        )(x, bundle, twin)
        pay, part = call(
            partial(second_kernel, rows, cols, spots),
            (shape(bf16, pay_rows, width), shape(bf16, pay_rows - lines, width)),
            flops=work,
            moved=flat.size,
            scratch_shapes=[pltpu.VMEM((blocks * LANES, lines), f32)],
            name="project_across",
        )(held, diag, across, along_short)
        pays = [swap(part if mask & (mask + 1) else pay, "grp", mask) for mask in range(1, groups)]
        coef, far = call(
            partial(far_kernel, rows, cols, groups, ncells_all, spots_of(away, True)),
            (shape(bf16, lines, ranks * rows), shape(bf16, len(away), lines, width)),
            flops=work // 2,
            moved=flat.size,
            name="term_first",
        )(scale, held, part, *pays)
        got = swap(far, "tile", 1)

        def term(*wanted, after=()):
            return call(
                partial(term_kernel, wanted, len(after)),
                in_specs=[pl.BlockSpec(memory_space=pltpu.VMEM)] * 2
                + [pl.BlockSpec(memory_space=pl.ANY)] * len(after),
                out_shape=[shape(dtype, len(spots), lines, width) for spots, dtype in wanted],
                flops=work // 2 * len(wanted),
                moved=flat.size,
                name="term",
            )(coef, held, *after)

        def pair(mine, got, masks):
            return call(
                pair_kernel,
                [shape(bf16 if mask else f32, 1, lines, width) for mask in masks],
                name="pair",
            )(mine, got)

        mine, far = term((spots_of(away, False), f32), (spots_of(close, True), bf16))
        sends = pair(mine, got, away)
        terms = [cross(send, mask) for send, mask in zip(sends, away)]
        got = swap(far, "tile", 1)
        (mine,) = term((spots_of(close, False), f32), after=sends)
        kept, *sends = pair(mine, got, close)
        terms += [cross(send, mask) for send, mask in zip(sends, close[1:])]
        rims = [pay for mask, pay in enumerate(pays, 1) if not mask & (mask + 1)]
        base = call(
            partial(local_kernel, rows, cols, halve), shape(f32, lines, width), name="local"
        )(b, x, amplitude, along, *rims)
        x, short = call(
            partial(update_kernel, halve, last),
            (
                shape(f32, lines, width),
                shape(f32, lines, width) if last else shape(bf16, 1, lines, width),
            ),
            name="update",
        )(x, base, kept, *terms)
    return x.reshape(cols, rows, width), short.reshape(cols, rows, width)


def solution(mesh):
    in_specs = (P(None, "grp", "tile"), P("grp", "tile"), P("tile", "grp", None), P("tile"))
    out_specs = (P(None, "grp", "tile"), P(None, "grp", "tile"))
    return jax.shard_map(
        on_device, mesh=mesh, in_specs=in_specs, out_specs=out_specs, check_vma=False
    )
```

```python
import math
from functools import partial

import jax
import jax.numpy as jnp
import numpy as np
from jax import lax
from jax.experimental import pallas as pl
from jax.experimental.pallas import tpu as pltpu
from jax.sharding import PartitionSpec as P

REACH = 8
ITERS = 2
LANES = 128


def taper(sigma):
    offsets = np.arange(-REACH, REACH + 1).astype(np.float64)
    values = np.exp(-offsets * offsets / (2.0 * sigma * sigma))
    values = values * np.cos(np.pi * offsets / (2.0 * REACH + 2.0)) ** 2
    return [float(v) for v in (values / values.sum()).astype(np.float32)]


ROW_TAPS = taper(3.0)
COL_TAPS = taper(5.0)


def stencil(low, own, high, taps, axis):
    size = own.shape[axis]
    place = lax.broadcasted_iota(jnp.int32, own.shape, axis)
    total = taps[REACH] * own
    for shift in range(1, REACH + 1):
        after = pltpu.roll(jnp.where(place < shift, high, own), size - shift, axis)
        before = pltpu.roll(jnp.where(place >= size - shift, low, own), shift, axis)
        total = total + taps[REACH + shift] * after + taps[REACH - shift] * before
    return total


def swap(value, axis, mask):
    return lax.ppermute(value, axis, [(i, i ^ mask) for i in range(lax.axis_size(axis))])


def place_of(spot):
    mask, other = spot
    me = lax.axis_index("tile")
    core = lax.rem(me, 2)
    return 2 * (lax.div(me, 2) ^ mask) + (1 - core if other else core)


def columns_of(spots):
    return [pl.multiple_of(place_of(spot) * LANES, LANES) for spot in spots]


def join_kernel(*refs):
    part_refs, out_ref = refs[2:-1], refs[-1]
    at = 0
    for ref in part_refs:
        out_ref[at : at + ref.shape[0]] = ref[...]
        at += ref.shape[0]


def load_kernel(source_ref, out_ref, sems):
    chunks = sems.shape[0]
    count = source_ref.shape[0] // chunks
    copies = [
        pltpu.make_async_copy(
            source_ref.at[pl.ds(n * count, count)], out_ref.at[pl.ds(n * count, count)], sems.at[n]
        )
        for n in range(chunks)
    ]
    for copy in copies:
        copy.start()
    for copy in copies:
        copy.wait()


def diagonal(rows, spots, fields, factor_ref, store):
    lines = fields[0].shape[0]
    count = factor_ref.shape[0]
    field = jnp.concatenate(fields, axis=1)
    step = min(2048, count)
    row_of = lax.broadcasted_iota(jnp.int32, (rows, lines), 0)
    lane_of = lax.broadcasted_iota(jnp.int32, (rows, lines), 1)
    same = (lax.rem(lane_of, rows) == row_of).astype(jnp.float32)
    starts = columns_of(spots)
    for at in range(0, count, step):
        left = jnp.concatenate(
            [factor_ref[at : at + step, pl.ds(start, LANES)] for start in starts], axis=1
        )
        part = lax.dot_general(
            left, field, (((1,), (1,)), ((), ())), preferred_element_type=jnp.float32
        )
        part = part.reshape(step // rows, rows, lines) * same[None]
        store(at // rows, (at + step) // rows, jnp.sum(part, axis=1))


def blocks_of(refs):
    return [ref[n] for ref in refs for n in range(ref.shape[0])]


def first_kernel(rows, spots, added, factor_ref, *refs):
    diag_ref = refs[-1]
    field_refs = refs[: len(refs) - 1 - added]
    ranks = factor_ref.shape[0] // rows
    if diag_ref.shape[0] > ranks:
        diag_ref[...] = jnp.zeros_like(diag_ref)

    def store(start, end, value):
        diag_ref[start:end, :] = refs[-2][start:end, :] + value if added else value

    diagonal(rows, spots, blocks_of(field_refs), factor_ref, store)


def columns_kernel(halve, masks, x_ref, bundle_ref, twin_ref, along_ref, short_ref):
    me = lax.axis_index("tile")
    chip, core = lax.div(me, 2), lax.rem(me, 2)
    near = bundle_ref.shape[0] + 1
    beside = chip + 2 * core - 1
    slot = 0
    for n, mask in enumerate(masks):
        slot = jnp.where((chip ^ beside) == mask, n, slot)
    far = bundle_ref[slot].astype(jnp.float32)
    far = jnp.where((beside >= 0) & (beside < near), far, 0.0)
    twin = twin_ref[0].astype(jnp.float32)
    low = jnp.where(core == 0, far, twin)
    high = jnp.where(core == 0, twin, far)
    own = 0.5 * x_ref[...] if halve else x_ref[...]
    along = stencil(low, own, high, COL_TAPS, 1)
    along_ref[...] = along
    short_ref[...] = along.astype(jnp.bfloat16)


def second_kernel(
    rows, cols, spots, factor_ref, diag_ref, fields_ref, short_ref, pay_ref, part_ref, total
):
    lines = cols * rows
    if total.shape[0] > factor_ref.shape[0] // rows:
        total[...] = jnp.zeros_like(total)

    def store(start, end, value):
        total[start:end, :] = diag_ref[start:end, :] + value

    diagonal(rows, spots, blocks_of([fields_ref]), factor_ref, store)
    pick = (
        lax.broadcasted_iota(jnp.int32, (cols, lines), 1) // rows
        == lax.broadcasted_iota(jnp.int32, (cols, lines), 0)
    ).astype(jnp.bfloat16)
    for at in range(0, total.shape[0], LANES):
        part = total[at : at + LANES, :]
        upper = part.astype(jnp.bfloat16)
        lower = (part - upper.astype(jnp.float32)).astype(jnp.bfloat16)
        dims = (((1,), (1,)), ((), ()))
        proj = lax.dot_general(pick, upper, dims, preferred_element_type=jnp.float32)
        proj = proj + lax.dot_general(pick, lower, dims, preferred_element_type=jnp.float32)
        first = at // LANES * 2 * cols
        upper = proj.astype(jnp.bfloat16)
        lower = (proj - upper.astype(jnp.float32)).astype(jnp.bfloat16)
        for ref in (pay_ref, part_ref):
            ref[first : first + cols, :] = upper
            ref[first + cols : first + 2 * cols, :] = lower

    head = total.shape[0] // LANES * 2 * cols
    pay_ref[head:, :] = short_ref[...]


def product(coef, spots, factor_ref, out_ref):
    starts = columns_of(spots)
    for n in range(0, len(starts), 2):
        pair = starts[n : n + 2]
        right = jnp.concatenate([factor_ref[:, pl.ds(start, LANES)] for start in pair], axis=1)
        term = jnp.dot(coef, right, preferred_element_type=jnp.float32)
        for m in range(len(pair)):
            out_ref[n + m] = term[:, m * LANES : (m + 1) * LANES].astype(out_ref.dtype)


def far_kernel(rows, cols, groups, ncells, spots, scale_ref, factor_ref, *refs):
    pay_refs, (coef_ref, out_ref) = refs[:groups], refs[groups:]
    ranks = factor_ref.shape[0] // rows
    lines = cols * rows
    span = LANES // rows

    spread = (
        lax.broadcasted_iota(jnp.int32, (LANES, LANES), 1) // rows
        == lax.broadcasted_iota(jnp.int32, (LANES, LANES), 0)
    ).astype(jnp.bfloat16)
    same = (
        lax.rem(lax.broadcasted_iota(jnp.int32, (lines, LANES), 1), rows)
        == lax.rem(lax.broadcasted_iota(jnp.int32, (lines, LANES), 0), rows)
    ).astype(jnp.float32)
    for at in range(0, ranks, LANES):
        count = min(LANES, ranks - at)
        first = at // LANES * 2 * cols
        both = pay_refs[0][first : first + 2 * cols, :].astype(jnp.float32)
        for ref in pay_refs[1:]:
            both = both + ref[first : first + 2 * cols, :].astype(jnp.float32)
        proj = both[:cols] + both[cols:]
        scale = scale_ref[:, at : at + count]
        weights = scale * scale / ncells
        if count < LANES:
            weights = jnp.concatenate([weights, jnp.zeros((1, LANES - count), jnp.float32)], axis=1)
        c = proj * weights
        turned = [c if n == 0 else pltpu.roll(c, LANES - n * span, 1) for n in range(rows)]
        stacked = jnp.concatenate(turned, axis=0).astype(jnp.bfloat16)
        wide = jnp.dot(stacked, spread, preferred_element_type=jnp.float32)
        for n in range(rows):
            start = (at + n * span) * rows
            if start >= ranks * rows:
                break
            piece = wide[n * cols : (n + 1) * cols, :]
            piece = jnp.broadcast_to(piece[:, None, :], (cols, rows, LANES)).reshape(lines, LANES)
            coef_ref[:, start : start + LANES] = (piece * same).astype(jnp.bfloat16)
    product(coef_ref[...], spots, factor_ref, out_ref)


def term_kernel(wanted, after, coef_ref, factor_ref, *refs):
    for (spots, _), out_ref in zip(wanted, refs[after:]):
        product(coef_ref[...], spots, factor_ref, out_ref)


def pair_kernel(mine_ref, got_ref, *out_refs):
    at = 0
    for ref in out_refs:
        end = at + ref.shape[0]
        ref[...] = (mine_ref[at:end] + got_ref[at:end].astype(jnp.float32)).astype(ref.dtype)
        at = end


def local_kernel(rows, cols, halve, b_ref, x_ref, amp_ref, along_ref, *refs):
    pay_refs, base_ref = refs[:-1], refs[-1]
    lines = cols * rows
    head = pay_refs[0].shape[0] - lines
    me = lax.axis_index("grp")
    low = jnp.zeros((lines, LANES), jnp.float32)
    high = low
    for n, ref in enumerate(pay_refs, 1):
        mask = (1 << n) - 1
        part = ref[head:, :].astype(jnp.float32)
        low = jnp.where((me ^ mask) == me - 1, part, low)
        high = jnp.where((me ^ mask) == me + 1, part, high)
    low = low.reshape(cols, rows, LANES)
    high = high.reshape(cols, rows, LANES)
    own = along_ref[...].reshape(cols, rows, LANES)
    conv = stencil(low, own, high, ROW_TAPS, 1)
    x = 0.5 * x_ref[...] if halve else x_ref[...]
    scaled = (amp_ref[...][None] * conv).reshape(lines, LANES)
    base_ref[...] = b_ref[...] - (x + scaled)


def update_kernel(halve, last, x_ref, base_ref, *refs):
    part_refs, (new_ref, other_ref) = refs[:-2], refs[-2:]
    rank_sum = part_refs[0][0]
    for ref in part_refs[1:]:
        rank_sum = rank_sum + ref[0].astype(jnp.float32)
    x = 0.5 * x_ref[...] if halve else x_ref[...]
    residual = base_ref[...] - rank_sum
    new = x + 0.5 * residual
    new_ref[...] = new
    if last:
        other_ref[...] = residual
    else:
        other_ref[0] = new.astype(jnp.bfloat16)


def on_device(right_side, amplitude, factor, scale):
    cols, rows, width = right_side.shape
    ranks = factor.shape[0]
    tiles = lax.axis_size("tile")
    groups = lax.axis_size("grp")
    near = tiles // 2
    lines = cols * rows
    ncells_all = rows * width * groups * tiles
    blocks = -(-ranks // LANES)
    flat = factor.reshape(ranks * rows, tiles * width)
    b = right_side.reshape(lines, width)
    scale = scale.reshape(1, ranks)
    x = b
    short = (0.5 * b).astype(jnp.bfloat16)[None]
    pay_rows = blocks * 2 * cols + lines

    f32, bf16 = jnp.float32, jnp.bfloat16

    def shape(dtype, *dims):
        return jax.ShapeDtypeStruct(dims, dtype)

    def call(kernel, out_shape, flops=0, moved=1 << 18, **options):
        return pl.pallas_call(
            kernel,
            out_shape=out_shape,
            compiler_params=pltpu.CompilerParams(vmem_limit_bytes=32 * 1024 * 1024),
            cost_estimate=pl.CostEstimate(flops=flops, bytes_accessed=moved, transcendentals=0),
            **options,
        )

    work = lines * ranks * rows * tiles * width
    held = call(
        load_kernel,
        shape(bf16, *flat.shape),
        moved=4 * flat.size,
        in_specs=[pl.BlockSpec(memory_space=pltpu.HBM)],
        out_specs=pl.BlockSpec(memory_space=pltpu.VMEM),
        scratch_shapes=[pltpu.SemaphoreType.DMA((8,))],
        name="load",
    )(flat)
    half = near // 2
    close = list(range(half))

    def spots_of(masks, other):
        return [(mask, other != (mask > 0)) for mask in masks]

    def cross(value, mask):
        return swap(value, "tile", 2 * mask + 1)

    def first(fields, spots, *before):
        return call(
            partial(first_kernel, rows, spots, len(before)),
            shape(f32, blocks * LANES, lines),
            flops=work,
            moved=flat.size,
            name="project_own",
        )(held, *fields, *before)

    for step in range(ITERS):
        halve = step == 0
        last = step == ITERS - 1
        away = sorted(range(half, near), reverse=last)
        order = list(range(1, near))
        if step:
            order.sort(key=lambda mask: (mask == half, mask))
        parts = [cross(short, mask) for mask in order]
        twin = swap(short, "tile", 1)
        diag = first([short], [(0, False)])
        bundle = call(
            join_kernel,
            shape(bf16, near - 1, lines, width),
            in_specs=[pl.BlockSpec(memory_space=pl.ANY)] * 2
            + [pl.BlockSpec(memory_space=pltpu.VMEM)] * (near - 1),
            name="join",
        )(diag, twin, *parts)
        across = swap(bundle, "tile", 1)
        known = spots_of(order, False) + [(0, True)]
        diag = first([bundle, twin], known, diag)
        spots = spots_of(order, True)
        along, along_short = call(
            partial(columns_kernel, halve, order),
            (shape(f32, lines, width), shape(bf16, lines, width)),
            name="columns",
        )(x, bundle, twin)
        pay, part = call(
            partial(second_kernel, rows, cols, spots),
            (shape(bf16, pay_rows, width), shape(bf16, pay_rows - lines, width)),
            flops=work,
            moved=flat.size,
            scratch_shapes=[pltpu.VMEM((blocks * LANES, lines), f32)],
            name="project_across",
        )(held, diag, across, along_short)
        pays = [swap(part if mask & (mask + 1) else pay, "grp", mask) for mask in range(1, groups)]
        coef, far = call(
            partial(far_kernel, rows, cols, groups, ncells_all, spots_of(away, True)),
            (shape(bf16, lines, ranks * rows), shape(bf16, half, lines, width)),
            flops=work // 2,
            moved=flat.size,
            name="term_first",
        )(scale, held, part, *pays)
        got = swap(far, "tile", 1)

        def term(*wanted, after=()):
            return call(
                partial(term_kernel, wanted, len(after)),
                in_specs=[pl.BlockSpec(memory_space=pltpu.VMEM)] * 2
                + [pl.BlockSpec(memory_space=pl.ANY)] * len(after),
                out_shape=[shape(dtype, len(spots), lines, width) for spots, dtype in wanted],
                flops=work // 2 * len(wanted),
                moved=flat.size,
                name="term",
            )(coef, held, *after)

        def pair(mine, got, masks):
            return call(
                pair_kernel,
                [shape(bf16 if mask else f32, 1, lines, width) for mask in masks],
                name="pair",
            )(mine, got)

        mine, far = term((spots_of(away, False), f32), (spots_of(close, True), bf16))
        sends = pair(mine, got, away)
        terms = [cross(send, mask) for send, mask in zip(sends, away)]
        got = swap(far, "tile", 1)
        (mine,) = term((spots_of(close, False), f32), after=sends)
        kept, *sends = pair(mine, got, close)
        terms += [cross(send, mask) for send, mask in zip(sends, close[1:])]
        rims = [pay for mask, pay in enumerate(pays, 1) if not mask & (mask + 1)]
        base = call(
            partial(local_kernel, rows, cols, halve), shape(f32, lines, width), name="local"
        )(b, x, amplitude, along, *rims)
        x, short = call(
            partial(update_kernel, halve, last),
            (
                shape(f32, lines, width),
                shape(f32, lines, width) if last else shape(bf16, 1, lines, width),
            ),
            name="update",
        )(x, base, kept, *terms)
    return x.reshape(cols, rows, width), short.reshape(cols, rows, width)


def solution(mesh):
    in_specs = (P(None, "grp", "tile"), P("grp", "tile"), P("tile", "grp", None), P("tile"))
    out_specs = (P(None, "grp", "tile"), P(None, "grp", "tile"))
    return jax.shard_map(
        on_device, mesh=mesh, in_specs=in_specs, out_specs=out_specs, check_vma=False
    )
```
